32 devices in a mesh: seq: 4 (over y, x), rows: 8 (over z, core).
Axes of the slice: x: 2, y: 2, z: 4, core: 2. Of those that a mesh axis runs over, the one named last changes fastest.
Arguments:
- block_input: bfloat16 [8, 1024, 1024], P('rows', 'seq'), may hold values from -6 to 6
- valid_length: int32 [8], P('rows'), may hold values from 1 to 1024, as said below
- query_weight: bfloat16 [1024, 1024], P(('seq', 'rows')), may hold values from -0.1875 to 0.1875
- key_weight: bfloat16 [1024, 2048], P(('seq', 'rows')), may hold values from -0.1875 to 0.1875
- value_weight: bfloat16 [1024, 2048], P(('seq', 'rows')), may hold values from -0.1875 to 0.1875
- beta_weight: bfloat16 [1024, 16], P(('seq', 'rows')), may hold values from -0.1875 to 0.1875
- decay_weight: bfloat16 [1024, 8], P(('seq', 'rows')), may hold values from -0.1875 to 0.1875
- gate_weight: bfloat16 [1024, 1024], P(('seq', 'rows')), may hold values from -0.1875 to 0.1875
- out_weight: bfloat16 [1024, 1024], P(('seq', 'rows')), may hold values from -0.375 to 0.375
- ffn_gate_weight: bfloat16 [1024, 2816], P(('seq', 'rows')), may hold values from -0.1875 to 0.1875
- ffn_up_weight: bfloat16 [1024, 2816], P(('seq', 'rows')), may hold values from -0.1875 to 0.1875
- ffn_down_weight: bfloat16 [1024, 2816], P(('seq', 'rows')), may hold values from -0.109375 to 0.109375
- norm_gain: bfloat16 [1024], P(('seq', 'rows')), may hold values from 0.5 to 1.5
- ffn_norm_gain: bfloat16 [1024], P(('seq', 'rows')), may hold values from 0.5 to 1.5
- head_norm_gain: float32 [128], replicated, may hold values from 0.5 to 1.5
- decay_log: float32 [8], replicated, may hold values from -2 to 1
- decay_bias: float32 [8], replicated, may hold values from -7 to -2
- conv_weight: float32 [4, 5120], replicated, may hold values from -3 to 3
- output_grad: bfloat16 [8, 1024, 1024], P('rows', 'seq'), may hold values from -6 to 6
Outputs:
- block_output: bfloat16 [8, 1024, 1024], P('rows', 'seq')
- input_grad: float32 [8, 1024, 1024], P('rows', 'seq')
- query_weight_grad: float32 [1024, 1024], P(('seq', 'rows'))
- key_weight_grad: float32 [1024, 2048], P(('seq', 'rows'))
- value_weight_grad: float32 [1024, 2048], P(('seq', 'rows'))
- beta_weight_grad: float32 [1024, 16], P(('seq', 'rows'))
- decay_weight_grad: float32 [1024, 8], P(('seq', 'rows'))
- gate_weight_grad: float32 [1024, 1024], P(('seq', 'rows'))
- out_weight_grad: float32 [1024, 1024], P(('seq', 'rows'))
- ffn_gate_weight_grad: float32 [1024, 2816], P(('seq', 'rows'))
- ffn_up_weight_grad: float32 [1024, 2816], P(('seq', 'rows'))
- ffn_down_weight_grad: float32 [1024, 2816], P(('seq', 'rows'))
- norm_gain_grad: float32 [1024], P(('seq', 'rows'))
- ffn_norm_gain_grad: float32 [1024], P(('seq', 'rows'))
- head_norm_gain_grad: float32 [128], replicated
- decay_log_grad: float32 [8], replicated
- decay_bias_grad: float32 [8], replicated
- conv_weight_grad: float32 [4, 5120], replicated
The draws below stay inside these ranges and needn't reach their ends.
Inputs may be any that keep to these rules, and one draw needn't show every extreme that they name: `valid_length`: each row's valid tokens come first; in every draw some row has all 1024 tokens valid.
All inputs are finite; a program needn't handle non-finite values.
Results may differ from the reference program's by a relative error of at most 0.01.
Values may be sent and summed in bfloat16 or wider, within the bound.
No kernel may reach another device: no remote copies, remote signals or barrier semaphores. Data moves between devices by JAX's collectives and lax.ppermute only.
A program may use at most 384 MiB of HBM per device.

```python
import jax
import jax.numpy as jnp
from jax import lax

D = 1024
H = 8
DK = 128
NH = 2
CONV = 4
GROUP = 64
FF = 2816
LENGTH = 1024
ROWS = 8
CHAN = 5120


def draw_valid_length(key, part):
    key = jax.random.fold_in(key, 11)
    key_one, key_two = jax.random.split(key)
    lengths = jax.random.randint(key_one, (ROWS,), 1, LENGTH + 1)
    chosen = jax.random.randint(key_two, (), 0, ROWS)
    return jnp.where(jnp.arange(ROWS) == chosen, LENGTH, lengths).astype(jnp.int32)


def block_levels(rng, dims, shards, low, high):
    level, own = 1.0, jax.random.fold_in(rng, 6)
    for position, blocks in shards:
        steps = jnp.exp(jax.random.uniform(jax.random.fold_in(own, position), (blocks,), jnp.float32, low / len(shards), high / len(shards)))
        level = level * jnp.repeat(steps, dims[position] // blocks).reshape([-1 if axis == position else 1 for axis in range(len(dims))])
    return level


def scatter_about(own_key, shape, scale, limit, cuts=(), held_as=jnp.bfloat16):
    array = jax.random.normal(own_key, shape, jnp.float32) * scale
    if len(cuts) > 0:
        array = block_levels(own_key, shape, cuts, -0.22, 0.18) * array
    return jnp.clip(array, min=-limit, max=limit).astype(held_as)


def setup_inputs(seed: int = 0) -> dict:
    seeds = jax.random.split(jax.random.key(seed), 20)
    return {
        "block_input": scatter_about(seeds[0], (ROWS, LENGTH, D), 1.0, 6.0, ((0, 8), (1, 4))),
        "valid_length": draw_valid_length(jax.random.fold_in(seeds[19], 71), 0),
        "query_weight": scatter_about(seeds[2], (D, H * DK), D ** -0.5, 0.1875, ((0, 32),)),
        "key_weight": scatter_about(seeds[3], (D, NH * H * DK), D ** -0.5, 0.1875, ((0, 32),)),
        "value_weight": scatter_about(seeds[4], (D, NH * H * DK), D ** -0.5, 0.1875, ((0, 32),)),
        "beta_weight": scatter_about(seeds[5], (D, NH * H), D ** -0.5, 0.1875, ((0, 32),)),
        "decay_weight": scatter_about(seeds[6], (D, H), D ** -0.5, 0.1875, ((0, 32),)),
        "gate_weight": scatter_about(seeds[7], (D, H * DK), D ** -0.5, 0.1875, ((0, 32),)),
        "out_weight": scatter_about(seeds[8], (D, H * DK), (H * DK // 4) ** -0.5, 0.375, ((0, 32),)),
        "ffn_gate_weight": scatter_about(seeds[9], (D, FF), D ** -0.5, 0.1875, ((0, 32),)),
        "ffn_up_weight": scatter_about(seeds[10], (D, FF), D ** -0.5, 0.1875, ((0, 32),)),
        "ffn_down_weight": scatter_about(seeds[11], (D, FF), FF ** -0.5, 0.109375, ((0, 32),)),
        "norm_gain": jnp.clip(1.0 + 0.1 * jax.random.normal(seeds[12], (D,), jnp.float32), 0.5, 1.5).astype(jnp.bfloat16),
        "ffn_norm_gain": jnp.clip(1.0 + 0.1 * jax.random.normal(seeds[13], (D,), jnp.float32), 0.5, 1.5).astype(jnp.bfloat16),
        "head_norm_gain": jnp.clip(1.0 + 0.1 * jax.random.normal(seeds[14], (DK,), jnp.float32), 0.5, 1.5),
        "decay_log": jnp.clip(jax.random.uniform(seeds[15], (H,), jnp.float32, -2.0, 1.0), -2.0, 1.0),
        "decay_bias": jnp.clip(jax.random.uniform(seeds[16], (H,), jnp.float32, -7.0, -2.0), -7.0, -2.0),
        "conv_weight": scatter_about(seeds[17], (CONV, CHAN), 0.5, 3.0, (), jnp.float32),
        "output_grad": scatter_about(seeds[18], (ROWS, LENGTH, D), 1.0, 6.0, ((0, 8), (1, 4))),
    }


EPS_NORM = 1e-06
EPS_KEY = 1e-06
EPS_HEAD = 1e-05
HIGHEST = lax.Precision.HIGHEST

@jax.custom_vjp
def low(v):
    return lax.optimization_barrier(v.astype(jnp.bfloat16)).astype(jnp.float32)

@jax.custom_vjp
def low_back(v):
    return v

def low_keep(v):
    return (low(v), None)

def low_pass(kept, grad):
    return (grad,)

def back_keep(v):
    return (v, None)

def back_low(kept, grad):
    return (low(grad),)
low.defvjp(low_keep, low_pass)
low_back.defvjp(back_keep, back_low)

def batched_product(matrix_one, matrix_two):
    return jnp.einsum('...ij,...jk->...ik', matrix_one, matrix_two, precision=HIGHEST)

def root_norm(features, gain):
    return features * lax.rsqrt(lax.optimization_barrier(jnp.mean(features * features, axis=-1, keepdims=True)) + EPS_NORM) * gain

def split_blocks(tensor_in, block_count):
    dims_in = tensor_in.shape
    tensor_in = tensor_in.reshape((dims_in[0], block_count, dims_in[1] // block_count) + dims_in[2:])
    return jnp.moveaxis(tensor_in, 1, 0)

def join_blocks(tensor_in):
    block_count, head_count, block_size, head_dim = tensor_in.shape
    return tensor_in.transpose(0, 2, 1, 3).reshape(block_count * block_size, head_count, head_dim)

def lower_solve(matrix, right_side):
    return jax.scipy.linalg.solve_triangular(matrix, right_side, lower=True)

def prepare(mixed_in, prev_rim, beta_pre, decay_pre, conv_weight, decay_log, decay_bias, valid_mask, block_count):
    token_count = mixed_in.shape[0]
    head_count = decay_log.shape[0]
    step_count = beta_pre.shape[1] // head_count
    padded = jnp.concatenate([prev_rim, mixed_in], axis=0)
    summed = padded[0:token_count] * conv_weight[0]
    for offset in range(1, conv_weight.shape[0]):
        summed = summed + padded[offset:offset + token_count] * conv_weight[offset]
    active = jax.nn.silu(summed)
    inner_width = active.shape[1] // (1 + 2 * step_count)
    head_dim = inner_width // head_count
    query_rows = active[:, :inner_width].reshape(token_count, head_count, head_dim)
    key_rows = active[:, inner_width:inner_width * (1 + step_count)].reshape(token_count, step_count, head_count, head_dim)
    value_rows = active[:, inner_width * (1 + step_count):].reshape(token_count, step_count, head_count, head_dim)
    query_rows = query_rows * lax.rsqrt(lax.optimization_barrier(jnp.sum(query_rows * query_rows, axis=-1, keepdims=True)) + EPS_KEY) * head_dim ** (-0.5)
    key_rows = key_rows * lax.rsqrt(lax.optimization_barrier(jnp.sum(key_rows * key_rows, axis=-1, keepdims=True)) + EPS_KEY)
    beta_rows = jax.nn.sigmoid(beta_pre).reshape(token_count, step_count, head_count) * valid_mask[:, None, None]
    log_decay = -jnp.exp(decay_log) * jax.nn.softplus(decay_pre + decay_bias) * valid_mask[:, None]
    log_decay = jnp.concatenate([log_decay[:, None, :], jnp.zeros((token_count, step_count - 1, head_count), jnp.float32)], axis=1)
    pseudo_count = token_count * step_count
    key_rows = key_rows.transpose(2, 0, 1, 3).reshape(head_count, pseudo_count, head_dim)
    value_rows = value_rows.transpose(2, 0, 1, 3).reshape(head_count, pseudo_count, head_dim)
    beta_rows = beta_rows.transpose(2, 0, 1).reshape(head_count, pseudo_count)
    log_decay = log_decay.transpose(2, 0, 1).reshape(head_count, pseudo_count)
    query_rows = query_rows.transpose(1, 0, 2)
    return (split_blocks(query_rows, block_count), split_blocks(key_rows, block_count), split_blocks(value_rows, block_count), split_blocks(beta_rows, block_count), split_blocks(log_decay, block_count))

def group_summary(key_rows, value_rows, beta_rows, log_decay):
    pseudo_count = key_rows.shape[1]
    head_dim = key_rows.shape[2]
    cum_decay = jnp.cumsum(log_decay, axis=1)
    row_place = lax.broadcasted_iota(jnp.int32, (pseudo_count, pseudo_count), 0)
    col_place = lax.broadcasted_iota(jnp.int32, (pseudo_count, pseudo_count), 1)
    strict = row_place > col_place
    spread = cum_decay[:, :, None] - cum_decay[:, None, :]
    pair_decay = jnp.where(strict, jnp.exp(jnp.where(strict, spread, 0.0)), 0.0)
    key_gram = jnp.einsum('hid,hjd->hij', key_rows, key_rows, precision=HIGHEST)
    system = jnp.eye(pseudo_count, dtype=jnp.float32) + beta_rows[:, :, None] * pair_decay * key_gram
    right_side = jnp.concatenate([(beta_rows * jnp.exp(cum_decay))[:, :, None] * key_rows, beta_rows[:, :, None] * value_rows], axis=2)
    solved = jax.vmap(lower_solve)(system, right_side)
    key_solve = solved[:, :, :head_dim]
    pseudo_values = solved[:, :, head_dim:]
    last_decay = cum_decay[:, -1]
    carry_keys = jnp.exp(last_decay[:, None] - cum_decay)[:, :, None] * key_rows
    transition = jnp.exp(last_decay)[:, None, None] * jnp.eye(head_dim, dtype=jnp.float32) - jnp.einsum('hcd,hce->hde', carry_keys, key_solve, precision=HIGHEST)
    injected = jnp.einsum('hcd,hce->hde', carry_keys, pseudo_values, precision=HIGHEST)
    return (cum_decay, key_solve, pseudo_values, transition, injected)

def group_output(query_rows, key_rows, cum_decay, key_solve, pseudo_values, carried):
    token_count = query_rows.shape[1]
    pseudo_count = key_rows.shape[1]
    step_count = pseudo_count // token_count
    picked = cum_decay[:, step_count - 1::step_count]
    out_place = lax.broadcasted_iota(jnp.int32, (token_count, pseudo_count), 0) * step_count + step_count - 1
    col_place = lax.broadcasted_iota(jnp.int32, (token_count, pseudo_count), 1)
    visible = col_place <= out_place
    spread = picked[:, :, None] - cum_decay[:, None, :]
    weights = jnp.where(visible, jnp.exp(jnp.where(visible, spread, 0.0)), 0.0) * jnp.einsum('htd,hjd->htj', query_rows, key_rows, precision=HIGHEST)
    fresh_values = pseudo_values - jnp.einsum('hcd,hde->hce', key_solve, carried, precision=HIGHEST)
    return jnp.exp(picked)[:, :, None] * jnp.einsum('htd,hde->hte', query_rows, carried, precision=HIGHEST) + jnp.einsum('htj,hje->hte', weights, fresh_values, precision=HIGHEST)

def advance_group(carried, group_in):
    query_rows, key_rows, value_rows, beta_rows, log_decay = group_in
    cum_decay, key_solve, pseudo_values, transition, injected = group_summary(key_rows, value_rows, beta_rows, log_decay)
    produced = group_output(query_rows, key_rows, cum_decay, key_solve, pseudo_values, carried)
    return (batched_product(transition, carried) + injected, produced)

def gated_norm(mixed_out, out_gate, head_gain, valid_mask):
    token_count, head_count, head_dim = mixed_out.shape
    normed = mixed_out * lax.rsqrt(lax.optimization_barrier(jnp.mean(mixed_out * mixed_out, axis=-1, keepdims=True)) + EPS_HEAD) * head_gain
    gated = normed * jax.nn.silu(out_gate.reshape(token_count, head_count, head_dim)) * valid_mask[:, None, None]
    return gated.reshape(token_count, head_count * head_dim)

def row_forward(tokens, row_length, query_weight, key_weight, value_weight, beta_weight, decay_weight, gate_weight, out_weight, ffn_gate_weight, ffn_up_weight, ffn_down_weight, norm_gain, ffn_norm_gain, head_norm_gain, decay_log, decay_bias, conv_weight):
    token_count = tokens.shape[0]
    valid_mask = (lax.broadcasted_iota(jnp.int32, (token_count,), 0) < row_length).astype(jnp.float32)
    normed = low(root_norm(tokens, norm_gain))

    def project(matrix):
        return low_back(jnp.dot(normed, matrix, precision=HIGHEST))
    mixed_in = jnp.concatenate([project(query_weight), project(key_weight), project(value_weight)], axis=1)
    beta_pre = project(beta_weight)
    decay_pre = project(decay_weight)
    gate_pre = project(gate_weight)
    prev_rim = jnp.zeros((conv_weight.shape[0] - 1, mixed_in.shape[1]), jnp.float32)
    pieces = prepare(mixed_in, prev_rim, beta_pre, decay_pre, conv_weight, decay_log, decay_bias, valid_mask, token_count // GROUP)
    head_count = decay_log.shape[0]
    head_dim = head_norm_gain.shape[0]
    start = jnp.zeros((head_count, head_dim, head_dim), jnp.float32)
    ending, group_outs = lax.scan(jax.checkpoint(advance_group), start, pieces)
    mixed = low(gated_norm(join_blocks(group_outs), gate_pre, head_norm_gain, valid_mask))
    second = tokens + low_back(jnp.dot(mixed, out_weight.T, precision=HIGHEST))
    normed_two = low(root_norm(second, ffn_norm_gain))
    gate_act = low_back(jnp.dot(normed_two, ffn_gate_weight, precision=HIGHEST))
    up_act = low_back(jnp.dot(normed_two, ffn_up_weight, precision=HIGHEST))
    hidden = low(jax.nn.silu(gate_act) * up_act)
    return second + low_back(jnp.dot(hidden, ffn_down_weight.T, precision=HIGHEST))

def reference(block_input, valid_length, query_weight, key_weight, value_weight, beta_weight, decay_weight, gate_weight, out_weight, ffn_gate_weight, ffn_up_weight, ffn_down_weight, norm_gain, ffn_norm_gain, head_norm_gain, decay_log, decay_bias, conv_weight, output_grad):
    floats = tuple((member.astype(jnp.float32) for member in (block_input, query_weight, key_weight, value_weight, beta_weight, decay_weight, gate_weight, out_weight, ffn_gate_weight, ffn_up_weight, ffn_down_weight, norm_gain, ffn_norm_gain, head_norm_gain, decay_log, decay_bias, conv_weight)))

    def forward(tokens, *params):

        def per_row(packed):
            return row_forward(packed[0], packed[1], *params)
        return lax.map(jax.checkpoint(per_row), (tokens, valid_length))
    result, backward = jax.vjp(forward, *floats)
    grads = backward(output_grad.astype(jnp.float32))
    return (result.astype(jnp.bfloat16), grads[0], grads[1], grads[2], grads[3], grads[4], grads[5], grads[6], grads[7], grads[8], grads[9], grads[10], grads[11], grads[12], grads[13], grads[14], grads[15], grads[16])
```

```python
import functools

import jax
import jax.numpy as jnp
from jax import lax
from jax.experimental import pallas as pl
from jax.experimental.pallas import tpu as pltpu
from jax.sharding import PartitionSpec as P

GROUP = 64
EPS_NORM = 1e-06
EPS_KEY = 1e-06
EPS_HEAD = 1e-05
LOW = jnp.bfloat16
F32 = jnp.float32
HIGHEST = lax.Precision.HIGHEST
BOTH = ("seq", "rows")

FORMS = {
    "nn": (((1,), (0,)), ((), ())),
    "nt": (((1,), (1,)), ((), ())),
    "tn": (((0,), (0,)), ((), ())),
}


def split_low(a):
    high = a.astype(LOW)
    return high, (a - high.astype(F32)).astype(LOW)


def mm(a, b, form):
    a_axis = 0 if form == "tn" else 1
    b_axis = 1 if form == "nt" else 0
    a_two = jnp.concatenate(split_low(a), axis=a_axis)
    b_high, b_low = split_low(b)
    b_two = jnp.concatenate([b_high, b_low], axis=1 - b_axis)
    b_two = jnp.concatenate([b_two, b_two], axis=b_axis)
    out = lax.dot_general(a_two, b_two, FORMS[form], preferred_element_type=F32)
    half = out.shape[1] // 2
    return out[:, :half] + out[:, half:]


def mm_low(a, b, form):
    return lax.dot_general(a.astype(LOW), b.astype(LOW), FORMS[form], preferred_element_type=F32)


def mm_high(a, b, form):
    return lax.dot_general(a, b, FORMS[form], precision=HIGHEST, preferred_element_type=F32)


def row_dot(a, b):
    return jnp.sum(a * b, axis=1, keepdims=True)


def place(shape, axis):
    return lax.broadcasted_iota(jnp.int32, shape, axis)


def level_table():
    time = 2 * (jnp.arange(2 * GROUP) % GROUP) + jnp.arange(2 * GROUP) // GROUP
    row, col = time[:, None], time[None, :]
    differ = row ^ col
    level = sum((differ >= 2**m).astype(jnp.int32) for m in range(1, 7))
    return jnp.where(row > col, level, -1)


def inverses(systems, level):
    size = level.shape[0]
    eye = (place((size, size), 0) == place((size, size), 1)).astype(F32)
    found = [eye - jnp.where(level == 0, a, 0.0) for a in systems]
    for m in range(1, 7):
        inner = [mm(jnp.where(level == m, a, 0.0), t, "nn") for a, t in zip(systems, found)]
        found = [t - mm(t, s, "nn") for t, s in zip(found, inner)]
    return found


def conv_active(pad_ref, taps_ref, first, count):
    cols = slice(first, first + 128)
    summed = 0.0
    for back in range(4):
        summed = summed + pad_ref[pl.ds(8 - back, count), cols] * taps_ref[3 - back : 4 - back, cols]
    return summed


def silu(x):
    return x * jax.nn.sigmoid(x)


def softplus(x):
    return jnp.maximum(x, 0.0) + jnp.log1p(jnp.exp(-jnp.abs(x)))


def cum_decays(log_decay):
    tril = (place((GROUP, GROUP), 0) >= place((GROUP, GROUP), 1)).astype(F32)
    across = (place((GROUP, 2 * GROUP), 0) <= place((GROUP, 2 * GROUP), 1) % GROUP).astype(F32)
    return mm_high(tril, log_decay, "nn"), mm_high(log_decay, across, "tn")


def twice(a):
    return jnp.concatenate([a, a], axis=0)


def group_setup(level, beta, cum, across, head, heads):
    lane = 2 * heads + head
    c = cum[:, lane : lane + 1]
    row = across[lane : lane + 1, :]
    c_two = twice(c)
    end = c[GROUP - 1 : GROUP, :]
    b = jnp.concatenate([beta[:, head : head + 1], beta[:, heads + head : heads + head + 1]], axis=0)
    strict = level >= 0
    pair = jnp.where(strict, jnp.exp(jnp.where(strict, c_two - row, 0.0)), 0.0)
    seen = place((GROUP, 2 * GROUP), 1) % GROUP <= place((GROUP, 2 * GROUP), 0)
    view = jnp.where(seen, jnp.exp(jnp.where(seen, c - row, 0.0)), 0.0)
    return c, c_two, end, b, pair, view


def forward_kernel(
    heads, length_ref, mixed_ref, halo_ref, gate_ref, taps_ref, small_ref, level_ref,
    out_ref, raw_ref, solve_ref, fresh_ref, state_ref, carried, padded,
):
    step = pl.program_id(0)
    count = mixed_ref.shape[0]
    groups = count // GROUP
    wide = heads * 128

    @pl.when(step == 0)
    def _():
        carried[...] = jnp.zeros_like(carried)

    padded[0:8, :] = jnp.where(step > 0, halo_ref[:, : 5 * wide], 0.0)
    padded[8 : 8 + count, :] = mixed_ref[:, : 5 * wide]
    valid = (step * count + place((count, 1), 0) < length_ref[0]).astype(F32)
    level = level_ref[...]
    tail = mixed_ref[:, 5 * wide :]
    beta = jax.nn.sigmoid(tail) * valid
    log_decay = small_ref[0:1, :] * softplus(tail + small_ref[1:2, :]) * valid

    def active(slot, head):
        return silu(conv_active(padded, taps_ref, slot * wide + head * 128, count))

    def unit(x):
        return x * lax.rsqrt(row_dot(x, x) + EPS_KEY)

    queries = [unit(active(0, h)) * 128**-0.5 for h in range(heads)]
    keys = [[unit(active(1 + j, h)) for j in range(2)] for h in range(heads)]
    values = [[active(3 + j, h) for j in range(2)] for h in range(heads)]
    work = []
    for g in range(groups):
        rows = slice(g * GROUP, (g + 1) * GROUP)
        cum, across = cum_decays(log_decay[rows])
        for h in range(heads):
            key = jnp.concatenate([keys[h][0][rows], keys[h][1][rows]], axis=0)
            value = jnp.concatenate([values[h][0][rows], values[h][1][rows]], axis=0)
            c, c_two, end, b, pair, view = group_setup(level, beta[rows], cum, across, h, heads)
            gram = mm(key, key, "nt")
            work.append((g, h, rows, key, value, c, c_two, end, b, view, b * pair * gram))
    solves = inverses([w[-1] for w in work], level)
    raws = [[None] * groups for _ in range(heads)]
    ready = []
    for (g, h, rows, key, value, c, c_two, end, b, view, _), solve in zip(work, solves):
        solve_ref[g, h] = solve
        query = queries[h][rows]
        weights = view * mm(query, key, "nt")
        key_solve = mm(solve, b * jnp.exp(c_two) * key, "nn")
        pseudo = mm(solve, b * value, "nn")
        ready.append((query, weights, key_solve, pseudo))
    for (g, h, rows, key, value, c, c_two, end, b, view, _), made in zip(work, ready):
        query, weights, key_solve, pseudo = made
        state = carried[h]
        state_ref[g, h] = state
        fresh = pseudo - mm(key_solve, state, "nn")
        fresh_ref[g, h] = fresh
        carried[h] = jnp.exp(end) * state + mm(jnp.exp(end - c_two) * key, fresh, "tn")
        raws[h][g] = jnp.exp(c) * mm(query, state, "nn") + mm(weights, fresh, "nn")
    for h in range(heads):
        cols = slice(h * 128, (h + 1) * 128)
        raw = jnp.concatenate(raws[h], axis=0)
        raw_ref[:, cols] = raw
        scale = lax.rsqrt(jnp.mean(raw * raw, axis=1, keepdims=True) + EPS_HEAD)
        gated = raw * scale * small_ref[2:3, :] * silu(gate_ref[:, cols]) * valid
        out_ref[:, cols] = gated.astype(LOW)


def backward_kernel(
    heads, length_ref, mixed_ref, halo_ref, gate_ref, raw_ref, grad_ref, taps_ref, small_ref, level_ref,
    solve_ref, fresh_ref, state_ref,
    grad_mixed_ref, grad_gate_ref, grad_taps_ref, grad_small_ref,
    carried, padded, spread,
):
    step = pl.program_id(0)
    block = pl.num_programs(0) - 1 - step
    count = mixed_ref.shape[0]
    groups = count // GROUP
    wide = heads * 128

    @pl.when(step == 0)
    def _():
        carried[...] = jnp.zeros_like(carried)
        spread[...] = jnp.zeros_like(spread)
        grad_taps_ref[...] = jnp.zeros_like(grad_taps_ref)
        grad_small_ref[...] = jnp.zeros_like(grad_small_ref)

    spread[count : count + 8, :] = spread[0:8, :]
    padded[0:8, :] = jnp.where(block > 0, halo_ref[:, : 5 * wide], 0.0)
    padded[8 : 8 + count, :] = mixed_ref[:, : 5 * wide]
    valid = (block * count + place((count, 1), 0) < length_ref[0]).astype(F32)
    level = level_ref[...]
    strict = level >= 0
    tail = mixed_ref[:, 5 * wide :]
    sigmoid_tail = jax.nn.sigmoid(tail)
    beta = sigmoid_tail * valid
    log_decay = small_ref[0:1, :] * softplus(tail + small_ref[1:2, :]) * valid
    lanes = place((1, 128), 1)

    grad_raws = []
    for h in range(heads):
        cols = slice(h * 128, (h + 1) * 128)
        raw, gate = raw_ref[:, cols], gate_ref[:, cols]
        grad = grad_ref[:, cols] * valid
        sig = jax.nn.sigmoid(gate)
        scale = lax.rsqrt(jnp.mean(raw * raw, axis=1, keepdims=True) + EPS_HEAD)
        shaped = raw * scale
        gain = small_ref[2:3, :]
        grad_gate_ref[:, cols] = (grad * shaped * gain * sig * (1.0 + gate * (1.0 - sig))).astype(LOW)
        grad_normed = grad * gate * sig
        grad_small_ref[2:3, :] += jnp.sum(grad_normed * shaped, axis=0, keepdims=True)
        grad_shaped = grad_normed * gain
        grad_raws.append(scale * (grad_shaped - shaped * jnp.mean(grad_shaped * shaped, axis=1, keepdims=True)))

    def summed(slot, head):
        return conv_active(padded, taps_ref, slot * wide + head * 128, count)

    def unit(x):
        return x * lax.rsqrt(row_dot(x, x) + EPS_KEY)

    queries = [unit(silu(summed(0, h))) * 128**-0.5 for h in range(heads)]
    keys = [[unit(silu(summed(1 + j, h))) for j in range(2)] for h in range(heads)]
    values = [[silu(summed(3 + j, h)) for j in range(2)] for h in range(heads)]
    work = []
    for g in reversed(range(groups)):
        rows = slice(g * GROUP, (g + 1) * GROUP)
        cum, across = cum_decays(log_decay[rows])
        for h in range(heads):
            key = jnp.concatenate([keys[h][0][rows], keys[h][1][rows]], axis=0)
            value = jnp.concatenate([values[h][0][rows], values[h][1][rows]], axis=0)
            c, c_two, end, b, pair, view = group_setup(level, beta[rows], cum, across, h, heads)
            query, grad_raw = queries[h][rows], grad_raws[h][rows]
            scores = view * mm(query, key, "nt")
            late = mm(scores, grad_raw, "tn")
            grad_scores = view * mm(grad_raw, fresh_ref[g, h], "nt")
            work.append((g, h, rows, key, value, c, c_two, end, b, pair, query, grad_raw, late, grad_scores))
    grad_parts = [[[None] * groups for _ in range(5)] for _ in range(heads)]
    grad_betas, grad_cums = [0.0] * groups, [0.0] * groups
    for (g, h, rows, key, value, c, c_two, end, b, pair, query, grad_raw, late, grad_scores) in work:
        state, fresh, solve = state_ref[g, h], fresh_ref[g, h], solve_ref[g, h]
        grad_state = carried[h]
        grow, fade, all_fade = jnp.exp(c_two), jnp.exp(end - c_two), jnp.exp(end)
        grad_seen = jnp.exp(c) * grad_raw
        grad_fresh = late + mm(fade * key, grad_state, "nn")
        adjoint = mm(solve, grad_fresh, "tn")
        carried[h] = (
            all_fade * grad_state
            + mm(query, grad_seen, "tn")
            - mm(b * grow * key, adjoint, "tn")
        )
        grad_query = mm(grad_seen, state, "nt") + mm(grad_scores, key, "nn")
        part_one = mm(grad_scores, query, "tn")
        part_two = fade * mm(fresh, grad_state, "nt")
        part_three = -mm(adjoint, state, "nt")
        coupled = jnp.where(strict, -mm(adjoint, fresh, "nt"), 0.0) * pair
        part_four = mm(coupled, key, "nn")
        part_five = mm(b * coupled, key, "tn")
        grad_key = part_one + part_two + b * grow * part_three + b * part_four + part_five
        grad_value = b * adjoint
        through = grow * row_dot(part_three, key)
        pulled = row_dot(part_four, key)
        grad_b = row_dot(adjoint, value) + through + pulled
        ends = row_dot(part_two, key)
        grad_c = b * (through + pulled) - ends - row_dot(part_one + part_five, key)
        grad_c = row_dot(query, grad_query) + grad_c[:GROUP] + grad_c[GROUP:]
        grad_end = jnp.sum(ends) + jnp.sum(all_fade * grad_state * state)
        grad_c = grad_c + jnp.where(place((GROUP, 1), 0) == GROUP - 1, grad_end, 0.0)
        grad_cums[g] = grad_cums[g] + jnp.where(lanes == 2 * heads + h, grad_c, 0.0)
        for j in range(2):
            half = slice(j * GROUP, (j + 1) * GROUP)
            grad_betas[g] = grad_betas[g] + jnp.where(lanes == j * heads + h, grad_b[half], 0.0)
            grad_parts[h][1 + j][g] = grad_key[half]
            grad_parts[h][3 + j][g] = grad_value[half]
        grad_parts[h][0][g] = grad_query
    triu = (place((GROUP, GROUP), 0) <= place((GROUP, GROUP), 1)).astype(F32)
    grad_log = jnp.concatenate([mm_high(triu, x, "nn") for x in grad_cums], axis=0)
    grad_beta = jnp.concatenate(grad_betas, axis=0)
    grad_decay = grad_log * small_ref[0:1, :] * valid * jax.nn.sigmoid(tail + small_ref[1:2, :])
    grad_mixed_ref[:, 5 * wide :] = (
        grad_beta * beta * (1.0 - sigmoid_tail) + grad_decay
    ).astype(LOW)
    grad_small_ref[0:1, :] += jnp.sum(grad_log * log_decay, axis=0, keepdims=True)
    grad_small_ref[1:2, :] += jnp.sum(grad_decay, axis=0, keepdims=True)

    for h in range(heads):
        for slot in range(5):
            cols = slice(slot * wide + h * 128, slot * wide + (h + 1) * 128)
            grad = jnp.concatenate(grad_parts[h][slot], axis=0)
            pre = summed(slot, h)
            sig = jax.nn.sigmoid(pre)
            if slot < 3:
                act = pre * sig
                scale = lax.rsqrt(row_dot(act, act) + EPS_KEY)
                shaped = act * scale
                if slot == 0:
                    grad = grad * 128**-0.5
                grad = scale * (grad - shaped * row_dot(grad, shaped))
            grad = grad * sig * (1.0 + pre * (1.0 - sig))
            spread[0:count, cols] = grad
            back = 0.0
            for ahead in range(4):
                back = back + spread[pl.ds(ahead, count), cols] * taps_ref[3 - ahead : 4 - ahead, cols]
            grad_mixed_ref[:, cols] = back.astype(LOW)
            for tap in range(4):
                grad_taps_ref[tap : tap + 1, cols] += jnp.sum(
                    grad * padded[pl.ds(5 + tap, count), cols], axis=0, keepdims=True
                )


def step_tokens(tokens):
    return min(128, tokens)


def block_specs(heads, count, order):
    wide = heads * 128
    all_wide = 5 * wide + 128
    whole = lambda *shape: pl.BlockSpec(shape, lambda i: (0,) * len(shape))
    return dict(
        length=pl.BlockSpec(memory_space=pltpu.SMEM),
        mixed=pl.BlockSpec((count, all_wide), lambda i: (order(i), 0)),
        halo=pl.BlockSpec((8, all_wide), lambda i: (jnp.maximum(order(i) * (count // 8) - 1, 0), 0)),
        head=pl.BlockSpec((count, wide), lambda i: (order(i), 0)),
        taps=whole(8, 5 * wide),
        small=whole(8, 128),
        level=whole(2 * GROUP, 2 * GROUP),
        kept=pl.BlockSpec((count // GROUP, heads, 128, 128), lambda i: (order(i), 0, 0, 0)),
    )


VMEM_BYTES = 56 * 2**20


def mixer_forward(heads, length, mixed, gate, taps, small, level):
    tokens = mixed.shape[0]
    count = step_tokens(tokens)
    steps = tokens // count
    wide = heads * 128
    s = block_specs(heads, count, lambda i: i)
    kept = jax.ShapeDtypeStruct((tokens // GROUP, heads, 128, 128), F32)
    return pl.pallas_call(
        functools.partial(forward_kernel, heads),
        grid=(steps,),
        in_specs=[s["length"], s["mixed"], s["halo"], s["head"], s["taps"], s["small"], s["level"]],
        out_specs=[s["head"], s["head"], s["kept"], s["kept"], s["kept"]],
        out_shape=[
            jax.ShapeDtypeStruct((tokens, wide), LOW),
            jax.ShapeDtypeStruct((tokens, wide), F32),
            kept, kept, kept,
        ],
        scratch_shapes=[pltpu.VMEM((heads, 128, 128), F32), pltpu.VMEM((count + 8, 5 * wide), F32)],
        compiler_params=pltpu.CompilerParams(vmem_limit_bytes=VMEM_BYTES),
        cost_estimate=pl.CostEstimate(
            flops=tokens * heads * 40_000_00, bytes_accessed=tokens * heads * 10_000, transcendentals=0
        ),
        name="mixer_forward",
    )(length, mixed, mixed, gate, taps, small, level)


def mixer_backward(heads, length, mixed, gate, raw, grad, taps, small, level, solve, fresh, state):
    tokens = mixed.shape[0]
    count = step_tokens(tokens)
    steps = tokens // count
    wide = heads * 128
    s = block_specs(heads, count, lambda i: steps - 1 - i)
    return pl.pallas_call(
        functools.partial(backward_kernel, heads),
        grid=(steps,),
        in_specs=[
            s["length"], s["mixed"], s["halo"], s["head"], s["head"], s["head"], s["taps"], s["small"], s["level"],
            s["kept"], s["kept"], s["kept"],
        ],
        out_specs=[s["mixed"], s["head"], s["taps"], s["small"]],
        out_shape=[
            jax.ShapeDtypeStruct(mixed.shape, LOW),
            jax.ShapeDtypeStruct((tokens, wide), LOW),
            jax.ShapeDtypeStruct((8, 5 * wide), F32),
            jax.ShapeDtypeStruct((8, 128), F32),
        ],
        scratch_shapes=[
            pltpu.VMEM((heads, 128, 128), F32),
            pltpu.VMEM((count + 8, 5 * wide), F32),
            pltpu.VMEM((count + 8, 5 * wide), F32),
        ],
        compiler_params=pltpu.CompilerParams(vmem_limit_bytes=VMEM_BYTES),
        cost_estimate=pl.CostEstimate(
            flops=tokens * heads * 60_000_00, bytes_accessed=tokens * heads * 10_000, transcendentals=0
        ),
        name="mixer_backward",
    )(length, mixed, mixed, gate, raw, grad, taps, small, level, solve, fresh, state)


def swap(array, axis, bits):
    return lax.ppermute(array, axis, [(i, i ^ bits) for i in range(lax.axis_size(axis))])


def on_square(axis):
    return lax.axis_size(axis) == 4


def power_of_two(axis):
    return lax.axis_size(axis) & (lax.axis_size(axis) - 1) == 0


def block_at(array, index, size):
    return lax.dynamic_slice_in_dim(array, index * size, size, 0)


def put(array, block, start):
    return lax.dynamic_update_slice(array, block, (start,) + (0,) * (array.ndim - 1))


def gather_tokens(array):
    if not on_square("seq"):
        return lax.all_gather(array, "seq", axis=0, tiled=True)
    me = lax.axis_index("seq")
    size = array.shape[0]
    half = size // 2
    beside, below = swap(array, "seq", 1), swap(array, "seq", 2)
    far_one = swap(below[:half], "seq", 1)
    far_two = swap(beside[half:], "seq", 2)
    out = jnp.zeros((4 * size,) + array.shape[1:], array.dtype)
    out = put(out, array, me * size)
    out = put(out, beside, (me ^ 1) * size)
    out = put(out, below, (me ^ 2) * size)
    out = put(out, far_one, (me ^ 3) * size)
    return put(out, far_two, (me ^ 3) * size + half)


def scatter_sum(array):
    count = lax.axis_size("seq")
    size = array.shape[0] // count
    if not on_square("seq"):
        return lax.psum_scatter(array.astype(LOW), "seq", scatter_dimension=0, tiled=True).astype(F32)
    me = lax.axis_index("seq")
    half = array.shape[1] // 2
    parts = []
    for cols, first, second in ((slice(0, half), 1, 2), (slice(half, None), 2, 1)):
        part = array[:, cols].reshape(count, size, half)

        def block(index):
            return lax.dynamic_index_in_dim(part, index, 0, False)

        near = swap(block(me ^ first).astype(LOW), "seq", first)
        sent = swap(block(me ^ first ^ second).astype(LOW), "seq", first)
        onward = (block(me ^ second) + sent.astype(F32)).astype(LOW)
        own = block(me) + near.astype(F32)
        parts.append((own, swap(onward, "seq", second)))
    return jnp.concatenate([own + got.astype(F32) for own, got in parts], axis=1)


def exchange(blocks):
    if not on_square("seq"):
        return lax.all_to_all(blocks, "seq", 0, 0, tiled=True)
    me = lax.axis_index("seq")
    out = blocks
    for bits in (3, 1, 2):
        sent = lax.dynamic_index_in_dim(blocks, me ^ bits, 0, True)
        out = put(out, swap(sent, "seq", bits), me ^ bits)
    return out


def sum_over_rows(array):
    if not power_of_two("rows"):
        return lax.psum(array, "rows")
    bits = 1
    while bits < lax.axis_size("rows"):
        array = array + swap(array, "rows", bits)
        bits *= 2
    return array


def gather_small(array):
    if not power_of_two("seq"):
        return lax.all_gather(array, "seq")
    count = lax.axis_size("seq")
    me = lax.axis_index("seq")
    out = put(jnp.zeros((count,) + array.shape, array.dtype), array[None], me)
    bits = 1
    while bits < count:
        out = out + swap(out, "seq", bits)
        bits *= 2
    return out


def gather_weights(blocks):
    mine = exchange(blocks)
    whole = lax.all_gather(mine, "rows", axis=0)
    rows, count, size, width = whole.shape
    return whole.transpose(1, 0, 2, 3).reshape(count * rows * size, width)


def scatter_weights(grad):
    count, rows = lax.axis_size("seq"), lax.axis_size("rows")
    size = grad.shape[0] // (count * rows)
    width = grad.shape[1]
    grad = grad.astype(LOW).reshape(count, rows, size, width).transpose(1, 0, 2, 3)
    summed = lax.psum_scatter(grad.reshape(-1, width), "rows", scatter_dimension=0, tiled=True)
    return exchange(summed.reshape(count, size, width))


def project(left, right):
    return jnp.dot(left, right, preferred_element_type=F32)


def outer_sum(left, right):
    return lax.dot_general(left, right, FORMS["tn"], preferred_element_type=F32)


def back_project(left, right):
    return lax.dot_general(left, right, FORMS["nt"], preferred_element_type=F32)


def norm_scale(features):
    return lax.rsqrt(jnp.mean(features * features, axis=-1, keepdims=True) + EPS_NORM)


def norm_back(features, scale, grad):
    return scale * grad - features * scale**3 * jnp.mean(grad * features, axis=-1, keepdims=True)


def on_device(
    block_input, valid_length, query_weight, key_weight, value_weight, beta_weight, decay_weight, gate_weight,
    out_weight, ffn_gate_weight, ffn_up_weight, ffn_down_weight, norm_gain, ffn_norm_gain, head_norm_gain,
    decay_log, decay_bias, conv_weight, output_grad,
):
    count = lax.axis_size("seq")
    me = lax.axis_index("seq")
    rows_here, tokens_here, model_width = block_input.shape
    share = query_weight.shape[0]
    head_count = decay_log.shape[0]
    heads = max(1, head_count // count)
    blocks = head_count // heads
    copies = count // blocks
    block = me // copies
    wide = heads * 128
    hidden = ffn_gate_weight.shape[1] // count
    all_wide = 5 * wide + 128

    def cut(weight, pieces):
        width = weight.shape[1] // (pieces * blocks)
        out = weight.reshape(share, pieces, blocks, width).transpose(2, 0, 1, 3)
        return jnp.repeat(out.reshape(blocks, share, pieces * width), copies, axis=0)

    def cut_hidden(weight):
        return weight.reshape(share, count, hidden).transpose(1, 0, 2)

    def gain_column(gain):
        return jnp.broadcast_to(gain[None, :, None], (count, share, 1))

    tail = jnp.concatenate(
        [cut(beta_weight, 2), cut(decay_weight, 1), gain_column(norm_gain), gain_column(ffn_norm_gain)], axis=2
    )
    tail = jnp.pad(tail, ((0, 0), (0, 0), (0, 128 - tail.shape[2])))
    first_pack = jnp.concatenate([cut(query_weight, 1), cut(key_weight, 2), cut(value_weight, 2), tail], axis=2)
    later_pack = jnp.concatenate(
        [cut(gate_weight, 1), cut(out_weight, 1), cut_hidden(ffn_gate_weight), cut_hidden(ffn_up_weight),
         cut_hidden(ffn_down_weight)], axis=2,
    )
    mixed_weight = gather_weights(first_pack)
    own = block_input.reshape(tokens_here, model_width)
    everyone = gather_tokens(own)
    later_weight = gather_weights(later_pack)
    gate_matrix = later_weight[:, :wide]
    out_matrix = later_weight[:, wide : 2 * wide]
    ffn_in = later_weight[:, 2 * wide : 2 * wide + 2 * hidden]
    ffn_down = later_weight[:, 2 * wide + 2 * hidden :]
    gain_first = mixed_weight[:, 5 * wide + 3 * heads].astype(F32)
    gain_second = mixed_weight[:, 5 * wide + 3 * heads + 1].astype(F32)
    grad_branch = gather_tokens(output_grad.reshape(tokens_here, model_width))

    def block_lanes(vector, first):
        mine = lax.dynamic_slice_in_dim(vector, block * heads, heads)
        return jnp.zeros((128,), F32).at[first : first + heads].set(mine)

    small = jnp.zeros((8, 128), F32)
    small = small.at[0].set(block_lanes(-jnp.exp(decay_log), 2 * heads))
    small = small.at[1].set(block_lanes(decay_bias, 2 * heads))
    small = small.at[2].set(head_norm_gain)
    taps = conv_weight.reshape(conv_weight.shape[0], 5, blocks, wide)
    taps = lax.dynamic_index_in_dim(taps, block, 2, False).reshape(conv_weight.shape[0], 5 * wide)
    taps = jnp.pad(taps, ((0, 8 - taps.shape[0]), (0, 0)))
    level = level_table()

    tokens_all = everyone.astype(F32)
    scale_all = norm_scale(tokens_all)
    shaped_all = tokens_all * scale_all
    normed = (shaped_all * gain_first).astype(LOW)
    mixed = project(normed, mixed_weight)
    gate_pre = project(normed, gate_matrix)
    gated, raw, solve, fresh, state = mixer_forward(heads, valid_length, mixed, gate_pre, taps, small, level)
    keep = (me % copies == 0).astype(F32)

    def once(array):
        return array if copies == 1 else array * keep.astype(array.dtype)

    tokens = own.astype(F32)
    second = tokens + scatter_sum(once(back_project(gated, out_matrix)))
    scale_second = norm_scale(second)
    normed_two = gather_tokens((second * scale_second * gain_second).astype(LOW))
    acts = project(normed_two, ffn_in)
    gate_act, up_act = acts[:, :hidden], acts[:, hidden:]
    sig = jax.nn.sigmoid(gate_act)
    hidden_low = (gate_act * sig * up_act).astype(LOW)
    result = second + scatter_sum(back_project(hidden_low, ffn_down))
    result = result.astype(LOW).reshape(block_input.shape)

    grad_hidden = project(grad_branch, ffn_down)
    grad_acts = jnp.concatenate(
        [grad_hidden * up_act * sig * (1.0 + gate_act * (1.0 - sig)), grad_hidden * gate_act * sig], axis=1
    ).astype(LOW)
    grad_normed_two = scatter_sum(back_project(grad_acts, ffn_in))
    grad_second = output_grad.reshape(tokens_here, model_width).astype(F32) + norm_back(
        second, scale_second, grad_normed_two * gain_second
    )
    grad_gain_second = jnp.sum(grad_normed_two * second * scale_second, axis=0)
    grad_mixed_low = gather_tokens(grad_second.astype(LOW))
    grad_gated = project(grad_mixed_low, out_matrix)
    ffn_grads = scatter_weights(
        jnp.concatenate([outer_sum(normed_two, grad_acts), outer_sum(grad_branch, hidden_low)], axis=1)
    )
    grad_pre, grad_gate, grad_taps, grad_small = mixer_backward(
        heads, valid_length, mixed, gate_pre, raw, grad_gated, taps, small, level, solve, fresh, state
    )
    grad_pre, grad_gate = once(grad_pre), once(grad_gate)
    pooled = jnp.concatenate([grad_taps[:4], jnp.pad(grad_small[:4], ((0, 0), (0, 5 * wide - 128)))], axis=0)
    pooled = gather_small(sum_over_rows(once(pooled)))

    late_grads = scatter_weights(
        jnp.concatenate([outer_sum(normed, grad_gate), once(outer_sum(grad_mixed_low, gated))], axis=1)
    )
    grad_normed = back_project(grad_pre, mixed_weight) + back_project(grad_gate, gate_matrix)
    grad_gain_first = jnp.sum(grad_normed * shaped_all, axis=0)
    mixed_grads = outer_sum(normed, grad_pre)
    first_gain = 5 * wide + 3 * heads
    mixed_grads = jnp.concatenate(
        [mixed_grads[:, :first_gain], grad_gain_first[:, None], grad_gain_second[:, None],
         jnp.zeros((model_width, all_wide - first_gain - 2), F32)], axis=1,
    )
    mixed_grads = scatter_weights(mixed_grads).astype(F32)
    grad_normed = scatter_sum(grad_normed)
    scale = norm_scale(tokens)
    grad_input = grad_second + norm_back(tokens, scale, grad_normed * gain_first)
    grad_input = grad_input.reshape(block_input.shape)

    def join(grads, pieces):
        grads = grads[::copies].astype(F32)
        width = grads.shape[2] // pieces
        return grads.reshape(blocks, share, pieces, width).transpose(1, 2, 0, 3).reshape(share, -1)

    def join_hidden(grads):
        return grads.astype(F32).transpose(1, 0, 2).reshape(share, -1)

    tail = mixed_grads[:, :, 5 * wide :]
    by_block = pooled[::copies]
    grad_conv = by_block[:, :4].reshape(blocks, 4, 5, wide).transpose(1, 2, 0, 3).reshape(4, -1)
    return (
        result,
        grad_input,
        join(mixed_grads[:, :, :wide], 1),
        join(mixed_grads[:, :, wide : 3 * wide], 2),
        join(mixed_grads[:, :, 3 * wide : 5 * wide], 2),
        join(tail[:, :, : 2 * heads], 2),
        join(tail[:, :, 2 * heads : 3 * heads], 1),
        join(late_grads[:, :, :wide], 1),
        join(late_grads[:, :, wide:], 1),
        join_hidden(ffn_grads[:, :, :hidden]),
        join_hidden(ffn_grads[:, :, hidden : 2 * hidden]),
        join_hidden(ffn_grads[:, :, 2 * hidden :]),
        jnp.sum(tail[:, :, 3 * heads], axis=0),
        jnp.sum(tail[:, :, 3 * heads + 1], axis=0),
        jnp.sum(by_block[:, 6, :128], axis=0),
        by_block[:, 4, 2 * heads : 3 * heads].reshape(-1),
        by_block[:, 5, 2 * heads : 3 * heads].reshape(-1),
        grad_conv,
    )


def solution(mesh):
    tokens, weight, vector, whole = P("rows", "seq", None), P(BOTH, None), P(BOTH), P()
    return jax.shard_map(
        on_device,
        mesh=mesh,
        in_specs=(tokens, P("rows")) + (weight,) * 10 + (vector,) * 2 + (whole,) * 4 + (tokens,),
        out_specs=(tokens, tokens) + (weight,) * 10 + (vector,) * 2 + (whole,) * 4,
        check_vma=False,
    )
```

```python
import functools

import jax
import jax.numpy as jnp
from jax import lax
from jax.experimental import pallas as pl
from jax.experimental.pallas import tpu as pltpu
from jax.sharding import PartitionSpec as P

GROUP = 64
EPS_NORM = 1e-06
EPS_KEY = 1e-06
EPS_HEAD = 1e-05
LOW = jnp.bfloat16
F32 = jnp.float32
HIGHEST = lax.Precision.HIGHEST
BOTH = ("seq", "rows")

FORMS = {
    "nn": (((1,), (0,)), ((), ())),
    "nt": (((1,), (1,)), ((), ())),
    "tn": (((0,), (0,)), ((), ())),
}


def split_low(a):
    high = a.astype(LOW)
    return high, (a - high.astype(F32)).astype(LOW)


def mm(a, b, form):
    a_axis = 0 if form == "tn" else 1
    b_axis = 1 if form == "nt" else 0
    a_two = jnp.concatenate(split_low(a), axis=a_axis)
    b_high, b_low = split_low(b)
    b_two = jnp.concatenate([b_high, b_low], axis=1 - b_axis)
    b_two = jnp.concatenate([b_two, b_two], axis=b_axis)
    out = lax.dot_general(a_two, b_two, FORMS[form], preferred_element_type=F32)
    half = out.shape[1] // 2
    return out[:, :half] + out[:, half:]


def mm_low(a, b, form):
    return lax.dot_general(a.astype(LOW), b.astype(LOW), FORMS[form], preferred_element_type=F32)


def mm_high(a, b, form):
    return lax.dot_general(a, b, FORMS[form], precision=HIGHEST, preferred_element_type=F32)


def row_dot(a, b):
    return jnp.sum(a * b, axis=1, keepdims=True)


def place(shape, axis):
    return lax.broadcasted_iota(jnp.int32, shape, axis)


def level_table():
    time = 2 * (jnp.arange(2 * GROUP) % GROUP) + jnp.arange(2 * GROUP) // GROUP
    row, col = time[:, None], time[None, :]
    differ = row ^ col
    level = sum((differ >= 2**m).astype(jnp.int32) for m in range(1, 7))
    return jnp.where(row > col, level, -1)


def inverses(systems, level):
    size = level.shape[0]
    eye = (place((size, size), 0) == place((size, size), 1)).astype(F32)
    found = [eye - jnp.where(level == 0, a, 0.0) for a in systems]
    for m in range(1, 7):
        inner = [mm(jnp.where(level == m, a, 0.0), t, "nn") for a, t in zip(systems, found)]
        found = [t - mm(t, s, "nn") for t, s in zip(found, inner)]
    return found


def conv_active(pad_ref, taps_ref, first, count):
    cols = slice(first, first + 128)
    summed = 0.0
    for back in range(4):
        summed = summed + pad_ref[pl.ds(8 - back, count), cols] * taps_ref[3 - back : 4 - back, cols]
    return summed


def silu(x):
    return x * jax.nn.sigmoid(x)


def softplus(x):
    return jnp.maximum(x, 0.0) + jnp.log1p(jnp.exp(-jnp.abs(x)))


def cum_decays(log_decay):
    tril = (place((GROUP, GROUP), 0) >= place((GROUP, GROUP), 1)).astype(F32)
    across = (place((GROUP, 2 * GROUP), 0) <= place((GROUP, 2 * GROUP), 1) % GROUP).astype(F32)
    return mm_high(tril, log_decay, "nn"), mm_high(log_decay, across, "tn")


def twice(a):
    return jnp.concatenate([a, a], axis=0)


def group_setup(level, beta, cum, across, head, heads):
    lane = 2 * heads + head
    c = cum[:, lane : lane + 1]
    row = across[lane : lane + 1, :]
    c_two = twice(c)
    end = c[GROUP - 1 : GROUP, :]
    b = jnp.concatenate([beta[:, head : head + 1], beta[:, heads + head : heads + head + 1]], axis=0)
    strict = level >= 0
    pair = jnp.where(strict, jnp.exp(jnp.where(strict, c_two - row, 0.0)), 0.0)
    seen = place((GROUP, 2 * GROUP), 1) % GROUP <= place((GROUP, 2 * GROUP), 0)
    view = jnp.where(seen, jnp.exp(jnp.where(seen, c - row, 0.0)), 0.0)
    return c, c_two, end, b, pair, view


def forward_kernel(
    heads, first, info_ref, mixed_ref, halo_ref, taps_ref, small_ref, level_ref, start_ref,
    out_ref, raw_ref, solve_ref, fresh_ref, state_ref, end_ref, carried, padded,
):
    step = pl.program_id(0)
    count = mixed_ref.shape[0]
    block = step + first // count
    groups = count // GROUP
    wide = heads * 128

    @pl.when(step == 0)
    def _():
        carried[...] = start_ref[...]

    padded[0:8, :] = jnp.where(block > 0, halo_ref[:, : 5 * wide], 0.0)
    padded[8 : 8 + count, :] = mixed_ref[:, : 5 * wide]
    valid = (block * count + place((count, 1), 0) < info_ref[0]).astype(F32)
    level = level_ref[...]
    tail = mixed_ref[:, 6 * wide :]
    beta = jax.nn.sigmoid(tail) * valid
    log_decay = small_ref[0:1, :] * softplus(tail + small_ref[1:2, :]) * valid

    def active(slot, head):
        return silu(conv_active(padded, taps_ref, slot * wide + head * 128, count))

    def unit(x):
        return x * lax.rsqrt(row_dot(x, x) + EPS_KEY)

    queries = [unit(active(0, h)) * 128**-0.5 for h in range(heads)]
    keys = [[unit(active(1 + j, h)) for j in range(2)] for h in range(heads)]
    values = [[active(3 + j, h) for j in range(2)] for h in range(heads)]
    work = []
    for g in range(groups):
        rows = slice(g * GROUP, (g + 1) * GROUP)
        cum, across = cum_decays(log_decay[rows])
        for h in range(heads):
            key = jnp.concatenate([keys[h][0][rows], keys[h][1][rows]], axis=0)
            value = jnp.concatenate([values[h][0][rows], values[h][1][rows]], axis=0)
            c, c_two, end, b, pair, view = group_setup(level, beta[rows], cum, across, h, heads)
            gram = mm(key, key, "nt")
            work.append((g, h, rows, key, value, c, c_two, end, b, view, b * pair * gram))
    solves = inverses([w[-1] for w in work], level)
    raws = [[None] * groups for _ in range(heads)]
    ready = []
    for (g, h, rows, key, value, c, c_two, end, b, view, _), solve in zip(work, solves):
        solve_ref[g, h] = solve
        query = queries[h][rows]
        weights = view * mm(query, key, "nt")
        key_solve = mm(solve, b * jnp.exp(c_two) * key, "nn")
        pseudo = mm(solve, b * value, "nn")
        ready.append((query, weights, key_solve, pseudo))
    for (g, h, rows, key, value, c, c_two, end, b, view, _), made in zip(work, ready):
        query, weights, key_solve, pseudo = made
        state = carried[h]
        state_ref[g, h] = state
        fresh = pseudo - mm(key_solve, state, "nn")
        fresh_ref[g, h] = fresh
        carried[h] = jnp.exp(end) * state + mm(jnp.exp(end - c_two) * key, fresh, "tn")
        raws[h][g] = jnp.exp(c) * mm(query, state, "nn") + mm(weights, fresh, "nn")
    for h in range(heads):
        cols = slice(h * 128, (h + 1) * 128)
        raw = jnp.concatenate(raws[h], axis=0)
        raw_ref[:, cols] = raw
        scale = lax.rsqrt(jnp.mean(raw * raw, axis=1, keepdims=True) + EPS_HEAD)
        gated = raw * scale * small_ref[2:3, :] * silu(mixed_ref[:, 5 * wide + h * 128 : 5 * wide + (h + 1) * 128]) * valid
        out_ref[:, cols] = gated.astype(LOW)
    end_ref[...] = carried[...]


def backward_kernel(
    heads, first, info_ref, mixed_ref, halo_ref, raw_ref, grad_ref, taps_ref, small_ref, level_ref,
    solve_ref, fresh_ref, state_ref, start_ref, rim_ref,
    grad_mixed_ref, grad_taps_ref, grad_small_ref, end_ref, last_rim_ref,
    carried, padded, spread,
):
    step = pl.program_id(0)
    count = mixed_ref.shape[0]
    block = pl.num_programs(0) - 1 - step + first // count
    groups = count // GROUP
    wide = heads * 128

    @pl.when(step == 0)
    def _():
        carried[...] = start_ref[...]
        spread[0:8, :] = rim_ref[...]
        grad_taps_ref[...] = jnp.zeros_like(grad_taps_ref)
        grad_small_ref[...] = jnp.zeros_like(grad_small_ref)

    spread[count : count + 8, :] = spread[0:8, :]
    padded[0:8, :] = jnp.where(block > 0, halo_ref[:, : 5 * wide], 0.0)
    padded[8 : 8 + count, :] = mixed_ref[:, : 5 * wide]
    valid = (block * count + place((count, 1), 0) < info_ref[0]).astype(F32)
    level = level_ref[...]
    strict = level >= 0
    tail = mixed_ref[:, 6 * wide :]
    sigmoid_tail = jax.nn.sigmoid(tail)
    beta = sigmoid_tail * valid
    log_decay = small_ref[0:1, :] * softplus(tail + small_ref[1:2, :]) * valid
    lanes = place((1, 128), 1)

    grad_raws = []
    for h in range(heads):
        cols = slice(h * 128, (h + 1) * 128)
        gate_cols = slice(5 * wide + h * 128, 5 * wide + (h + 1) * 128)
        raw, gate = raw_ref[:, cols], mixed_ref[:, gate_cols]
        grad = grad_ref[:, cols] * valid
        sig = jax.nn.sigmoid(gate)
        scale = lax.rsqrt(jnp.mean(raw * raw, axis=1, keepdims=True) + EPS_HEAD)
        shaped = raw * scale
        gain = small_ref[2:3, :]
        grad_mixed_ref[:, gate_cols] = (grad * shaped * gain * sig * (1.0 + gate * (1.0 - sig))).astype(LOW)
        grad_normed = grad * gate * sig
        grad_small_ref[2:3, :] += jnp.sum(grad_normed * shaped, axis=0, keepdims=True)
        grad_shaped = grad_normed * gain
        grad_raws.append(scale * (grad_shaped - shaped * jnp.mean(grad_shaped * shaped, axis=1, keepdims=True)))

    def summed(slot, head):
        return conv_active(padded, taps_ref, slot * wide + head * 128, count)

    def unit(x):
        return x * lax.rsqrt(row_dot(x, x) + EPS_KEY)

    queries = [unit(silu(summed(0, h))) * 128**-0.5 for h in range(heads)]
    keys = [[unit(silu(summed(1 + j, h))) for j in range(2)] for h in range(heads)]
    values = [[silu(summed(3 + j, h)) for j in range(2)] for h in range(heads)]
    work = []
    for g in reversed(range(groups)):
        rows = slice(g * GROUP, (g + 1) * GROUP)
        cum, across = cum_decays(log_decay[rows])
        for h in range(heads):
            key = jnp.concatenate([keys[h][0][rows], keys[h][1][rows]], axis=0)
            value = jnp.concatenate([values[h][0][rows], values[h][1][rows]], axis=0)
            c, c_two, end, b, pair, view = group_setup(level, beta[rows], cum, across, h, heads)
            query, grad_raw = queries[h][rows], grad_raws[h][rows]
            scores = view * mm(query, key, "nt")
            late = mm(scores, grad_raw, "tn")
            grad_scores = view * mm(grad_raw, fresh_ref[g, h], "nt")
            work.append((g, h, rows, key, value, c, c_two, end, b, pair, query, grad_raw, late, grad_scores))
    grad_parts = [[[None] * groups for _ in range(5)] for _ in range(heads)]
    grad_betas, grad_cums = [0.0] * groups, [0.0] * groups
    for (g, h, rows, key, value, c, c_two, end, b, pair, query, grad_raw, late, grad_scores) in work:
        state, fresh, solve = state_ref[g, h], fresh_ref[g, h], solve_ref[g, h]
        grad_state = carried[h]
        grow, fade, all_fade = jnp.exp(c_two), jnp.exp(end - c_two), jnp.exp(end)
        grad_seen = jnp.exp(c) * grad_raw
        grad_fresh = late + mm(fade * key, grad_state, "nn")
        adjoint = mm(solve, grad_fresh, "tn")
        carried[h] = (
            all_fade * grad_state
            + mm(query, grad_seen, "tn")
            - mm(b * grow * key, adjoint, "tn")
        )
        grad_query = mm(grad_seen, state, "nt") + mm(grad_scores, key, "nn")
        part_one = mm(grad_scores, query, "tn")
        part_two = fade * mm(fresh, grad_state, "nt")
        part_three = -mm(adjoint, state, "nt")
        coupled = jnp.where(strict, -mm(adjoint, fresh, "nt"), 0.0) * pair
        part_four = mm(coupled, key, "nn")
        part_five = mm(b * coupled, key, "tn")
        grad_key = part_one + part_two + b * grow * part_three + b * part_four + part_five
        grad_value = b * adjoint
        through = grow * row_dot(part_three, key)
        pulled = row_dot(part_four, key)
        grad_b = row_dot(adjoint, value) + through + pulled
        ends = row_dot(part_two, key)
        grad_c = b * (through + pulled) - ends - row_dot(part_one + part_five, key)
        grad_c = row_dot(query, grad_query) + grad_c[:GROUP] + grad_c[GROUP:]
        grad_end = jnp.sum(ends) + jnp.sum(all_fade * grad_state * state)
        grad_c = grad_c + jnp.where(place((GROUP, 1), 0) == GROUP - 1, grad_end, 0.0)
        grad_cums[g] = grad_cums[g] + jnp.where(lanes == 2 * heads + h, grad_c, 0.0)
        for j in range(2):
            half = slice(j * GROUP, (j + 1) * GROUP)
            grad_betas[g] = grad_betas[g] + jnp.where(lanes == j * heads + h, grad_b[half], 0.0)
            grad_parts[h][1 + j][g] = grad_key[half]
            grad_parts[h][3 + j][g] = grad_value[half]
        grad_parts[h][0][g] = grad_query
    triu = (place((GROUP, GROUP), 0) <= place((GROUP, GROUP), 1)).astype(F32)
    grad_log = jnp.concatenate([mm_high(triu, x, "nn") for x in grad_cums], axis=0)
    grad_beta = jnp.concatenate(grad_betas, axis=0)
    grad_decay = grad_log * small_ref[0:1, :] * valid * jax.nn.sigmoid(tail + small_ref[1:2, :])
    grad_mixed_ref[:, 6 * wide :] = (
        grad_beta * beta * (1.0 - sigmoid_tail) + grad_decay
    ).astype(LOW)
    grad_small_ref[0:1, :] += jnp.sum(grad_log * log_decay, axis=0, keepdims=True)
    grad_small_ref[1:2, :] += jnp.sum(grad_decay, axis=0, keepdims=True)

    for h in range(heads):
        for slot in range(5):
            cols = slice(slot * wide + h * 128, slot * wide + (h + 1) * 128)
            grad = jnp.concatenate(grad_parts[h][slot], axis=0)
            pre = summed(slot, h)
            sig = jax.nn.sigmoid(pre)
            if slot < 3:
                act = pre * sig
                scale = lax.rsqrt(row_dot(act, act) + EPS_KEY)
                shaped = act * scale
                if slot == 0:
                    grad = grad * 128**-0.5
                grad = scale * (grad - shaped * row_dot(grad, shaped))
            grad = grad * sig * (1.0 + pre * (1.0 - sig))
            spread[0:count, cols] = grad
            back = 0.0
            for ahead in range(4):
                back = back + spread[pl.ds(ahead, count), cols] * taps_ref[3 - ahead : 4 - ahead, cols]
            grad_mixed_ref[:, cols] = back.astype(LOW)
            for tap in range(4):
                grad_taps_ref[tap : tap + 1, cols] += jnp.sum(
                    grad * padded[pl.ds(5 + tap, count), cols], axis=0, keepdims=True
                )
    end_ref[...] = carried[...]
    last_rim_ref[...] = spread[0:8, :]


def step_tokens(tokens):
    return min(128, tokens)


def block_specs(heads, count, first, per, order):
    wide = heads * 128
    all_wide = 6 * wide + 128
    skip, per = first // count, max(per // count, 1)

    def moved(i, info):
        return ((i // per) ^ info[1]) * per + i % per

    whole = lambda *shape: pl.BlockSpec(shape, lambda i, info: (0,) * len(shape))
    return dict(
        mixed=pl.BlockSpec((count, all_wide), lambda i, info: (order(i) + skip, 0)),
        halo=pl.BlockSpec(
            (8, all_wide), lambda i, info: (jnp.maximum((order(i) + skip) * (count // 8) - 1, 0), 0)
        ),
        mixed_part=pl.BlockSpec((count, all_wide), lambda i, info: (order(i), 0)),
        head=pl.BlockSpec((count, wide), lambda i, info: (order(i), 0)),
        moved_head=pl.BlockSpec((count, wide), lambda i, info: (moved(order(i), info), 0)),
        taps=whole(8, 5 * wide),
        small=whole(8, 128),
        level=whole(2 * GROUP, 2 * GROUP),
        state=whole(heads, 128, 128),
        kept=pl.BlockSpec((count // GROUP, heads, 128, 128), lambda i, info: (order(i), 0, 0, 0)),
    )


VMEM_BYTES = 56 * 2**20


def mixer_forward(heads, first, tokens, info, mixed, taps, small, level, start):
    count = step_tokens(tokens)
    steps = tokens // count
    wide = heads * 128
    s = block_specs(heads, count, first, count, lambda i: i)
    kept = jax.ShapeDtypeStruct((tokens // GROUP, heads, 128, 128), F32)
    return pl.pallas_call(
        functools.partial(forward_kernel, heads, first),
        grid_spec=pltpu.PrefetchScalarGridSpec(
            num_scalar_prefetch=1,
            grid=(steps,),
            in_specs=[s["mixed"], s["halo"], s["taps"], s["small"], s["level"], s["state"]],
            out_specs=[s["head"], s["head"], s["kept"], s["kept"], s["kept"], s["state"]],
            scratch_shapes=[pltpu.VMEM((heads, 128, 128), F32), pltpu.VMEM((count + 8, 5 * wide), F32)],
        ),
        out_shape=[
            jax.ShapeDtypeStruct((tokens, wide), LOW),
            jax.ShapeDtypeStruct((tokens, wide), F32),
            kept, kept, kept,
            jax.ShapeDtypeStruct(start.shape, F32),
        ],
        compiler_params=pltpu.CompilerParams(vmem_limit_bytes=VMEM_BYTES),
        cost_estimate=pl.CostEstimate(
            flops=tokens * heads * (4_000_000 if first == 0 else 18_000_000), bytes_accessed=tokens * heads * 10_000, transcendentals=0
        ),
        name="mixer_forward",
    )(info, mixed, mixed, taps, small, level, start)


def mixer_backward(
    heads, first, tokens, per, info, mixed, raw, grad, taps, small, level, solve, fresh, state, start, rim
):
    count = step_tokens(tokens)
    steps = tokens // count
    wide = heads * 128
    s = block_specs(heads, count, first, per, lambda i: steps - 1 - i)
    return pl.pallas_call(
        functools.partial(backward_kernel, heads, first),
        grid_spec=pltpu.PrefetchScalarGridSpec(
            num_scalar_prefetch=1,
            grid=(steps,),
            in_specs=[
                s["mixed"], s["halo"], s["head"], s["moved_head"], s["taps"], s["small"], s["level"],
                s["kept"], s["kept"], s["kept"], s["state"], s["taps"],
            ],
            out_specs=[s["mixed_part"], s["taps"], s["small"], s["state"], s["taps"]],
            scratch_shapes=[
                pltpu.VMEM((heads, 128, 128), F32),
                pltpu.VMEM((count + 8, 5 * wide), F32),
                pltpu.VMEM((count + 8, 5 * wide), F32),
            ],
        ),
        out_shape=[
            jax.ShapeDtypeStruct((tokens, mixed.shape[1]), LOW),
            jax.ShapeDtypeStruct((8, 5 * wide), F32),
            jax.ShapeDtypeStruct((8, 128), F32),
            jax.ShapeDtypeStruct(start.shape, F32),
            jax.ShapeDtypeStruct(rim.shape, F32),
        ],
        compiler_params=pltpu.CompilerParams(vmem_limit_bytes=VMEM_BYTES),
        cost_estimate=pl.CostEstimate(
            flops=tokens * heads * 26_000_000, bytes_accessed=tokens * heads * 10_000, transcendentals=0
        ),
        name="mixer_backward",
    )(info, mixed, mixed, raw, grad, taps, small, level, solve, fresh, state, start, rim)


def swap(array, axis, bits):
    return lax.ppermute(array, axis, [(i, i ^ bits) for i in range(lax.axis_size(axis))])


def on_square():
    return lax.axis_size("seq") == 4


def power_of_two(axis):
    return lax.axis_size(axis) & (lax.axis_size(axis) - 1) == 0


def after(array, *others):
    return lax.optimization_barrier((array,) + others)[0]


def spread_out(array):
    if not on_square():
        whole = lax.all_gather(array, "seq")
        return [whole[i] for i in range(whole.shape[0])]
    far, beside, below = (swap(array, "seq", bits) for bits in (3, 1, 2))
    return [array, beside, below, far]


def in_place_order(blocks):
    if not on_square():
        return jnp.concatenate(blocks, axis=0)
    me = lax.axis_index("seq")
    size = blocks[0].shape[0]
    out = jnp.zeros((len(blocks) * size,) + blocks[0].shape[1:], blocks[0].dtype)
    for bits, block in enumerate(blocks):
        out = lax.dynamic_update_slice(out, block, ((me ^ bits) * size, 0))
    return out


def row_block(array, index):
    size = array.shape[0] // lax.axis_size("seq")
    return lax.dynamic_slice_in_dim(array, index * size, size, 0)


def to_send(array):
    if not on_square():
        return [array.astype(LOW)]
    me = lax.axis_index("seq")
    return [row_block(array, me ^ bits).astype(LOW) for bits in (3, 1, 2)]


def send(blocks):
    if not on_square():
        return [lax.psum_scatter(blocks[0], "seq", scatter_dimension=0, tiled=True)]
    return [swap(block, "seq", bits) for bits, block in zip((3, 1, 2), blocks)]


def total(array, got):
    if not on_square():
        return got[0].astype(F32)
    return row_block(array, lax.axis_index("seq")) + sum(block.astype(F32) for block in got)


def exchange(blocks):
    if not on_square():
        return lax.all_to_all(blocks, "seq", 0, 0, tiled=True)
    me = lax.axis_index("seq")
    others = (3, 1, 2)
    sends = lax.optimization_barrier(tuple(lax.dynamic_index_in_dim(blocks, me ^ bits, 0, True) for bits in others))
    got = lax.optimization_barrier(tuple(swap(block, "seq", bits) for bits, block in zip(others, sends)))
    out = blocks
    for bits, block in zip(others, got):
        out = lax.dynamic_update_slice(out, block, (me ^ bits, 0, 0))
    return out


def sum_over(array, axis):
    if not power_of_two(axis):
        return lax.psum(array, axis)
    bits = 1
    while bits < lax.axis_size(axis):
        array = array + swap(array, axis, bits)
        bits *= 2
    return array


def gather_rows(mine):
    whole = lax.all_gather(mine, "rows", axis=0)
    rows, count, size, width = whole.shape
    return whole.transpose(1, 0, 2, 3).reshape(count * rows * size, width)


def by_rows(grad):
    count, rows = lax.axis_size("seq"), lax.axis_size("rows")
    size = grad.shape[0] // (count * rows)
    grad = grad.astype(LOW).reshape(count, rows, size, grad.shape[1])
    return grad.transpose(1, 0, 2, 3).reshape(-1, grad.shape[3])


def sum_rows(grad):
    count = lax.axis_size("seq")
    summed = lax.psum_scatter(grad, "rows", scatter_dimension=0, tiled=True)
    return summed.reshape(count, -1, grad.shape[1])


def project(left, right):
    return jnp.dot(left, right, preferred_element_type=F32)


def outer_sum(left, right):
    return lax.dot_general(left, right, FORMS["tn"], preferred_element_type=F32)


def back_project(left, right):
    return lax.dot_general(left, right, FORMS["nt"], preferred_element_type=F32)


def norm_scale(features):
    return lax.rsqrt(jnp.mean(features * features, axis=-1, keepdims=True) + EPS_NORM)


def norm_back(features, scale, grad):
    return scale * grad - features * scale**3 * jnp.mean(grad * features, axis=-1, keepdims=True)


def on_device(
    block_input, valid_length, query_weight, key_weight, value_weight, beta_weight, decay_weight, gate_weight,
    out_weight, ffn_gate_weight, ffn_up_weight, ffn_down_weight, norm_gain, ffn_norm_gain, head_norm_gain,
    decay_log, decay_bias, conv_weight, output_grad,
):
    count = lax.axis_size("seq")
    me = lax.axis_index("seq")
    rows_here, tokens_here, model_width = block_input.shape
    share = query_weight.shape[0]
    head_count = decay_log.shape[0]
    heads = max(1, head_count // count)
    blocks = head_count // heads
    copies = count // blocks
    block = me // copies
    wide = heads * 128
    hidden = ffn_gate_weight.shape[1] // count

    def cut(weight, pieces, at):
        width = weight.shape[1] // (pieces * blocks)
        at = at // copies
        return [
            weight[:, (p * blocks + at) * width : (p * blocks + at + 1) * width] for p in range(pieces)
        ]

    def cut_hidden(weight, at):
        return [weight[:, at * hidden : (at + 1) * hidden]]

    gains = jnp.stack([norm_gain, ffn_norm_gain], axis=1)

    def tail_of(at):
        parts = cut(beta_weight, 2, at) + cut(decay_weight, 1, at) + [gains]
        return parts + [jnp.zeros((share, 128 - 3 * heads - 2), LOW)]

    def first_of(at):
        parts = cut(query_weight, 1, at) + cut(key_weight, 2, at) + cut(value_weight, 2, at)
        return jnp.concatenate(parts + cut(gate_weight, 1, at) + tail_of(at), axis=1)

    def rest_of(at):
        order = [at ^ bits for bits in range(count)] if on_square() else range(0, count, copies)
        parts = sum((cut(out_weight, 1, other) for other in order), [])
        parts += cut_hidden(ffn_gate_weight, at) + cut_hidden(ffn_up_weight, at) + cut_hidden(ffn_down_weight, at)
        return jnp.concatenate(parts, axis=1)

    def pack(part):
        return jnp.stack([part(at) for at in range(count)])

    first_share = exchange(pack(first_of))
    mixed_weight = gather_rows(first_share)
    own = after(block_input.reshape(tokens_here, model_width), first_share)
    everyone = in_place_order(spread_out(own))
    rest_pack, everyone = lax.optimization_barrier((pack(rest_of), everyone))
    rest_share = exchange(rest_pack)
    rest_weight = gather_rows(rest_share)
    out_all = rest_weight[:, : blocks * wide]
    ffn_in = rest_weight[:, blocks * wide : blocks * wide + 2 * hidden]
    ffn_down = rest_weight[:, blocks * wide + 2 * hidden :]
    if on_square():
        out_own = out_all[:, :wide]
    else:
        out_own = lax.dynamic_slice_in_dim(out_all, block * wide, wide, 1)
    gain_first = mixed_weight[:, 6 * wide + 3 * heads].astype(F32)
    gain_second = mixed_weight[:, 6 * wide + 3 * heads + 1].astype(F32)

    def block_lanes(vector, first):
        mine = lax.dynamic_slice_in_dim(vector, block * heads, heads)
        return jnp.pad(mine, (first, 128 - first - heads))

    small = jnp.stack([block_lanes(-jnp.exp(decay_log), 2 * heads), block_lanes(decay_bias, 2 * heads), head_norm_gain])
    small = jnp.pad(small, ((0, 5), (0, 0)))
    taps = [
        lax.dynamic_slice_in_dim(conv_weight, (slot * blocks + block) * wide, wide, 1) for slot in range(5)
    ]
    taps = jnp.pad(jnp.concatenate(taps, axis=1), ((0, 8 - conv_weight.shape[0]), (0, 0)))
    level = level_table()
    info = jnp.stack([valid_length[0], me if on_square() else jnp.int32(0)])

    length = count * tokens_here
    part = length // 2
    tie = lax.optimization_barrier

    tokens_all = everyone.astype(F32)
    normed = (tokens_all * norm_scale(tokens_all) * gain_first).astype(LOW)
    mixed = project(normed, mixed_weight)
    mixed, own_grad = tie((mixed, output_grad.reshape(tokens_here, model_width)))
    grads_got = spread_out(own_grad)
    zero_state = jnp.zeros((heads, 128, 128), F32)
    gated_a, *kept_a, end = mixer_forward(heads, 0, part, info, mixed, taps, small, level, zero_state)
    end, grads_got, everyone_late = tie((end, grads_got, everyone))
    gated_got_a = spread_out(gated_a)
    gated_b, *kept_b, end = mixer_forward(heads, part, part, info, mixed, taps, small, level, end)
    gated_b, gated_got_a = tie((gated_b, gated_got_a))
    gated_got_b = spread_out(gated_b)
    grad_branch = in_place_order(grads_got)

    def feed_forward(index, gated_got, got=None):
        rows = slice(index * part, (index + 1) * part)
        gated_all = jnp.concatenate(gated_got[:: 1 if on_square() else copies], axis=1)
        second = everyone_late[rows].astype(F32) + back_project(gated_all, out_all)
        normed_two = (second * norm_scale(second) * gain_second).astype(LOW)
        if got is not None:
            normed_two, got = tie((normed_two, got))
        acts = project(normed_two, ffn_in)
        gate_act, up_act = acts[:, :hidden], acts[:, hidden:]
        sig = jax.nn.sigmoid(gate_act)
        hidden_low = (gate_act * sig * up_act).astype(LOW)
        grad_hidden = project(grad_branch[rows], ffn_down)
        grad_acts = [grad_hidden * up_act * sig * (1.0 + gate_act * (1.0 - sig)), grad_hidden * gate_act * sig]
        grad_acts = jnp.concatenate(grad_acts, axis=1).astype(LOW)
        return second, normed_two, hidden_low, grad_acts, back_project(grad_acts, ffn_in), got

    def second_back(index, second, partial, got):
        grad = total(partial, got) * gain_second
        second = row_block(second, me)
        out_grad = row_block(grad_branch[index * part : (index + 1) * part], me)
        return (out_grad.astype(F32) + norm_back(second, norm_scale(second), grad)).astype(LOW)

    second_a, normed_two_a, hidden_a, grad_acts_a, partial_a, _ = feed_forward(0, gated_got_a)
    sends_a, gated_got_b = tie((to_send(partial_a), gated_got_b))
    got_a = send(sends_a)
    second_b, normed_two_b, hidden_b, grad_acts_b, partial_b, got_a = feed_forward(1, gated_got_b, got_a)
    sends_b, hidden_b, grad_acts_b = tie((to_send(partial_b), hidden_b, grad_acts_b))
    got_b = send(sends_b)

    join_parts = lambda a, b: jnp.concatenate([a, b], axis=0)
    normed_two, hidden_low = join_parts(normed_two_a, normed_two_b), join_parts(hidden_a, hidden_b)
    grad_acts = join_parts(grad_acts_a, grad_acts_b)
    early_in = outer_sum(normed_two, grad_acts).astype(LOW)
    early_down = outer_sum(grad_branch, hidden_low).astype(LOW)
    grad_second_a = second_back(0, second_a, partial_a, got_a)
    got_b, early_in, early_down, grad_second_a = tie((got_b, early_in, early_down, grad_second_a))
    grads_two_b = spread_out(second_back(1, second_b, partial_b, got_b))
    early = by_rows(jnp.concatenate([early_in, early_down], axis=1))
    down = back_project(hidden_low, ffn_down)
    down_sends = to_send(down)
    grads_two_b, early, down_sends, grad_second_a = tie((grads_two_b, early, down_sends, grad_second_a))
    early = sum_rows(early)
    grads_two_a = spread_out(grad_second_a)

    grad_gated = project(jnp.concatenate(grads_two_b, axis=0), out_own)
    rim = jnp.zeros((8, 5 * wide), F32)
    grad_pre_b, taps_b, small_b, end, rim = mixer_backward(
        heads, part, part, part // count, info, mixed, kept_b[0], grad_gated, taps, small, level, *kept_b[1:],
        zero_state, rim,
    )
    end, grads_two_a, down_sends = tie((end, grads_two_a, down_sends))
    down_got = send(down_sends)
    grad_gated = project(jnp.concatenate(grads_two_a, axis=0), out_own)
    grad_second = join_parts(in_place_order(grads_two_a), in_place_order(grads_two_b))

    def once(array):
        return array if copies == 1 else array * (me % copies == 0).astype(array.dtype)

    grad_pre_a, taps_a, small_a, end, rim = mixer_backward(
        heads, 0, part, part // count, info, mixed, kept_a[0], grad_gated, taps, small, level, *kept_a[1:], end, rim
    )
    grad_pre = once(join_parts(grad_pre_a, grad_pre_b))
    out_grad = once(outer_sum(grad_second, join_parts(gated_a, gated_b)).astype(LOW))
    late = by_rows(jnp.concatenate([outer_sum(normed, grad_pre).astype(LOW), out_grad], axis=1))
    grad_taps, grad_small = taps_a + taps_b, small_a + small_b
    grad_pre, late, down_got, early, grad_taps, grad_small = tie(
        (grad_pre, late, down_got, early, grad_taps, grad_small)
    )
    late = sum_rows(late)
    grad_normed = back_project(grad_pre, mixed_weight)
    grad_normed_got = send(to_send(grad_normed))

    def at_block(vector, first, width):
        mine = once(vector[first : first + width])
        return lax.dynamic_update_slice(jnp.zeros((blocks * width,), F32), mine, (block * width,))

    flat = [once(grad_small[2]), at_block(grad_small[0], 2 * heads, heads), at_block(grad_small[1], 2 * heads, heads)]
    flat = jnp.concatenate(flat)
    taps_wide = 5 * wide
    flat = jnp.pad(flat, (0, -flat.shape[0] % taps_wide)).reshape(-1, taps_wide)
    pooled = sum_over(jnp.concatenate([once(grad_taps[:4]), flat], axis=0), "rows")
    by_place = lax.dynamic_update_slice(jnp.zeros((blocks, 4, taps_wide), F32), pooled[None, :4], (block, 0, 0))
    pooled = sum_over(jnp.concatenate([by_place.reshape(-1, taps_wide), pooled[4:]], axis=0), "seq")
    ends = [128, 128 + head_count, 128 + 2 * head_count]

    second = row_block(join_parts(second_a, second_b), me)
    result = (second + total(down, down_got)).astype(LOW).reshape(block_input.shape)
    tokens = own.astype(F32)
    grad_tokens = norm_back(tokens, norm_scale(tokens), total(grad_normed, grad_normed_got) * gain_first)
    grad_input = row_block(grad_second, me).astype(F32) + grad_tokens
    grad_input = grad_input.reshape(block_input.shape)

    def join(grads, first, pieces, width, every=copies):
        return jnp.concatenate(
            [
                grads[b, :, first + p * width : first + (p + 1) * width]
                for p in range(pieces)
                for b in range(0, count, every)
            ],
            axis=1,
        ).astype(F32)

    early = exchange(early)
    late, early, result, grad_input, pooled = tie((late, early, result, grad_input, pooled))
    late = exchange(late)
    flat = pooled[4 * blocks :].reshape(-1)
    grad_conv = pooled[: 4 * blocks].reshape(blocks, 4, taps_wide)
    grad_conv = jnp.concatenate(
        [grad_conv[b, :, slot * wide : (slot + 1) * wide] for slot in range(5) for b in range(blocks)], axis=1
    )
    grad_query = join(late, 0, 1, wide)
    grad_key = join(late, wide, 2, wide)
    grad_value = join(late, 3 * wide, 2, wide)
    grad_beta = join(late, 6 * wide, 2, heads)
    grad_decay = join(late, 6 * wide + 2 * heads, 1, heads)
    grad_gate = join(late, 5 * wide, 1, wide)
    grad_ffn_gate = join(early, 0, 1, hidden, 1)
    grad_ffn_up = join(early, hidden, 1, hidden, 1)
    grad_ffn_down = join(early, 2 * hidden, 1, hidden, 1)

    def gain_grad(gain, *pairs):
        summed = sum(jnp.sum(weight.astype(F32) * grad, axis=1) for weight, grad in pairs)
        return summed / gain.astype(F32)

    grad_gain_first = gain_grad(
        norm_gain, (query_weight, grad_query), (key_weight, grad_key), (value_weight, grad_value),
        (beta_weight, grad_beta), (decay_weight, grad_decay), (gate_weight, grad_gate),
    )
    grad_gain_second = gain_grad(ffn_norm_gain, (ffn_gate_weight, grad_ffn_gate), (ffn_up_weight, grad_ffn_up))
    return (
        result,
        grad_input,
        grad_query,
        grad_key,
        grad_value,
        grad_beta,
        grad_decay,
        grad_gate,
        join(late, 6 * wide + 128, 1, wide),
        grad_ffn_gate,
        grad_ffn_up,
        grad_ffn_down,
        grad_gain_first,
        grad_gain_second,
        flat[: ends[0]],
        flat[ends[0] : ends[1]],
        flat[ends[1] : ends[2]],
        grad_conv,
    )


def solution(mesh):
    tokens, weight, vector, whole = P("rows", "seq", None), P(BOTH, None), P(BOTH), P()
    return jax.shard_map(
        on_device,
        mesh=mesh,
        in_specs=(tokens, P("rows")) + (weight,) * 10 + (vector,) * 2 + (whole,) * 4 + (tokens,),
        out_specs=(tokens, tokens) + (weight,) * 10 + (vector,) * 2 + (whole,) * 4,
        check_vma=False,
    )
```

```python
import functools

import jax
import jax.numpy as jnp
from jax import lax
from jax.experimental import pallas as pl
from jax.experimental.pallas import tpu as pltpu
from jax.sharding import PartitionSpec as P

GROUP = 64
EPS_NORM = 1e-06
EPS_KEY = 1e-06
EPS_HEAD = 1e-05
LOW = jnp.bfloat16
F32 = jnp.float32
HIGHEST = lax.Precision.HIGHEST
BOTH = ("seq", "rows")

FORMS = {
    "nn": (((1,), (0,)), ((), ())),
    "nt": (((1,), (1,)), ((), ())),
    "tn": (((0,), (0,)), ((), ())),
}


def split_low(a):
    high = a.astype(LOW)
    return high, (a - high.astype(F32)).astype(LOW)


def mm(a, b, form):
    a_axis = 0 if form == "tn" else 1
    b_axis = 1 if form == "nt" else 0
    a_two = jnp.concatenate(split_low(a), axis=a_axis)
    b_high, b_low = split_low(b)
    b_two = jnp.concatenate([b_high, b_low], axis=1 - b_axis)
    b_two = jnp.concatenate([b_two, b_two], axis=b_axis)
    out = lax.dot_general(a_two, b_two, FORMS[form], preferred_element_type=F32)
    half = out.shape[1] // 2
    return out[:, :half] + out[:, half:]


def mm_low(a, b, form):
    return lax.dot_general(a.astype(LOW), b.astype(LOW), FORMS[form], preferred_element_type=F32)


def mm_high(a, b, form):
    return lax.dot_general(a, b, FORMS[form], precision=HIGHEST, preferred_element_type=F32)


def row_dot(a, b):
    return jnp.sum(a * b, axis=1, keepdims=True)


def place(shape, axis):
    return lax.broadcasted_iota(jnp.int32, shape, axis)


def level_table():
    time = 2 * (jnp.arange(2 * GROUP) % GROUP) + jnp.arange(2 * GROUP) // GROUP
    row, col = time[:, None], time[None, :]
    differ = row ^ col
    level = sum((differ >= 2**m).astype(jnp.int32) for m in range(1, 7))
    return jnp.where(row > col, level, -1)


def inverses(systems, level):
    size = level.shape[0]
    eye = (place((size, size), 0) == place((size, size), 1)).astype(F32)
    found = [eye - jnp.where(level == 0, a, 0.0) for a in systems]
    for m in range(1, 7):
        inner = [mm(jnp.where(level == m, a, 0.0), t, "nn") for a, t in zip(systems, found)]
        found = [t - mm(t, s, "nn") for t, s in zip(found, inner)]
    return found


def conv_active(pad_ref, taps_ref, first, count):
    cols = slice(first, first + 128)
    summed = 0.0
    for back in range(4):
        summed = summed + pad_ref[pl.ds(8 - back, count), cols] * taps_ref[3 - back : 4 - back, cols]
    return summed


def silu(x):
    return x * jax.nn.sigmoid(x)


def softplus(x):
    return jnp.maximum(x, 0.0) + jnp.log1p(jnp.exp(-jnp.abs(x)))


def cum_decays(log_decay):
    tril = (place((GROUP, GROUP), 0) >= place((GROUP, GROUP), 1)).astype(F32)
    across = (place((GROUP, 2 * GROUP), 0) <= place((GROUP, 2 * GROUP), 1) % GROUP).astype(F32)
    return mm_high(tril, log_decay, "nn"), mm_high(log_decay, across, "tn")


def twice(a):
    return jnp.concatenate([a, a], axis=0)


def group_setup(level, beta, cum, across, head, heads):
    lane = 2 * heads + head
    c = cum[:, lane : lane + 1]
    row = across[lane : lane + 1, :]
    c_two = twice(c)
    end = c[GROUP - 1 : GROUP, :]
    b = jnp.concatenate([beta[:, head : head + 1], beta[:, heads + head : heads + head + 1]], axis=0)
    strict = level >= 0
    pair = jnp.where(strict, jnp.exp(jnp.where(strict, c_two - row, 0.0)), 0.0)
    seen = place((GROUP, 2 * GROUP), 1) % GROUP <= place((GROUP, 2 * GROUP), 0)
    view = jnp.where(seen, jnp.exp(jnp.where(seen, c - row, 0.0)), 0.0)
    return c, c_two, end, b, pair, view


def forward_kernel(
    heads, first, info_ref, mixed_ref, halo_ref, taps_ref, small_ref, level_ref, start_ref,
    out_ref, raw_ref, solve_ref, fresh_ref, state_ref, end_ref, carried, padded,
):
    step = pl.program_id(0)
    count = mixed_ref.shape[0]
    block = step + first // count
    groups = count // GROUP
    wide = heads * 128

    @pl.when(step == 0)
    def _():
        carried[...] = start_ref[...]

    padded[0:8, :] = jnp.where(block > 0, halo_ref[:, : 5 * wide], 0.0)
    padded[8 : 8 + count, :] = mixed_ref[:, : 5 * wide]
    valid = (block * count + place((count, 1), 0) < info_ref[0]).astype(F32)
    level = level_ref[...]
    tail = mixed_ref[:, 6 * wide :]
    beta = jax.nn.sigmoid(tail) * valid
    log_decay = small_ref[0:1, :] * softplus(tail + small_ref[1:2, :]) * valid

    def active(slot, head):
        return silu(conv_active(padded, taps_ref, slot * wide + head * 128, count))

    def unit(x):
        return x * lax.rsqrt(row_dot(x, x) + EPS_KEY)

    queries = [unit(active(0, h)) * 128**-0.5 for h in range(heads)]
    keys = [[unit(active(1 + j, h)) for j in range(2)] for h in range(heads)]
    values = [[active(3 + j, h) for j in range(2)] for h in range(heads)]
    work = []
    for g in range(groups):
        rows = slice(g * GROUP, (g + 1) * GROUP)
        cum, across = cum_decays(log_decay[rows])
        for h in range(heads):
            key = jnp.concatenate([keys[h][0][rows], keys[h][1][rows]], axis=0)
            value = jnp.concatenate([values[h][0][rows], values[h][1][rows]], axis=0)
            c, c_two, end, b, pair, view = group_setup(level, beta[rows], cum, across, h, heads)
            gram = mm(key, key, "nt")
            work.append((g, h, rows, key, value, c, c_two, end, b, view, b * pair * gram))
    solves = inverses([w[-1] for w in work], level)
    raws = [[None] * groups for _ in range(heads)]
    ready = []
    for (g, h, rows, key, value, c, c_two, end, b, view, _), solve in zip(work, solves):
        solve_ref[g, h] = solve
        query = queries[h][rows]
        weights = view * mm(query, key, "nt")
        key_solve = mm(solve, b * jnp.exp(c_two) * key, "nn")
        pseudo = mm(solve, b * value, "nn")
        ready.append((query, weights, key_solve, pseudo))
    for (g, h, rows, key, value, c, c_two, end, b, view, _), made in zip(work, ready):
        query, weights, key_solve, pseudo = made
        state = carried[h]
        state_ref[g, h] = state
        fresh = pseudo - mm(key_solve, state, "nn")
        fresh_ref[g, h] = fresh
        carried[h] = jnp.exp(end) * state + mm(jnp.exp(end - c_two) * key, fresh, "tn")
        raws[h][g] = jnp.exp(c) * mm(query, state, "nn") + mm(weights, fresh, "nn")
    for h in range(heads):
        cols = slice(h * 128, (h + 1) * 128)
        raw = jnp.concatenate(raws[h], axis=0)
        raw_ref[:, cols] = raw
        scale = lax.rsqrt(jnp.mean(raw * raw, axis=1, keepdims=True) + EPS_HEAD)
        gated = raw * scale * small_ref[2:3, :] * silu(mixed_ref[:, 5 * wide + h * 128 : 5 * wide + (h + 1) * 128]) * valid
        out_ref[:, cols] = gated.astype(LOW)
    end_ref[...] = carried[...]


def backward_kernel(
    heads, first, pieces, info_ref, mixed_ref, halo_ref, raw_ref, taps_ref, small_ref, level_ref,
    solve_ref, fresh_ref, state_ref, start_ref, rim_ref, *refs,
):
    grad_refs = refs[:pieces]
    grad_mixed_ref, grad_taps_ref, grad_small_ref, end_ref, last_rim_ref, carried, padded, spread = refs[pieces:]
    step = pl.program_id(0)
    count = mixed_ref.shape[0]
    block = pl.num_programs(0) - 1 - step + first // count
    groups = count // GROUP
    wide = heads * 128

    @pl.when(step == 0)
    def _():
        carried[...] = start_ref[...]
        spread[0:8, :] = rim_ref[...]
        grad_taps_ref[...] = jnp.zeros_like(grad_taps_ref)
        grad_small_ref[...] = jnp.zeros_like(grad_small_ref)

    spread[count : count + 8, :] = spread[0:8, :]
    padded[0:8, :] = jnp.where(block > 0, halo_ref[:, : 5 * wide], 0.0)
    padded[8 : 8 + count, :] = mixed_ref[:, : 5 * wide]
    valid = (block * count + place((count, 1), 0) < info_ref[0]).astype(F32)
    level = level_ref[...]
    strict = level >= 0
    tail = mixed_ref[:, 6 * wide :]
    sigmoid_tail = jax.nn.sigmoid(tail)
    beta = sigmoid_tail * valid
    log_decay = small_ref[0:1, :] * softplus(tail + small_ref[1:2, :]) * valid
    lanes = place((1, 128), 1)

    grad_raws = []
    for h in range(heads):
        cols = slice(h * 128, (h + 1) * 128)
        gate_cols = slice(5 * wide + h * 128, 5 * wide + (h + 1) * 128)
        raw, gate = raw_ref[:, cols], mixed_ref[:, gate_cols]
        grad = jnp.concatenate([ref[:, cols] for ref in grad_refs], axis=0) * valid
        sig = jax.nn.sigmoid(gate)
        scale = lax.rsqrt(jnp.mean(raw * raw, axis=1, keepdims=True) + EPS_HEAD)
        shaped = raw * scale
        gain = small_ref[2:3, :]
        grad_mixed_ref[:, gate_cols] = (grad * shaped * gain * sig * (1.0 + gate * (1.0 - sig))).astype(LOW)
        grad_normed = grad * gate * sig
        grad_small_ref[2:3, :] += jnp.sum(grad_normed * shaped, axis=0, keepdims=True)
        grad_shaped = grad_normed * gain
        grad_raws.append(scale * (grad_shaped - shaped * jnp.mean(grad_shaped * shaped, axis=1, keepdims=True)))

    def summed(slot, head):
        return conv_active(padded, taps_ref, slot * wide + head * 128, count)

    def unit(x):
        return x * lax.rsqrt(row_dot(x, x) + EPS_KEY)

    queries = [unit(silu(summed(0, h))) * 128**-0.5 for h in range(heads)]
    keys = [[unit(silu(summed(1 + j, h))) for j in range(2)] for h in range(heads)]
    values = [[silu(summed(3 + j, h)) for j in range(2)] for h in range(heads)]
    work = []
    for g in reversed(range(groups)):
        rows = slice(g * GROUP, (g + 1) * GROUP)
        cum, across = cum_decays(log_decay[rows])
        for h in range(heads):
            key = jnp.concatenate([keys[h][0][rows], keys[h][1][rows]], axis=0)
            value = jnp.concatenate([values[h][0][rows], values[h][1][rows]], axis=0)
            c, c_two, end, b, pair, view = group_setup(level, beta[rows], cum, across, h, heads)
            query, grad_raw = queries[h][rows], grad_raws[h][rows]
            scores = view * mm(query, key, "nt")
            late = mm(scores, grad_raw, "tn")
            grad_scores = view * mm(grad_raw, fresh_ref[g, h], "nt")
            work.append((g, h, rows, key, value, c, c_two, end, b, pair, query, grad_raw, late, grad_scores))
    grad_parts = [[[None] * groups for _ in range(5)] for _ in range(heads)]
    grad_betas, grad_cums = [0.0] * groups, [0.0] * groups
    for (g, h, rows, key, value, c, c_two, end, b, pair, query, grad_raw, late, grad_scores) in work:
        state, fresh, solve = state_ref[g, h], fresh_ref[g, h], solve_ref[g, h]
        grad_state = carried[h]
        grow, fade, all_fade = jnp.exp(c_two), jnp.exp(end - c_two), jnp.exp(end)
        grad_seen = jnp.exp(c) * grad_raw
        grad_fresh = late + mm(fade * key, grad_state, "nn")
        adjoint = mm(solve, grad_fresh, "tn")
        carried[h] = (
            all_fade * grad_state
            + mm(query, grad_seen, "tn")
            - mm(b * grow * key, adjoint, "tn")
        )
        grad_query = mm(grad_seen, state, "nt") + mm(grad_scores, key, "nn")
        part_one = mm(grad_scores, query, "tn")
        part_two = fade * mm(fresh, grad_state, "nt")
        part_three = -mm(adjoint, state, "nt")
        coupled = jnp.where(strict, -mm(adjoint, fresh, "nt"), 0.0) * pair
        part_four = mm(coupled, key, "nn")
        part_five = mm(b * coupled, key, "tn")
        grad_key = part_one + part_two + b * grow * part_three + b * part_four + part_five
        grad_value = b * adjoint
        through = grow * row_dot(part_three, key)
        pulled = row_dot(part_four, key)
        grad_b = row_dot(adjoint, value) + through + pulled
        ends = row_dot(part_two, key)
        grad_c = b * (through + pulled) - ends - row_dot(part_one + part_five, key)
        grad_c = row_dot(query, grad_query) + grad_c[:GROUP] + grad_c[GROUP:]
        grad_end = jnp.sum(ends) + jnp.sum(all_fade * grad_state * state)
        grad_c = grad_c + jnp.where(place((GROUP, 1), 0) == GROUP - 1, grad_end, 0.0)
        grad_cums[g] = grad_cums[g] + jnp.where(lanes == 2 * heads + h, grad_c, 0.0)
        for j in range(2):
            half = slice(j * GROUP, (j + 1) * GROUP)
            grad_betas[g] = grad_betas[g] + jnp.where(lanes == j * heads + h, grad_b[half], 0.0)
            grad_parts[h][1 + j][g] = grad_key[half]
            grad_parts[h][3 + j][g] = grad_value[half]
        grad_parts[h][0][g] = grad_query
    triu = (place((GROUP, GROUP), 0) <= place((GROUP, GROUP), 1)).astype(F32)
    grad_log = jnp.concatenate([mm_high(triu, x, "nn") for x in grad_cums], axis=0)
    grad_beta = jnp.concatenate(grad_betas, axis=0)
    grad_decay = grad_log * small_ref[0:1, :] * valid * jax.nn.sigmoid(tail + small_ref[1:2, :])
    grad_mixed_ref[:, 6 * wide :] = (
        grad_beta * beta * (1.0 - sigmoid_tail) + grad_decay
    ).astype(LOW)
    grad_small_ref[0:1, :] += jnp.sum(grad_log * log_decay, axis=0, keepdims=True)
    grad_small_ref[1:2, :] += jnp.sum(grad_decay, axis=0, keepdims=True)

    for h in range(heads):
        for slot in range(5):
            cols = slice(slot * wide + h * 128, slot * wide + (h + 1) * 128)
            grad = jnp.concatenate(grad_parts[h][slot], axis=0)
            pre = summed(slot, h)
            sig = jax.nn.sigmoid(pre)
            if slot < 3:
                act = pre * sig
                scale = lax.rsqrt(row_dot(act, act) + EPS_KEY)
                shaped = act * scale
                if slot == 0:
                    grad = grad * 128**-0.5
                grad = scale * (grad - shaped * row_dot(grad, shaped))
            grad = grad * sig * (1.0 + pre * (1.0 - sig))
            spread[0:count, cols] = grad
            back = 0.0
            for ahead in range(4):
                back = back + spread[pl.ds(ahead, count), cols] * taps_ref[3 - ahead : 4 - ahead, cols]
            grad_mixed_ref[:, cols] = back.astype(LOW)
            for tap in range(4):
                grad_taps_ref[tap : tap + 1, cols] += jnp.sum(
                    grad * padded[pl.ds(5 + tap, count), cols], axis=0, keepdims=True
                )
    end_ref[...] = carried[...]
    last_rim_ref[...] = spread[0:8, :]


def step_tokens(tokens):
    return min(256, tokens)


def block_specs(heads, count, first, per, order):
    wide = heads * 128
    all_wide = 6 * wide + 128
    skip = first // count
    piece = min(per, count)
    per, pieces = per // piece, count // piece

    def moved(j):
        def at(i, info):
            i = order(i) * pieces + j
            return (((i // per) ^ info[1]) * per + i % per, 0)

        return at

    whole = lambda *shape: pl.BlockSpec(shape, lambda i, info: (0,) * len(shape))
    return dict(
        mixed=pl.BlockSpec((count, all_wide), lambda i, info: (order(i) + skip, 0)),
        halo=pl.BlockSpec(
            (8, all_wide), lambda i, info: (jnp.maximum((order(i) + skip) * (count // 8) - 1, 0), 0)
        ),
        mixed_part=pl.BlockSpec((count, all_wide), lambda i, info: (order(i), 0)),
        head=pl.BlockSpec((count, wide), lambda i, info: (order(i), 0)),
        moved_head=[pl.BlockSpec((piece, wide), moved(j)) for j in range(pieces)],
        taps=whole(8, 5 * wide),
        small=whole(8, 128),
        level=whole(2 * GROUP, 2 * GROUP),
        state=whole(heads, 128, 128),
        kept=pl.BlockSpec((count // GROUP, heads, 128, 128), lambda i, info: (order(i), 0, 0, 0)),
    )


VMEM_BYTES = 40 * 2**20


def mixer_forward(heads, first, tokens, info, mixed, taps, small, level, start):
    count = step_tokens(tokens)
    steps = tokens // count
    wide = heads * 128
    s = block_specs(heads, count, first, count, lambda i: i)
    kept = jax.ShapeDtypeStruct((tokens // GROUP, heads, 128, 128), F32)
    return pl.pallas_call(
        functools.partial(forward_kernel, heads, first),
        grid_spec=pltpu.PrefetchScalarGridSpec(
            num_scalar_prefetch=1,
            grid=(steps,),
            in_specs=[s["mixed"], s["halo"], s["taps"], s["small"], s["level"], s["state"]],
            out_specs=[s["head"], s["head"], s["kept"], s["kept"], s["kept"], s["state"]],
            scratch_shapes=[pltpu.VMEM((heads, 128, 128), F32), pltpu.VMEM((count + 8, 5 * wide), F32)],
        ),
        out_shape=[
            jax.ShapeDtypeStruct((tokens, wide), LOW),
            jax.ShapeDtypeStruct((tokens, wide), F32),
            kept, kept, kept,
            jax.ShapeDtypeStruct(start.shape, F32),
        ],
        compiler_params=pltpu.CompilerParams(vmem_limit_bytes=VMEM_BYTES),
        cost_estimate=pl.CostEstimate(
            flops=tokens * heads * (4_000_000 if first == 0 else 18_000_000), bytes_accessed=tokens * heads * 10_000, transcendentals=0
        ),
        name="mixer_forward",
    )(info, mixed, mixed, taps, small, level, start)


def mixer_backward(
    heads, first, tokens, per, info, mixed, raw, grad, taps, small, level, solve, fresh, state, start, rim
):
    count = step_tokens(tokens)
    steps = tokens // count
    wide = heads * 128
    s = block_specs(heads, count, first, per, lambda i: steps - 1 - i)
    return pl.pallas_call(
        functools.partial(backward_kernel, heads, first, len(s["moved_head"])),
        grid_spec=pltpu.PrefetchScalarGridSpec(
            num_scalar_prefetch=1,
            grid=(steps,),
            in_specs=[
                s["mixed"], s["halo"], s["head"], s["taps"], s["small"], s["level"],
                s["kept"], s["kept"], s["kept"], s["state"], s["taps"], *s["moved_head"],
            ],
            out_specs=[s["mixed_part"], s["taps"], s["small"], s["state"], s["taps"]],
            scratch_shapes=[
                pltpu.VMEM((heads, 128, 128), F32),
                pltpu.VMEM((count + 8, 5 * wide), F32),
                pltpu.VMEM((count + 8, 5 * wide), F32),
            ],
        ),
        out_shape=[
            jax.ShapeDtypeStruct((tokens, mixed.shape[1]), LOW),
            jax.ShapeDtypeStruct((8, 5 * wide), F32),
            jax.ShapeDtypeStruct((8, 128), F32),
            jax.ShapeDtypeStruct(start.shape, F32),
            jax.ShapeDtypeStruct(rim.shape, F32),
        ],
        compiler_params=pltpu.CompilerParams(vmem_limit_bytes=VMEM_BYTES),
        cost_estimate=pl.CostEstimate(
            flops=tokens * heads * 26_000_000, bytes_accessed=tokens * heads * 10_000, transcendentals=0
        ),
        name="mixer_backward",
    )(info, mixed, mixed, raw, taps, small, level, solve, fresh, state, start, rim, *(grad,) * len(s["moved_head"]))


def unpack_kernel(heads, head_count, info_ref, *refs):
    blocks, refs = refs[:4], refs[4:]
    query_weight, key_weight, value_weight, gate_weight, beta_across, decay_across, gain = refs[:7]
    grad_query, grad_key, grad_value, grad_gate, grad_out, grad_beta, grad_decay, grad_gain = refs[7:]
    wide, full = heads * 128, head_count * 128
    small = 0.0
    for bits, block in enumerate(blocks):
        source = info_ref[1] ^ bits
        slot = 0
        for ref, pieces in ((grad_query, 1), (grad_key, 2), (grad_value, 2), (grad_gate, 1)):
            for piece in range(pieces):
                cols = pl.ds(pl.multiple_of(piece * full + source * wide, 128), wide)
                ref[:, cols] = block[0, :, slot * wide : (slot + 1) * wide].astype(F32)
                slot += 1
        cols = pl.ds(pl.multiple_of(source * wide, 128), wide)
        grad_out[:, cols] = block[0, :, 6 * wide + 128 :].astype(F32)
        row, col = place((128, 128), 1), place((128, 128), 0)
        chosen = (row < 3 * heads) & (col == row // heads * head_count + source * heads + row % heads)
        small = small + mm_low(chosen.astype(F32), block[0, :, 6 * wide : 6 * wide + 128], "nt")
    grad_beta[...] = small[: 2 * head_count]
    grad_decay[...] = small[2 * head_count : 3 * head_count]
    total = 0.0
    for weight, grad in (
        (query_weight, grad_query), (key_weight, grad_key), (value_weight, grad_value), (gate_weight, grad_gate),
    ):
        product = weight[...].astype(F32) * grad[...]
        total = total + mm_high(jnp.ones((8, product.shape[1]), F32), product, "nt")[0:1]
    for weight, grad in ((beta_across, grad_beta), (decay_across, grad_decay)):
        total = total + jnp.sum(weight[...].astype(F32) * grad[...], axis=0, keepdims=True)
    grad_gain[...] = total / gain[...]


def unpack_grads(heads, head_count, info, blocks, weights, gain):
    query, key, value, beta, decay, gate = weights
    share = query.shape[0]
    like = lambda rows, cols: jax.ShapeDtypeStruct((rows, cols), F32)
    vmem = pl.BlockSpec(memory_space=pltpu.VMEM)
    outs = [like(share, weight.shape[1]) for weight in (query, key, value, gate)]
    outs += [like(share, head_count * 128), like(2 * head_count, share), like(head_count, share), like(1, share)]
    ins = [*blocks, query, key, value, gate, beta.T, decay.T, gain.astype(F32)[None, :]]
    query, key, value, gate, out, beta, decay, gain = pl.pallas_call(
        functools.partial(unpack_kernel, heads, head_count),
        in_specs=[pl.BlockSpec(memory_space=pltpu.SMEM)] + [vmem] * len(ins),
        out_specs=[vmem] * len(outs),
        out_shape=outs,
        name="unpack_grads",
    )(info, *ins)
    return query, key, value, beta.T, decay.T, gate, out, gain[0]


def pack_kernel(heads, head_count, info_ref, query, key, value, gate, beta_across, decay_across, gains, *outs):
    wide, full = heads * 128, head_count * 128
    small = [ref[...].astype(F32) for ref in (beta_across, decay_across, gains)]
    small = jnp.concatenate(small, axis=0)
    for bits, out in enumerate(outs):
        target = info_ref[1] ^ bits
        slot = 0
        for ref, pieces in ((query, 1), (key, 2), (value, 2), (gate, 1)):
            for piece in range(pieces):
                cols = pl.ds(pl.multiple_of(piece * full + target * wide, 128), wide)
                out[0, :, slot * wide : (slot + 1) * wide] = ref[:, cols]
                slot += 1
        row, col = place((small.shape[0], 128), 0), place((small.shape[0], 128), 1)
        head = col // heads * head_count + target * heads + col % heads
        gain = 3 * head_count + col - 3 * heads
        chosen = row == jnp.where(col < 3 * heads, head, jnp.where(col < 3 * heads + 2, gain, -1))
        out[0, :, 6 * wide :] = mm_low(small, chosen.astype(F32), "tn").astype(LOW)


def pack_weights(heads, head_count, info, weights, gains):
    query, key, value, beta, decay, gate = weights
    share = query.shape[0]
    vmem = pl.BlockSpec(memory_space=pltpu.VMEM)
    gains = jnp.concatenate([gain.astype(F32)[None, :] for gain in gains] + [jnp.zeros((6, share), F32)], axis=0)
    out = jax.ShapeDtypeStruct((1, share, 6 * heads * 128 + 128), LOW)
    return pl.pallas_call(
        functools.partial(pack_kernel, heads, head_count),
        in_specs=[pl.BlockSpec(memory_space=pltpu.SMEM)] + [vmem] * 7,
        out_specs=[vmem] * 4,
        out_shape=[out] * 4,
        name="pack_weights",
    )(info, query, key, value, gate, beta.T, decay.T, gains)


def features(weight_ref, index, first=0, last=None):
    piece = weight_ref[:, index, :, first:last]
    return piece.reshape(piece.shape[0] * piece.shape[1], piece.shape[2])


def hold(weight_ref, held_ref):
    size = weight_ref.shape[0] * weight_ref.shape[2]

    @pl.when(pl.program_id(0) == 0)
    def _():
        for index in range(weight_ref.shape[1]):
            held_ref[index * size : (index + 1) * size, :] = features(weight_ref, index)


def mixer_in_kernel(heads, tokens_ref, weight_ref, normed_ref, mixed_ref, gains_ref, held_ref):
    hold(weight_ref, held_ref)
    tail = 6 * heads * 128
    tokens = tokens_ref[...].astype(F32)
    scale = lax.rsqrt(jnp.mean(tokens * tokens, axis=1, keepdims=True) + EPS_NORM)
    chosen = (place((8, 128), 1) == place((8, 128), 0) + 3 * heads).astype(F32)
    gains = mm_low(chosen, held_ref[:, tail:], "nt")
    gains_ref[...] = gains
    normed = (tokens * scale * gains[0:1]).astype(LOW)
    normed_ref[...] = normed
    mixed_ref[...] = jnp.dot(normed, held_ref[...], preferred_element_type=F32)


def mixer_in(heads, tokens, weight):
    length, width = tokens.shape
    count = min(256, length)
    wide = weight.shape[3]
    rows = lambda cols: pl.BlockSpec((count, cols), lambda i: (i, 0))
    return pl.pallas_call(
        functools.partial(mixer_in_kernel, heads),
        grid=(length // count,),
        in_specs=[rows(width), pl.BlockSpec(weight.shape, lambda i: (0, 0, 0, 0))],
        out_specs=[rows(width), rows(wide), pl.BlockSpec((8, width), lambda i: (0, 0))],
        out_shape=[
            jax.ShapeDtypeStruct((length, width), LOW),
            jax.ShapeDtypeStruct((length, wide), F32),
            jax.ShapeDtypeStruct((8, width), F32),
        ],
        scratch_shapes=[pltpu.VMEM((width, wide), LOW)],
        compiler_params=pltpu.CompilerParams(vmem_limit_bytes=VMEM_BYTES),
        cost_estimate=pl.CostEstimate(
            flops=2 * length * width * wide, bytes_accessed=length * wide * 4, transcendentals=0
        ),
        name="mixer_in",
    )(tokens, weight)


def feed_forward_kernel(hidden, blocks, *refs):
    gated_refs, refs = refs[:blocks], refs[blocks:]
    tokens_ref, grad_ref, weight_ref, gains_ref, second_ref, normed_ref, hidden_ref, acts_ref, partial_ref = refs[:9]
    *kept, held = refs[9:]
    hold(weight_ref, held)
    gated = jnp.concatenate([ref[...] for ref in gated_refs], axis=1)
    first = gated.shape[1]
    last = first + 2 * hidden
    if kept:

        @pl.when(pl.program_id(0) == 0)
        def _():
            kept[0][...] = held[:, : kept[0].shape[1]]
            kept[1][...] = held[:, last:]

    second = tokens_ref[...].astype(F32) + mm_low(gated, held[:, :first], "nt")
    second_ref[...] = second
    scale = lax.rsqrt(jnp.mean(second * second, axis=1, keepdims=True) + EPS_NORM)
    normed = (second * scale * gains_ref[1:2, :]).astype(LOW)
    normed_ref[...] = normed
    grad_hidden = mm_low(grad_ref[...], held[:, last:], "nn")
    acts = mm_low(normed, held[:, first:last], "nn")
    gate, up = acts[:, :hidden], acts[:, hidden:]
    sig = jax.nn.sigmoid(gate)
    silu_gate = gate * sig
    hidden_ref[...] = (silu_gate * up).astype(LOW)
    grads = [grad_hidden * up * sig * (1.0 + gate * (1.0 - sig)), grad_hidden * silu_gate]
    grads = jnp.concatenate(grads, axis=1).astype(LOW)
    acts_ref[...] = grads
    partial_ref[...] = mm_low(grads, held[:, first:last], "nt")


def feed_forward_part(hidden, first, tokens, grads, gated, weight, gains):
    length, width = gated[0].shape[0], tokens.shape[1]
    count = min(256, length)
    skip = first // count
    whole_rows = pl.BlockSpec((count, width), lambda i: (i + skip, 0))
    rows = lambda cols: pl.BlockSpec((count, cols), lambda i: (i, 0))
    out = lambda cols, kind: jax.ShapeDtypeStruct((length, cols), kind)
    kept = [gated[0].shape[1], hidden] if first == 0 else []
    return pl.pallas_call(
        functools.partial(feed_forward_kernel, hidden, len(gated)),
        grid=(length // count,),
        in_specs=[rows(block.shape[1]) for block in gated]
        + [whole_rows, whole_rows, pl.BlockSpec(weight.shape, lambda i: (0, 0, 0, 0))]
        + [pl.BlockSpec((8, width), lambda i: (0, 0))],
        out_specs=[rows(width), rows(width), rows(hidden), rows(2 * hidden), rows(width)]
        + [pl.BlockSpec((width, cols), lambda i: (0, 0)) for cols in kept],
        out_shape=[out(width, F32), out(width, LOW), out(hidden, LOW), out(2 * hidden, LOW), out(width, F32)]
        + [jax.ShapeDtypeStruct((width, cols), LOW) for cols in kept],
        scratch_shapes=[pltpu.VMEM((width, weight.shape[3]), LOW)],
        compiler_params=pltpu.CompilerParams(vmem_limit_bytes=VMEM_BYTES),
        cost_estimate=pl.CostEstimate(flops=8 * 10**9, bytes_accessed=10**7, transcendentals=0),
        name="feed_forward",
    )(*gated, tokens, grads, weight, gains)


def weight_grads_kernel(counts, *refs):
    *refs, out_ref = refs
    first = 0
    places, share = out_ref.shape[0], out_ref.shape[2]
    for lefts, rights in counts:
        left_refs, right_refs, refs = refs[:lefts], refs[lefts : lefts + rights], refs[lefts + rights :]
        total, at = 0.0, 0
        for right in right_refs:
            tokens = right.shape[0]
            if lefts == rights:
                left = left_refs[at // tokens][...]
            else:
                left = left_refs[0][at : at + tokens, :]
            total = total + mm_low(left, right[...], "tn")
            at += tokens
        width = total.shape[1]
        out_ref[:, 0, :, first : first + width] = total.astype(LOW).reshape(places, share, width)
        first += width


def weight_grads(places, count, pairs):
    features_all = pairs[0][0][0].shape[1]
    size = features_all // count
    share = size // places
    width = sum(rights[0].shape[1] for _, rights in pairs)
    specs, arrays, flops = [], [], 0
    for lefts, rights in pairs:
        specs += [pl.BlockSpec((left.shape[0], size), lambda i: (0, i)) for left in lefts]
        specs += [pl.BlockSpec(right.shape, lambda i: (0, 0)) for right in rights]
        arrays += [*lefts, *rights]
        flops += sum(2 * right.shape[0] * right.shape[1] * features_all for right in rights)
    out = pl.pallas_call(
        functools.partial(weight_grads_kernel, tuple((len(lefts), len(rights)) for lefts, rights in pairs)),
        grid=(count,),
        in_specs=specs,
        out_specs=pl.BlockSpec((places, 1, share, width), lambda i: (0, i, 0, 0)),
        out_shape=jax.ShapeDtypeStruct((places, count, share, width), LOW),
        compiler_params=pltpu.CompilerParams(vmem_limit_bytes=VMEM_BYTES),
        cost_estimate=pl.CostEstimate(flops=flops, bytes_accessed=10**7, transcendentals=0),
        name="weight_grads",
    )(*arrays)
    return out.reshape(-1, width)


def swap(array, axis, bits):
    return lax.ppermute(array, axis, [(i, i ^ bits) for i in range(lax.axis_size(axis))])


def on_square():
    return lax.axis_size("seq") == 4


def power_of_two(axis):
    return lax.axis_size(axis) & (lax.axis_size(axis) - 1) == 0


def after(array, *others):
    return lax.optimization_barrier((array,) + others)[0]


def spread_out(array):
    if not on_square():
        whole = lax.all_gather(array, "seq")
        return [whole[i] for i in range(whole.shape[0])]
    far, beside, below = (swap(array, "seq", bits) for bits in (3, 1, 2))
    return [array, beside, below, far]


def in_place_order(blocks):
    if not on_square():
        return jnp.concatenate(blocks, axis=0)
    me = lax.axis_index("seq")
    size = blocks[0].shape[0]
    out = jnp.zeros((len(blocks) * size,) + blocks[0].shape[1:], blocks[0].dtype)
    for bits, block in enumerate(blocks):
        out = lax.dynamic_update_slice(out, block, ((me ^ bits) * size, 0))
    return out


def row_block(array, index):
    size = array.shape[0] // lax.axis_size("seq")
    return lax.dynamic_slice_in_dim(array, index * size, size, 0)


def to_send(array):
    if not on_square():
        return [array.astype(LOW)]
    me = lax.axis_index("seq")
    return [row_block(array, me ^ bits).astype(LOW) for bits in (3, 1, 2)]


def send(blocks):
    if not on_square():
        return [lax.psum_scatter(blocks[0], "seq", scatter_dimension=0, tiled=True)]
    return [swap(block, "seq", bits) for bits, block in zip((3, 1, 2), blocks)]


def total(array, got):
    if not on_square():
        return got[0].astype(F32)
    return row_block(array, lax.axis_index("seq")) + sum(block.astype(F32) for block in got)


def exchange_unordered(blocks):
    me = lax.axis_index("seq")
    sends = tuple(lax.dynamic_index_in_dim(blocks, me ^ bits, 0, True) for bits in (0, 1, 2, 3))
    sends = lax.optimization_barrier(sends)
    got = tuple(swap(sends[bits], "seq", bits) for bits in (3, 1, 2))
    far, beside, below = lax.optimization_barrier(got)
    return [sends[0], beside, below, far]


def exchange(blocks):
    if not on_square():
        return lax.all_to_all(blocks, "seq", 0, 0, tiled=True)
    me = lax.axis_index("seq")
    others = (3, 1, 2)
    sends = lax.optimization_barrier(tuple(lax.dynamic_index_in_dim(blocks, me ^ bits, 0, True) for bits in others))
    got = lax.optimization_barrier(tuple(swap(block, "seq", bits) for bits, block in zip(others, sends)))
    out = blocks
    for bits, block in zip(others, got):
        out = lax.dynamic_update_slice(out, block, (me ^ bits, 0, 0))
    return out


def sum_over(array, axis):
    if not power_of_two(axis):
        return lax.psum(array, axis)
    bits = 1
    while bits < lax.axis_size(axis):
        array = array + swap(array, axis, bits)
        bits *= 2
    return array


def gather_rows(mine):
    return lax.all_gather(mine, "rows", axis=0)


def in_rows(whole):
    rows, count, size, width = whole.shape
    return whole.transpose(1, 0, 2, 3).reshape(count * rows * size, width)


def by_rows(grad):
    count, rows = lax.axis_size("seq"), lax.axis_size("rows")
    size = grad.shape[0] // (count * rows)
    grad = grad.astype(LOW).reshape(count, rows, size, grad.shape[1])
    return grad.transpose(1, 0, 2, 3).reshape(-1, grad.shape[3])


def sum_rows(grad):
    count = lax.axis_size("seq")
    summed = lax.psum_scatter(grad, "rows", scatter_dimension=0, tiled=True)
    return summed.reshape(count, -1, grad.shape[1])


def project(left, right):
    return jnp.dot(left, right, preferred_element_type=F32)


def outer_sum(left, right):
    return lax.dot_general(left, right, FORMS["tn"], preferred_element_type=F32)


def back_project(left, right):
    return lax.dot_general(left, right, FORMS["nt"], preferred_element_type=F32)


def norm_scale(features):
    return lax.rsqrt(jnp.mean(features * features, axis=-1, keepdims=True) + EPS_NORM)


def norm_back(features, scale, grad):
    return scale * grad - features * scale**3 * jnp.mean(grad * features, axis=-1, keepdims=True)


def on_device(
    block_input, valid_length, query_weight, key_weight, value_weight, beta_weight, decay_weight, gate_weight,
    out_weight, ffn_gate_weight, ffn_up_weight, ffn_down_weight, norm_gain, ffn_norm_gain, head_norm_gain,
    decay_log, decay_bias, conv_weight, output_grad,
):
    count = lax.axis_size("seq")
    me = lax.axis_index("seq")
    rows_here, tokens_here, model_width = block_input.shape
    share = query_weight.shape[0]
    head_count = decay_log.shape[0]
    heads = max(1, head_count // count)
    blocks = head_count // heads
    copies = count // blocks
    block = me // copies
    wide = heads * 128
    hidden = ffn_gate_weight.shape[1] // count
    square = on_square() and copies == 1

    def cut(weight, pieces, at):
        width = weight.shape[1] // (pieces * blocks)
        at = at // copies
        return [
            weight[:, (p * blocks + at) * width : (p * blocks + at + 1) * width] for p in range(pieces)
        ]

    def cut_hidden(weight, at):
        return [weight[:, at * hidden : (at + 1) * hidden]]

    gains = jnp.stack([norm_gain, ffn_norm_gain], axis=1)

    def tail_of(at):
        parts = cut(beta_weight, 2, at) + cut(decay_weight, 1, at) + [gains]
        return parts + [jnp.zeros((share, 128 - 3 * heads - 2), LOW)]

    def first_of(at):
        parts = cut(query_weight, 1, at) + cut(key_weight, 2, at) + cut(value_weight, 2, at)
        return jnp.concatenate(parts + cut(gate_weight, 1, at) + tail_of(at), axis=1)

    def rest_of(at):
        order = [at ^ bits for bits in range(count)] if on_square() else range(0, count, copies)
        parts = sum((cut(out_weight, 1, other) for other in order), [])
        parts += cut_hidden(ffn_gate_weight, at) + cut_hidden(ffn_up_weight, at) + cut_hidden(ffn_down_weight, at)
        return jnp.concatenate(parts, axis=1)

    def pack(part):
        return jnp.stack([part(at) for at in range(count)])

    info = jnp.stack([valid_length[0], me if on_square() else jnp.int32(0)])
    mixer_weights = (query_weight, key_weight, value_weight, beta_weight, decay_weight, gate_weight)
    if on_square():
        packed = pack_weights(heads, head_count, info, mixer_weights, (norm_gain, ffn_norm_gain))
        got = tuple(swap(packed[bits], "seq", bits) for bits in (3, 1, 2))
        far, beside, below = lax.optimization_barrier(got)
        first_share = jnp.zeros((count,) + packed[0].shape[1:], LOW)
        for bits, block_got in enumerate((packed[0], beside, below, far)):
            first_share = lax.dynamic_update_slice(first_share, block_got, (me ^ bits, 0, 0))
    else:
        first_share = exchange(pack(first_of))
    mixed_parts = gather_rows(first_share)
    mixed_weight = in_rows(mixed_parts)
    own = after(block_input.reshape(tokens_here, model_width), first_share)
    everyone = in_place_order(spread_out(own))
    rest_pack, everyone = lax.optimization_barrier((pack(rest_of), everyone))
    rest_share = exchange(rest_pack)
    rest_parts = gather_rows(rest_share)

    if not square:
        rest_weight = in_rows(rest_parts)
        out_all = rest_weight[:, : blocks * wide]
        ffn_in = rest_weight[:, blocks * wide : blocks * wide + 2 * hidden]
        ffn_down = rest_weight[:, blocks * wide + 2 * hidden :]
        out_own = out_all[:, :wide] if on_square() else lax.dynamic_slice_in_dim(out_all, block * wide, wide, 1)
    gain_first = mixed_weight[:, 6 * wide + 3 * heads].astype(F32)
    gain_second = mixed_weight[:, 6 * wide + 3 * heads + 1].astype(F32)

    def block_lanes(vector, first):
        mine = lax.dynamic_slice_in_dim(vector, block * heads, heads)
        return jnp.pad(mine, (first, 128 - first - heads))

    small = jnp.stack([block_lanes(-jnp.exp(decay_log), 2 * heads), block_lanes(decay_bias, 2 * heads), head_norm_gain])
    small = jnp.pad(small, ((0, 5), (0, 0)))
    taps = [
        lax.dynamic_slice_in_dim(conv_weight, (slot * blocks + block) * wide, wide, 1) for slot in range(5)
    ]
    taps = jnp.pad(jnp.concatenate(taps, axis=1), ((0, 8 - conv_weight.shape[0]), (0, 0)))
    level = level_table()

    length = count * tokens_here
    part = length // 2
    tie = lax.optimization_barrier

    if square:
        normed, mixed, gains = mixer_in(heads, everyone, mixed_parts)
    else:
        tokens_all = everyone.astype(F32)
        normed = (tokens_all * norm_scale(tokens_all) * gain_first).astype(LOW)
        mixed = project(normed, mixed_weight)
    mixed, own_grad = tie((mixed, output_grad.reshape(tokens_here, model_width)))
    grads_got = spread_out(own_grad)
    zero_state = jnp.zeros((heads, 128, 128), F32)
    gated_a, *kept_a, end = mixer_forward(heads, 0, part, info, mixed, taps, small, level, zero_state)
    end, grads_got, everyone_late = tie((end, grads_got, everyone))
    gated_got_a = spread_out(gated_a)
    gated_b, *kept_b, end = mixer_forward(heads, part, part, info, mixed, taps, small, level, end)
    gated_b, gated_got_a = tie((gated_b, gated_got_a))
    gated_got_b = spread_out(gated_b)
    grad_branch = in_place_order(grads_got)

    def feed_forward(index, gated_got, got=None):
        if square:
            outs = feed_forward_part(hidden, index * part, everyone_late, grad_branch, gated_got, rest_parts, gains)
            return (*tie(tuple(outs[:5]) + (got,)), outs[5:])
        rows = slice(index * part, (index + 1) * part)
        gated_all = jnp.concatenate(gated_got[:: 1 if on_square() else copies], axis=1)
        second = everyone_late[rows].astype(F32) + back_project(gated_all, out_all)
        normed_two = (second * norm_scale(second) * gain_second).astype(LOW)
        if got is not None:
            normed_two, got = tie((normed_two, got))
        acts = project(normed_two, ffn_in)
        gate_act, up_act = acts[:, :hidden], acts[:, hidden:]
        sig = jax.nn.sigmoid(gate_act)
        hidden_low = (gate_act * sig * up_act).astype(LOW)
        grad_hidden = project(grad_branch[rows], ffn_down)
        grad_acts = [grad_hidden * up_act * sig * (1.0 + gate_act * (1.0 - sig)), grad_hidden * gate_act * sig]
        grad_acts = jnp.concatenate(grad_acts, axis=1).astype(LOW)
        return second, normed_two, hidden_low, grad_acts, back_project(grad_acts, ffn_in), got, None

    def second_back(index, second, partial, got):
        grad = total(partial, got) * gain_second
        second = row_block(second, me)
        out_grad = row_block(grad_branch[index * part : (index + 1) * part], me)
        return (out_grad.astype(F32) + norm_back(second, norm_scale(second), grad)).astype(LOW)

    second_a, normed_two_a, hidden_a, grad_acts_a, partial_a, _, kept = feed_forward(0, gated_got_a)
    if square:
        out_own, ffn_down = kept
    sends_a, gated_got_b = tie((to_send(partial_a), gated_got_b))
    got_a = send(sends_a)
    second_b, normed_two_b, hidden_b, grad_acts_b, partial_b, got_a, _ = feed_forward(1, gated_got_b, got_a)
    sends_b, hidden_b, grad_acts_b = tie((to_send(partial_b), hidden_b, grad_acts_b))
    got_b = send(sends_b)

    join_parts = lambda a, b: jnp.concatenate([a, b], axis=0)
    hidden_low = join_parts(hidden_a, hidden_b)
    down = back_project(hidden_low, ffn_down)
    down_sends = to_send(down)
    grad_second_a = second_back(0, second_a, partial_a, got_a)
    got_b, down_sends, grad_second_a = tie((got_b, down_sends, grad_second_a))
    grad_second_b, grad_acts_b = tie((second_back(1, second_b, partial_b, got_b), grad_acts_b))
    grads_two_b = spread_out(grad_second_b)
    if square:
        pairs = [((normed_two_a, normed_two_b), (grad_acts_a, grad_acts_b)), ((grad_branch,), (hidden_a, hidden_b))]
        early = weight_grads(lax.axis_size("rows"), count, pairs)
    else:
        early_in = outer_sum(join_parts(normed_two_a, normed_two_b), join_parts(grad_acts_a, grad_acts_b))
        early = by_rows(jnp.concatenate([early_in, outer_sum(grad_branch, hidden_low)], axis=1))
    grads_two_b, early, down_sends, grad_second_a = tie((grads_two_b, early, down_sends, grad_second_a))
    early = sum_rows(early)
    grads_two_a = spread_out(grad_second_a)

    grad_gated = project(jnp.concatenate(grads_two_b, axis=0), out_own)
    rim = jnp.zeros((8, 5 * wide), F32)
    grad_pre_b, taps_b, small_b, end, rim = mixer_backward(
        heads, part, part, part // count, info, mixed, kept_b[0], grad_gated, taps, small, level, *kept_b[1:],
        zero_state, rim,
    )
    end, grads_two_a, down_sends = tie((end, grads_two_a, down_sends))
    down_got = send(down_sends)
    grad_gated = project(jnp.concatenate(grads_two_a, axis=0), out_own)
    grad_second = join_parts(in_place_order(grads_two_a), in_place_order(grads_two_b))

    def once(array):
        return array if copies == 1 else array * (me % copies == 0).astype(array.dtype)

    grad_pre_a, taps_a, small_a, end, rim = mixer_backward(
        heads, 0, part, part // count, info, mixed, kept_a[0], grad_gated, taps, small, level, *kept_a[1:], end, rim
    )
    grad_pre_a, taps_a, small_a, down_got = tie((grad_pre_a, taps_a, small_a, down_got))
    grad_pre_a, grad_pre_b = once(grad_pre_a), once(grad_pre_b)
    grad_normed = back_project(join_parts(grad_pre_a, grad_pre_b), mixed_weight)
    grad_normed_sends, grad_pre_a, grad_pre_b = tie((to_send(grad_normed), grad_pre_a, grad_pre_b))
    grad_normed_got = send(grad_normed_sends)
    if square:
        pairs = [((normed,), (grad_pre_a, grad_pre_b)), ((grad_second,), (gated_a, gated_b))]
        late = weight_grads(lax.axis_size("rows"), count, pairs)
    else:
        out_grad = once(outer_sum(grad_second, join_parts(gated_a, gated_b)).astype(LOW))
        late = outer_sum(normed, join_parts(grad_pre_a, grad_pre_b)).astype(LOW)
        late = by_rows(jnp.concatenate([late, out_grad], axis=1))
    grad_taps, grad_small = taps_a + taps_b, small_a + small_b
    late, early, grad_taps, grad_small, down_got = tie((late, early, grad_taps, grad_small, down_got))
    late = sum_rows(late)
    early = exchange(early)

    def at_block(vector, first, width):
        mine = once(vector[first : first + width])
        return lax.dynamic_update_slice(jnp.zeros((blocks * width,), F32), mine, (block * width,))

    flat = [once(grad_small[2]), at_block(grad_small[0], 2 * heads, heads), at_block(grad_small[1], 2 * heads, heads)]
    flat = jnp.concatenate(flat)
    taps_wide = 5 * wide
    flat = jnp.pad(flat, (0, -flat.shape[0] % taps_wide)).reshape(-1, taps_wide)
    pooled = sum_over(jnp.concatenate([once(grad_taps[:4]), flat], axis=0), "rows")
    pooled, grad_normed_got = tie((pooled, grad_normed_got))
    by_place = lax.dynamic_update_slice(jnp.zeros((blocks, 4, taps_wide), F32), pooled[None, :4], (block, 0, 0))
    pooled = sum_over(jnp.concatenate([by_place.reshape(-1, taps_wide), pooled[4:]], axis=0), "seq")
    ends = [128, 128 + head_count, 128 + 2 * head_count]

    second = row_block(join_parts(second_a, second_b), me)
    result = (second + total(down, down_got)).astype(LOW).reshape(block_input.shape)
    def join(grads, first, pieces, width, every=copies):
        return jnp.concatenate(
            [
                grads[b, :, first + p * width : first + (p + 1) * width]
                for p in range(pieces)
                for b in range(0, count, every)
            ],
            axis=1,
        ).astype(F32)

    def gain_grad(gain, *pairs):
        summed = sum(jnp.sum(weight.astype(F32) * grad, axis=1) for weight, grad in pairs)
        return summed / gain.astype(F32)

    grad_ffn_gate = join(early, 0, 1, hidden, 1)
    grad_ffn_up = join(early, hidden, 1, hidden, 1)
    grad_ffn_down = join(early, 2 * hidden, 1, hidden, 1)
    grad_gain_second = gain_grad(ffn_norm_gain, (ffn_gate_weight, grad_ffn_gate), (ffn_up_weight, grad_ffn_up))
    flat = pooled[4 * blocks :].reshape(-1)
    grad_conv = pooled[: 4 * blocks].reshape(blocks, 4, taps_wide)
    grad_conv = jnp.concatenate(
        [grad_conv[b, :, slot * wide : (slot + 1) * wide] for slot in range(5) for b in range(blocks)], axis=1
    )
    late, result, grad_ffn_gate, grad_ffn_up, grad_ffn_down, grad_gain_second, grad_normed_got = tie(
        (late, result, grad_ffn_gate, grad_ffn_up, grad_ffn_down, grad_gain_second, grad_normed_got)
    )
    tokens = own.astype(F32)
    grad_tokens = norm_back(tokens, norm_scale(tokens), total(grad_normed, grad_normed_got) * gain_first)
    grad_input = row_block(grad_second, me).astype(F32) + grad_tokens
    grad_input = grad_input.reshape(block_input.shape)

    if on_square():
        late = exchange_unordered(late)
        *mixer_grads, grad_out, grad_gain_first = unpack_grads(heads, head_count, info, late, mixer_weights, norm_gain)
        grad_query, grad_key, grad_value, grad_beta, grad_decay, grad_gate = mixer_grads
    else:
        late = exchange(late)
        grad_query = join(late, 0, 1, wide)
        grad_key = join(late, wide, 2, wide)
        grad_value = join(late, 3 * wide, 2, wide)
        grad_beta = join(late, 6 * wide, 2, heads)
        grad_decay = join(late, 6 * wide + 2 * heads, 1, heads)
        grad_gate = join(late, 5 * wide, 1, wide)
        grad_out = join(late, 6 * wide + 128, 1, wide)
        mixer_grads = (grad_query, grad_key, grad_value, grad_beta, grad_decay, grad_gate)
        grad_gain_first = gain_grad(norm_gain, *zip(mixer_weights, mixer_grads))
    return (
        result,
        grad_input,
        grad_query,
        grad_key,
        grad_value,
        grad_beta,
        grad_decay,
        grad_gate,
        grad_out,
        grad_ffn_gate,
        grad_ffn_up,
        grad_ffn_down,
        grad_gain_first,
        grad_gain_second,
        flat[: ends[0]],
        flat[ends[0] : ends[1]],
        flat[ends[1] : ends[2]],
        grad_conv,
    )


def solution(mesh):
    tokens, weight, vector, whole = P("rows", "seq", None), P(BOTH, None), P(BOTH), P()
    return jax.shard_map(
        on_device,
        mesh=mesh,
        in_specs=(tokens, P("rows")) + (weight,) * 10 + (vector,) * 2 + (whole,) * 4 + (tokens,),
        out_specs=(tokens, tokens) + (weight,) * 10 + (vector,) * 2 + (whole,) * 4,
        check_vma=False,
    )
```

```python
import functools

import jax
import jax.numpy as jnp
from jax import lax
from jax.experimental import pallas as pl
from jax.experimental.pallas import tpu as pltpu
from jax.sharding import PartitionSpec as P

GROUP = 64
EPS_NORM = 1e-06
EPS_KEY = 1e-06
EPS_HEAD = 1e-05
LOW = jnp.bfloat16
F32 = jnp.float32
HIGHEST = lax.Precision.HIGHEST
BOTH = ("seq", "rows")

FORMS = {
    "nn": (((1,), (0,)), ((), ())),
    "nt": (((1,), (1,)), ((), ())),
    "tn": (((0,), (0,)), ((), ())),
}


def split_low(a):
    high = a.astype(LOW)
    return high, (a - high.astype(F32)).astype(LOW)


def mm(a, b, form):
    a_axis = 0 if form == "tn" else 1
    b_axis = 1 if form == "nt" else 0
    a_two = jnp.concatenate(split_low(a), axis=a_axis)
    b_high, b_low = split_low(b)
    b_two = jnp.concatenate([b_high, b_low], axis=1 - b_axis)
    b_two = jnp.concatenate([b_two, b_two], axis=b_axis)
    out = lax.dot_general(a_two, b_two, FORMS[form], preferred_element_type=F32)
    half = out.shape[1] // 2
    return out[:, :half] + out[:, half:]


def mm_low(a, b, form):
    return lax.dot_general(a.astype(LOW), b.astype(LOW), FORMS[form], preferred_element_type=F32)


def mm_high(a, b, form):
    return lax.dot_general(a, b, FORMS[form], precision=HIGHEST, preferred_element_type=F32)


def row_dot(a, b):
    return jnp.sum(a * b, axis=1, keepdims=True)


def place(shape, axis):
    return lax.broadcasted_iota(jnp.int32, shape, axis)


def level_table():
    time = 2 * (jnp.arange(2 * GROUP) % GROUP) + jnp.arange(2 * GROUP) // GROUP
    row, col = time[:, None], time[None, :]
    differ = row ^ col
    level = sum((differ >= 2**m).astype(jnp.int32) for m in range(1, 7))
    return jnp.where(row > col, level, -1)


def inverses(systems, level):
    size = level.shape[0]
    eye = (place((size, size), 0) == place((size, size), 1)).astype(F32)
    found = [eye - jnp.where(level == 0, a, 0.0) for a in systems]
    for m in range(1, 7):
        inner = [mm(jnp.where(level == m, a, 0.0), t, "nn") for a, t in zip(systems, found)]
        found = [t - mm(t, s, "nn") for t, s in zip(found, inner)]
    return found


def conv_active(pad_ref, taps_ref, first, count):
    cols = slice(first, first + 128)
    summed = 0.0
    for back in range(4):
        summed = summed + pad_ref[pl.ds(8 - back, count), cols] * taps_ref[3 - back : 4 - back, cols]
    return summed


def silu(x):
    return x * jax.nn.sigmoid(x)


def softplus(x):
    return jnp.maximum(x, 0.0) + jnp.log1p(jnp.exp(-jnp.abs(x)))


def cum_decays(log_decay):
    tril = (place((GROUP, GROUP), 0) >= place((GROUP, GROUP), 1)).astype(F32)
    across = (place((GROUP, 2 * GROUP), 0) <= place((GROUP, 2 * GROUP), 1) % GROUP).astype(F32)
    return mm_high(tril, log_decay, "nn"), mm_high(log_decay, across, "tn")


def twice(a):
    return jnp.concatenate([a, a], axis=0)


def group_setup(level, beta, cum, across, head, heads):
    lane = 2 * heads + head
    c = cum[:, lane : lane + 1]
    row = across[lane : lane + 1, :]
    c_two = twice(c)
    end = c[GROUP - 1 : GROUP, :]
    b = jnp.concatenate([beta[:, head : head + 1], beta[:, heads + head : heads + head + 1]], axis=0)
    strict = level >= 0
    pair = jnp.where(strict, jnp.exp(jnp.where(strict, c_two - row, 0.0)), 0.0)
    seen = place((GROUP, 2 * GROUP), 1) % GROUP <= place((GROUP, 2 * GROUP), 0)
    view = jnp.where(seen, jnp.exp(jnp.where(seen, c - row, 0.0)), 0.0)
    return c, c_two, end, b, pair, view


def forward_kernel(
    heads, first, info_ref, tokens_ref, weight_ref, taps_ref, small_ref, level_ref, start_ref, rim_ref,
    out_ref, raw_ref, solve_ref, fresh_ref, state_ref, end_ref, mixed_ref, normed_ref, gains_ref, last_rim_ref,
    carried, padded, held,
):
    step = pl.program_id(0)
    count = mixed_ref.shape[0]
    hold(weight_ref, held)
    tokens = tokens_ref[...].astype(F32)
    scale = lax.rsqrt(jnp.mean(tokens * tokens, axis=1, keepdims=True) + EPS_NORM)
    chosen = (place((8, 128), 1) == place((8, 128), 0) + 3 * heads).astype(F32)
    gains = mm_low(chosen, held[:, 6 * heads * 128 :], "nt")
    gains_ref[...] = gains
    normed = (tokens * scale * gains[0:1]).astype(LOW)
    normed_ref[...] = normed
    mixed_ref[...] = jnp.dot(normed, held[...], preferred_element_type=F32)
    block = step + first // count
    groups = count // GROUP
    wide = heads * 128

    @pl.when(step == 0)
    def _():
        carried[...] = start_ref[...]

    padded[0:8, :] = jnp.where(step > 0, padded[count : count + 8, :], rim_ref[...])
    padded[8 : 8 + count, :] = mixed_ref[:, : 5 * wide]
    last_rim_ref[...] = padded[count : count + 8, :]
    valid = (block * count + place((count, 1), 0) < info_ref[0]).astype(F32)
    level = level_ref[...]
    tail = mixed_ref[:, 6 * wide :]
    beta = jax.nn.sigmoid(tail) * valid
    log_decay = small_ref[0:1, :] * softplus(tail + small_ref[1:2, :]) * valid

    def active(slot, head):
        return silu(conv_active(padded, taps_ref, slot * wide + head * 128, count))

    def unit(x):
        return x * lax.rsqrt(row_dot(x, x) + EPS_KEY)

    queries = [unit(active(0, h)) * 128**-0.5 for h in range(heads)]
    keys = [[unit(active(1 + j, h)) for j in range(2)] for h in range(heads)]
    values = [[active(3 + j, h) for j in range(2)] for h in range(heads)]
    work = []
    for g in range(groups):
        rows = slice(g * GROUP, (g + 1) * GROUP)
        cum, across = cum_decays(log_decay[rows])
        for h in range(heads):
            key = jnp.concatenate([keys[h][0][rows], keys[h][1][rows]], axis=0)
            value = jnp.concatenate([values[h][0][rows], values[h][1][rows]], axis=0)
            c, c_two, end, b, pair, view = group_setup(level, beta[rows], cum, across, h, heads)
            gram = mm(key, key, "nt")
            work.append((g, h, rows, key, value, c, c_two, end, b, view, b * pair * gram))
    solves = inverses([w[-1] for w in work], level)
    raws = [[None] * groups for _ in range(heads)]
    ready = []
    for (g, h, rows, key, value, c, c_two, end, b, view, _), solve in zip(work, solves):
        solve_ref[g, h] = solve
        query = queries[h][rows]
        weights = view * mm(query, key, "nt")
        key_solve = mm(solve, b * jnp.exp(c_two) * key, "nn")
        pseudo = mm(solve, b * value, "nn")
        ready.append((query, weights, key_solve, pseudo))
    for (g, h, rows, key, value, c, c_two, end, b, view, _), made in zip(work, ready):
        query, weights, key_solve, pseudo = made
        state = carried[h]
        state_ref[g, h] = state
        fresh = pseudo - mm(key_solve, state, "nn")
        fresh_ref[g, h] = fresh
        carried[h] = jnp.exp(end) * state + mm(jnp.exp(end - c_two) * key, fresh, "tn")
        raws[h][g] = jnp.exp(c) * mm(query, state, "nn") + mm(weights, fresh, "nn")
    for h in range(heads):
        cols = slice(h * 128, (h + 1) * 128)
        raw = jnp.concatenate(raws[h], axis=0)
        raw_ref[:, cols] = raw
        scale = lax.rsqrt(jnp.mean(raw * raw, axis=1, keepdims=True) + EPS_HEAD)
        gated = raw * scale * small_ref[2:3, :] * silu(mixed_ref[:, 5 * wide + h * 128 : 5 * wide + (h + 1) * 128]) * valid
        out_ref[:, cols] = gated.astype(LOW)
    end_ref[...] = carried[...]


def backward_kernel(
    heads, first, pieces, info_ref, mixed_ref, halo_ref, raw_ref, taps_ref, small_ref, level_ref,
    solve_ref, fresh_ref, state_ref, start_ref, rim_ref, before_ref, *refs,
):
    grad_refs = refs[:pieces]
    grad_mixed_ref, grad_taps_ref, grad_small_ref, end_ref, last_rim_ref, carried, padded, spread = refs[pieces:]
    step = pl.program_id(0)
    count = mixed_ref.shape[0]
    local = pl.num_programs(0) - 1 - step
    block = local + first // count
    groups = count // GROUP
    wide = heads * 128

    @pl.when(step == 0)
    def _():
        carried[...] = start_ref[...]
        spread[0:8, :] = rim_ref[...]
        grad_taps_ref[...] = jnp.zeros_like(grad_taps_ref)
        grad_small_ref[...] = jnp.zeros_like(grad_small_ref)

    spread[count : count + 8, :] = spread[0:8, :]
    padded[0:8, :] = jnp.where(local > 0, halo_ref[:, : 5 * wide], before_ref[...])
    padded[8 : 8 + count, :] = mixed_ref[:, : 5 * wide]
    valid = (block * count + place((count, 1), 0) < info_ref[0]).astype(F32)
    level = level_ref[...]
    strict = level >= 0
    tail = mixed_ref[:, 6 * wide :]
    sigmoid_tail = jax.nn.sigmoid(tail)
    beta = sigmoid_tail * valid
    log_decay = small_ref[0:1, :] * softplus(tail + small_ref[1:2, :]) * valid
    lanes = place((1, 128), 1)

    grad_raws = []
    for h in range(heads):
        cols = slice(h * 128, (h + 1) * 128)
        gate_cols = slice(5 * wide + h * 128, 5 * wide + (h + 1) * 128)
        raw, gate = raw_ref[:, cols], mixed_ref[:, gate_cols]
        grad = jnp.concatenate([ref[:, cols] for ref in grad_refs], axis=0) * valid
        sig = jax.nn.sigmoid(gate)
        scale = lax.rsqrt(jnp.mean(raw * raw, axis=1, keepdims=True) + EPS_HEAD)
        shaped = raw * scale
        gain = small_ref[2:3, :]
        grad_mixed_ref[:, gate_cols] = (grad * shaped * gain * sig * (1.0 + gate * (1.0 - sig))).astype(LOW)
        grad_normed = grad * gate * sig
        grad_small_ref[2:3, :] += jnp.sum(grad_normed * shaped, axis=0, keepdims=True)
        grad_shaped = grad_normed * gain
        grad_raws.append(scale * (grad_shaped - shaped * jnp.mean(grad_shaped * shaped, axis=1, keepdims=True)))

    def summed(slot, head):
        return conv_active(padded, taps_ref, slot * wide + head * 128, count)

    def unit(x):
        return x * lax.rsqrt(row_dot(x, x) + EPS_KEY)

    queries = [unit(silu(summed(0, h))) * 128**-0.5 for h in range(heads)]
    keys = [[unit(silu(summed(1 + j, h))) for j in range(2)] for h in range(heads)]
    values = [[silu(summed(3 + j, h)) for j in range(2)] for h in range(heads)]
    work = []
    for g in reversed(range(groups)):
        rows = slice(g * GROUP, (g + 1) * GROUP)
        cum, across = cum_decays(log_decay[rows])
        for h in range(heads):
            key = jnp.concatenate([keys[h][0][rows], keys[h][1][rows]], axis=0)
            value = jnp.concatenate([values[h][0][rows], values[h][1][rows]], axis=0)
            c, c_two, end, b, pair, view = group_setup(level, beta[rows], cum, across, h, heads)
            query, grad_raw = queries[h][rows], grad_raws[h][rows]
            scores = view * mm(query, key, "nt")
            late = mm(scores, grad_raw, "tn")
            grad_scores = view * mm(grad_raw, fresh_ref[g, h], "nt")
            work.append((g, h, rows, key, value, c, c_two, end, b, pair, query, grad_raw, late, grad_scores))
    grad_parts = [[[None] * groups for _ in range(5)] for _ in range(heads)]
    grad_betas, grad_cums = [0.0] * groups, [0.0] * groups
    for (g, h, rows, key, value, c, c_two, end, b, pair, query, grad_raw, late, grad_scores) in work:
        state, fresh, solve = state_ref[g, h], fresh_ref[g, h], solve_ref[g, h]
        grad_state = carried[h]
        grow, fade, all_fade = jnp.exp(c_two), jnp.exp(end - c_two), jnp.exp(end)
        grad_seen = jnp.exp(c) * grad_raw
        grad_fresh = late + mm(fade * key, grad_state, "nn")
        adjoint = mm(solve, grad_fresh, "tn")
        carried[h] = (
            all_fade * grad_state
            + mm(query, grad_seen, "tn")
            - mm(b * grow * key, adjoint, "tn")
        )
        grad_query = mm(grad_seen, state, "nt") + mm(grad_scores, key, "nn")
        part_one = mm(grad_scores, query, "tn")
        part_two = fade * mm(fresh, grad_state, "nt")
        part_three = -mm(adjoint, state, "nt")
        coupled = jnp.where(strict, -mm(adjoint, fresh, "nt"), 0.0) * pair
        part_four = mm(coupled, key, "nn")
        part_five = mm(b * coupled, key, "tn")
        grad_key = part_one + part_two + b * grow * part_three + b * part_four + part_five
        grad_value = b * adjoint
        through = grow * row_dot(part_three, key)
        pulled = row_dot(part_four, key)
        grad_b = row_dot(adjoint, value) + through + pulled
        ends = row_dot(part_two, key)
        grad_c = b * (through + pulled) - ends - row_dot(part_one + part_five, key)
        grad_c = row_dot(query, grad_query) + grad_c[:GROUP] + grad_c[GROUP:]
        grad_end = jnp.sum(ends) + jnp.sum(all_fade * grad_state * state)
        grad_c = grad_c + jnp.where(place((GROUP, 1), 0) == GROUP - 1, grad_end, 0.0)
        grad_cums[g] = grad_cums[g] + jnp.where(lanes == 2 * heads + h, grad_c, 0.0)
        for j in range(2):
            half = slice(j * GROUP, (j + 1) * GROUP)
            grad_betas[g] = grad_betas[g] + jnp.where(lanes == j * heads + h, grad_b[half], 0.0)
            grad_parts[h][1 + j][g] = grad_key[half]
            grad_parts[h][3 + j][g] = grad_value[half]
        grad_parts[h][0][g] = grad_query
    triu = (place((GROUP, GROUP), 0) <= place((GROUP, GROUP), 1)).astype(F32)
    grad_log = jnp.concatenate([mm_high(triu, x, "nn") for x in grad_cums], axis=0)
    grad_beta = jnp.concatenate(grad_betas, axis=0)
    grad_decay = grad_log * small_ref[0:1, :] * valid * jax.nn.sigmoid(tail + small_ref[1:2, :])
    grad_mixed_ref[:, 6 * wide :] = (
        grad_beta * beta * (1.0 - sigmoid_tail) + grad_decay
    ).astype(LOW)
    grad_small_ref[0:1, :] += jnp.sum(grad_log * log_decay, axis=0, keepdims=True)
    grad_small_ref[1:2, :] += jnp.sum(grad_decay, axis=0, keepdims=True)

    for h in range(heads):
        for slot in range(5):
            cols = slice(slot * wide + h * 128, slot * wide + (h + 1) * 128)
            grad = jnp.concatenate(grad_parts[h][slot], axis=0)
            pre = summed(slot, h)
            sig = jax.nn.sigmoid(pre)
            if slot < 3:
                act = pre * sig
                scale = lax.rsqrt(row_dot(act, act) + EPS_KEY)
                shaped = act * scale
                if slot == 0:
                    grad = grad * 128**-0.5
                grad = scale * (grad - shaped * row_dot(grad, shaped))
            grad = grad * sig * (1.0 + pre * (1.0 - sig))
            spread[0:count, cols] = grad
            back = 0.0
            for ahead in range(4):
                back = back + spread[pl.ds(ahead, count), cols] * taps_ref[3 - ahead : 4 - ahead, cols]
            grad_mixed_ref[:, cols] = back.astype(LOW)
            for tap in range(4):
                grad_taps_ref[tap : tap + 1, cols] += jnp.sum(
                    grad * padded[pl.ds(5 + tap, count), cols], axis=0, keepdims=True
                )
    end_ref[...] = carried[...]
    last_rim_ref[...] = spread[0:8, :]


def step_tokens(tokens):
    return min(256, tokens)


def block_specs(heads, count, per, order):
    wide = heads * 128
    all_wide = 6 * wide + 128
    piece = min(per, count)
    per, pieces = per // piece, count // piece

    def moved(j):
        def at(i, info):
            i = order(i) * pieces + j
            return (((i // per) ^ info[1]) * per + i % per, 0)

        return at

    whole = lambda *shape: pl.BlockSpec(shape, lambda i, info: (0,) * len(shape))
    return dict(
        mixed=pl.BlockSpec((count, all_wide), lambda i, info: (order(i), 0)),
        halo=pl.BlockSpec((8, all_wide), lambda i, info: (jnp.maximum(order(i) * (count // 8) - 1, 0), 0)),
        head=pl.BlockSpec((count, wide), lambda i, info: (order(i), 0)),
        moved_head=[pl.BlockSpec((piece, wide), moved(j)) for j in range(pieces)],
        taps=whole(8, 5 * wide),
        small=whole(8, 128),
        level=whole(2 * GROUP, 2 * GROUP),
        state=whole(heads, 128, 128),
        kept=pl.BlockSpec((count // GROUP, heads, 128, 128), lambda i, info: (order(i), 0, 0, 0)),
    )


VMEM_BYTES = 40 * 2**20


def mixer_forward(heads, first, length, info, tokens, weight, taps, small, level, start, rim):
    count = step_tokens(length)
    skip = first // count
    wide = heads * 128
    width = tokens.shape[1]
    all_wide = 6 * wide + 128
    s = block_specs(heads, count, count, lambda i: i)
    kept = jax.ShapeDtypeStruct((length // GROUP, heads, 128, 128), F32)
    out = lambda cols, kind: jax.ShapeDtypeStruct((length, cols), kind)
    rows = pl.BlockSpec((count, width), lambda i, info: (i, 0))
    gains = pl.BlockSpec((8, width), lambda i, info: (0, 0))
    held = weight.shape[:3] + (all_wide,)
    return pl.pallas_call(
        functools.partial(forward_kernel, heads, first),
        grid_spec=pltpu.PrefetchScalarGridSpec(
            num_scalar_prefetch=1,
            grid=(length // count,),
            in_specs=[
                pl.BlockSpec((count, width), lambda i, info: (i + skip, 0)),
                pl.BlockSpec(held, lambda i, info: (0, 0, 0, 0)),
                s["taps"], s["small"], s["level"], s["state"], s["taps"],
            ],
            out_specs=[
                s["head"], s["head"], s["kept"], s["kept"], s["kept"], s["state"], s["mixed"], rows, gains, s["taps"]
            ],
            scratch_shapes=[
                pltpu.VMEM((heads, 128, 128), F32),
                pltpu.VMEM((count + 8, 5 * wide), F32),
                pltpu.VMEM((width, all_wide), LOW),
            ],
        ),
        out_shape=[
            out(wide, LOW), out(wide, F32), kept, kept, kept, jax.ShapeDtypeStruct(start.shape, F32),
            out(all_wide, F32), out(width, LOW), jax.ShapeDtypeStruct((8, width), F32),
            jax.ShapeDtypeStruct(rim.shape, F32),
        ],
        compiler_params=pltpu.CompilerParams(vmem_limit_bytes=56 * 2**20),
        cost_estimate=pl.CostEstimate(
            flops=length * heads * (4_000_000 if first == 0 else 18_000_000),
            bytes_accessed=length * heads * 10_000,
            transcendentals=0,
        ),
        name="mixer_forward",
    )(info, tokens, weight, taps, small, level, start, rim)


def mixer_backward(
    heads, first, tokens, per, info, mixed, raw, grad, taps, small, level, solve, fresh, state, start, rim, before
):
    count = step_tokens(tokens)
    steps = tokens // count
    wide = heads * 128
    s = block_specs(heads, count, per, lambda i: steps - 1 - i)
    return pl.pallas_call(
        functools.partial(backward_kernel, heads, first, len(s["moved_head"])),
        grid_spec=pltpu.PrefetchScalarGridSpec(
            num_scalar_prefetch=1,
            grid=(steps,),
            in_specs=[
                s["mixed"], s["halo"], s["head"], s["taps"], s["small"], s["level"],
                s["kept"], s["kept"], s["kept"], s["state"], s["taps"], s["taps"], *s["moved_head"],
            ],
            out_specs=[s["mixed"], s["taps"], s["small"], s["state"], s["taps"]],
            scratch_shapes=[
                pltpu.VMEM((heads, 128, 128), F32),
                pltpu.VMEM((count + 8, 5 * wide), F32),
                pltpu.VMEM((count + 8, 5 * wide), F32),
            ],
        ),
        out_shape=[
            jax.ShapeDtypeStruct((tokens, mixed.shape[1]), LOW),
            jax.ShapeDtypeStruct((8, 5 * wide), F32),
            jax.ShapeDtypeStruct((8, 128), F32),
            jax.ShapeDtypeStruct(start.shape, F32),
            jax.ShapeDtypeStruct(rim.shape, F32),
        ],
        compiler_params=pltpu.CompilerParams(vmem_limit_bytes=VMEM_BYTES),
        cost_estimate=pl.CostEstimate(
            flops=tokens * heads * 26_000_000, bytes_accessed=tokens * heads * 10_000, transcendentals=0
        ),
        name="mixer_backward",
    )(info, mixed, mixed, raw, taps, small, level, solve, fresh, state, start, rim, before, *(grad,) * len(s["moved_head"]))


def unpack_kernel(heads, head_count, info_ref, *refs):
    blocks, refs = refs[:4], refs[4:]
    query_weight, key_weight, value_weight, gate_weight, beta_across, decay_across, gain = refs[:7]
    grad_query, grad_key, grad_value, grad_gate, grad_out, grad_beta, grad_decay, grad_gain = refs[7:]
    wide, full = heads * 128, head_count * 128
    small = 0.0
    for bits, block in enumerate(blocks):
        source = info_ref[1] ^ bits
        slot = 0
        for ref, pieces in ((grad_query, 1), (grad_key, 2), (grad_value, 2), (grad_gate, 1)):
            for piece in range(pieces):
                cols = pl.ds(pl.multiple_of(piece * full + source * wide, 128), wide)
                ref[:, cols] = block[0, :, slot * wide : (slot + 1) * wide].astype(F32)
                slot += 1
        cols = pl.ds(pl.multiple_of(source * wide, 128), wide)
        grad_out[:, cols] = block[0, :, 6 * wide + 128 :].astype(F32)
        row, col = place((128, 128), 1), place((128, 128), 0)
        chosen = (row < 3 * heads) & (col == row // heads * head_count + source * heads + row % heads)
        small = small + mm_low(chosen.astype(F32), block[0, :, 6 * wide : 6 * wide + 128], "nt")
    grad_beta[...] = small[: 2 * head_count]
    grad_decay[...] = small[2 * head_count : 3 * head_count]
    total = 0.0
    for weight, grad in (
        (query_weight, grad_query), (key_weight, grad_key), (value_weight, grad_value), (gate_weight, grad_gate),
    ):
        product = weight[...].astype(F32) * grad[...]
        total = total + mm_high(jnp.ones((8, product.shape[1]), F32), product, "nt")[0:1]
    for weight, grad in ((beta_across, grad_beta), (decay_across, grad_decay)):
        total = total + jnp.sum(weight[...].astype(F32) * grad[...], axis=0, keepdims=True)
    grad_gain[...] = total / gain[...]


def unpack_grads(heads, head_count, info, blocks, weights, gain):
    query, key, value, beta, decay, gate = weights
    share = query.shape[0]
    like = lambda rows, cols: jax.ShapeDtypeStruct((rows, cols), F32)
    vmem = pl.BlockSpec(memory_space=pltpu.VMEM)
    outs = [like(share, weight.shape[1]) for weight in (query, key, value, gate)]
    outs += [like(share, head_count * 128), like(2 * head_count, share), like(head_count, share), like(1, share)]
    ins = [*blocks, query, key, value, gate, beta.T, decay.T, gain.astype(F32)[None, :]]
    query, key, value, gate, out, beta, decay, gain = pl.pallas_call(
        functools.partial(unpack_kernel, heads, head_count),
        in_specs=[pl.BlockSpec(memory_space=pltpu.SMEM)] + [vmem] * len(ins),
        out_specs=[vmem] * len(outs),
        out_shape=outs,
        name="unpack_grads",
    )(info, *ins)
    return query, key, value, beta.T, decay.T, gate, out, gain[0]


def pack_kernel(heads, head_count, info_ref, query, key, value, gate, last, beta_across, decay_across, gains, *outs):
    wide, full = heads * 128, head_count * 128
    small = [ref[...].astype(F32) for ref in (beta_across, decay_across, gains)]
    small = jnp.concatenate(small, axis=0)
    for bits, out in enumerate(outs):
        target = info_ref[1] ^ bits
        slot = 0
        for ref, pieces in ((query, 1), (key, 2), (value, 2), (gate, 1)):
            for piece in range(pieces):
                cols = pl.ds(pl.multiple_of(piece * full + target * wide, 128), wide)
                out[0, :, slot * wide : (slot + 1) * wide] = ref[:, cols]
                slot += 1
        row, col = place((small.shape[0], 128), 0), place((small.shape[0], 128), 1)
        head = col // heads * head_count + target * heads + col % heads
        gain = 3 * head_count + col - 3 * heads
        chosen = row == jnp.where(col < 3 * heads, head, jnp.where(col < 3 * heads + 2, gain, -1))
        out[0, :, 6 * wide + 128 :] = last[:, pl.ds(pl.multiple_of(target * wide, 128), wide)]
        out[0, :, 6 * wide : 6 * wide + 128] = mm_low(small, chosen.astype(F32), "tn").astype(LOW)


def pack_weights(heads, head_count, info, weights, last, gains):
    query, key, value, beta, decay, gate = weights
    share = query.shape[0]
    vmem = pl.BlockSpec(memory_space=pltpu.VMEM)
    gains = jnp.concatenate([gain.astype(F32)[None, :] for gain in gains] + [jnp.zeros((6, share), F32)], axis=0)
    out = jax.ShapeDtypeStruct((1, share, 7 * heads * 128 + 128), LOW)
    return pl.pallas_call(
        functools.partial(pack_kernel, heads, head_count),
        in_specs=[pl.BlockSpec(memory_space=pltpu.SMEM)] + [vmem] * 8,
        out_specs=[vmem] * 4,
        out_shape=[out] * 4,
        name="pack_weights",
    )(info, query, key, value, gate, last, beta.T, decay.T, gains)


def features(weight_ref, index, first=0, last=None):
    piece = weight_ref[:, index, :, first:last]
    return piece.reshape(piece.shape[0] * piece.shape[1], piece.shape[2])


def hold(weight_ref, held_ref, first=0):
    size = weight_ref.shape[0] * weight_ref.shape[2]

    @pl.when(pl.program_id(0) == 0)
    def _():
        for index in range(weight_ref.shape[1]):
            held_ref[index * size : (index + 1) * size, first : first + weight_ref.shape[3]] = features(weight_ref, index)


def feed_forward_kernel(hidden, blocks, *refs):
    gated_refs, out_refs, refs = refs[:blocks], refs[blocks : 2 * blocks], refs[2 * blocks :]
    tokens_ref, grad_ref, weight_ref, gains_ref, second_ref, normed_ref, hidden_ref, acts_ref, partial_ref = refs[:9]
    *kept, held = refs[9:]
    gated = jnp.concatenate([ref[...] for ref in gated_refs], axis=1)
    first = gated.shape[1]
    for index, ref in enumerate(out_refs):
        hold(ref, held, index * ref.shape[3])
    hold(weight_ref, held, first)
    last = first + 2 * hidden
    if kept:

        @pl.when(pl.program_id(0) == 0)
        def _():
            kept[0][...] = held[:, : kept[0].shape[1]]
            kept[1][...] = held[:, last:]

    second = tokens_ref[...].astype(F32) + mm_low(gated, held[:, :first], "nt")
    second_ref[...] = second
    scale = lax.rsqrt(jnp.mean(second * second, axis=1, keepdims=True) + EPS_NORM)
    normed = (second * scale * gains_ref[1:2, :]).astype(LOW)
    normed_ref[...] = normed
    grad_hidden = mm_low(grad_ref[...], held[:, last:], "nn")
    acts = mm_low(normed, held[:, first:last], "nn")
    gate, up = acts[:, :hidden], acts[:, hidden:]
    sig = jax.nn.sigmoid(gate)
    silu_gate = gate * sig
    hidden_ref[...] = (silu_gate * up).astype(LOW)
    grads = [grad_hidden * up * sig * (1.0 + gate * (1.0 - sig)), grad_hidden * silu_gate]
    grads = jnp.concatenate(grads, axis=1).astype(LOW)
    acts_ref[...] = grads
    partial_ref[...] = mm_low(grads, held[:, first:last], "nt").astype(LOW)


def feed_forward_part(hidden, first, tokens, grads, gated, outs, weight, gains):
    length, width = gated[0].shape[0], tokens.shape[1]
    count = min(256, length)
    skip = first // count
    whole_rows = pl.BlockSpec((count, width), lambda i: (i + skip, 0))
    rows = lambda cols: pl.BlockSpec((count, cols), lambda i: (i, 0))
    out = lambda cols, kind: jax.ShapeDtypeStruct((length, cols), kind)
    kept = [gated[0].shape[1], hidden] if first == 0 else []
    return pl.pallas_call(
        functools.partial(feed_forward_kernel, hidden, len(gated)),
        grid=(length // count,),
        in_specs=[rows(block.shape[1]) for block in gated]
        + [pl.BlockSpec(block.shape, lambda i: (0, 0, 0, 0)) for block in outs]
        + [whole_rows, whole_rows, pl.BlockSpec(weight.shape, lambda i: (0, 0, 0, 0))]
        + [pl.BlockSpec((8, width), lambda i: (0, 0))],
        out_specs=[rows(width), rows(width), rows(hidden), rows(2 * hidden), rows(width)]
        + [pl.BlockSpec((width, cols), lambda i: (0, 0)) for cols in kept],
        out_shape=[out(width, F32), out(width, LOW), out(hidden, LOW), out(2 * hidden, LOW), out(width, LOW)]
        + [jax.ShapeDtypeStruct((width, cols), LOW) for cols in kept],
        scratch_shapes=[pltpu.VMEM((width, weight.shape[3] + sum(block.shape[3] for block in outs)), LOW)],
        compiler_params=pltpu.CompilerParams(vmem_limit_bytes=56 * 2**20),
        cost_estimate=pl.CostEstimate(flops=8 * 10**9, bytes_accessed=10**7, transcendentals=0),
        name="feed_forward",
    )(*gated, *outs, tokens, grads, weight, gains)


def weight_grads_kernel(counts, back, *refs):
    if back:
        refs, weight_ref, out_ref, back_ref = refs[:-3], *refs[-3:]
        weight, at = features(weight_ref, 0), 0
        for ref in refs[counts[0][0] : counts[0][0] + counts[0][1]]:
            tokens = ref.shape[0]
            back_ref[at : at + tokens, :] = mm_low(ref[...], weight, "nt").astype(LOW)
            at += tokens
    else:
        *refs, out_ref = refs
    first = 0
    places, share = out_ref.shape[0], out_ref.shape[2]
    for lefts, rights in counts:
        left_refs, right_refs, refs = refs[:lefts], refs[lefts : lefts + rights], refs[lefts + rights :]
        total, at = 0.0, 0
        for right in right_refs:
            tokens = right.shape[0]
            if lefts == rights:
                left = left_refs[at // tokens][...]
            else:
                left = left_refs[0][at : at + tokens, :]
            total = total + mm_low(left, right[...], "tn")
            at += tokens
        width = total.shape[1]
        out_ref[:, 0, :, first : first + width] = total.astype(LOW).reshape(places, share, width)
        first += width


def weight_grads(places, count, pairs, weight=None):
    features_all = pairs[0][0][0].shape[1]
    size = features_all // count
    share = size // places
    width = sum(rights[0].shape[1] for _, rights in pairs)
    specs, arrays, flops = [], [], 0
    for lefts, rights in pairs:
        specs += [pl.BlockSpec((left.shape[0], size), lambda i: (0, i)) for left in lefts]
        specs += [pl.BlockSpec(right.shape, lambda i: (0, 0)) for right in rights]
        arrays += [*lefts, *rights]
        flops += sum(2 * right.shape[0] * right.shape[1] * features_all for right in rights)
    out_specs = [pl.BlockSpec((places, 1, share, width), lambda i: (0, i, 0, 0))]
    out_shape = [jax.ShapeDtypeStruct((places, count, share, width), LOW)]
    if weight is not None:
        tokens = sum(right.shape[0] for right in pairs[0][1])
        specs.append(pl.BlockSpec((places, 1, share, pairs[0][1][0].shape[1]), lambda i: (0, i, 0, 0)))
        arrays.append(weight)
        out_specs.append(pl.BlockSpec((tokens, size), lambda i: (0, i)))
        out_shape.append(jax.ShapeDtypeStruct((tokens, features_all), LOW))
    counts = tuple((len(lefts), len(rights)) for lefts, rights in pairs)
    out, *back = pl.pallas_call(
        functools.partial(weight_grads_kernel, counts, weight is not None),
        grid=(count,),
        in_specs=specs,
        out_specs=out_specs,
        out_shape=out_shape,
        compiler_params=pltpu.CompilerParams(vmem_limit_bytes=VMEM_BYTES),
        cost_estimate=pl.CostEstimate(flops=flops, bytes_accessed=10**7, transcendentals=0),
        name="weight_grads",
    )(*arrays)
    return out.reshape(-1, width), *back


def swap(array, axis, bits):
    return lax.ppermute(array, axis, [(i, i ^ bits) for i in range(lax.axis_size(axis))])


def on_square():
    return lax.axis_size("seq") == 4


def power_of_two(axis):
    return lax.axis_size(axis) & (lax.axis_size(axis) - 1) == 0


def after(array, *others):
    return lax.optimization_barrier((array,) + others)[0]


def spread_out(array):
    if not on_square():
        whole = lax.all_gather(array, "seq")
        return [whole[i] for i in range(whole.shape[0])]
    far, beside, below = (swap(array, "seq", bits) for bits in (3, 1, 2))
    return [array, beside, below, far]


def spread_out_near(*arrays):
    if not on_square():
        return [spread_out(array) for array in arrays]
    half = arrays[0].shape[0] // 2
    near = [(swap(array, "seq", 1), swap(array, "seq", 2)) for array in arrays]
    far = [(swap(below[:half], "seq", 1), swap(beside[half:], "seq", 2)) for beside, below in near]
    return [
        [array, beside, below, jnp.concatenate(parts, axis=0)]
        for array, (beside, below), parts in zip(arrays, near, far)
    ]


def in_place_order(blocks):
    if not on_square():
        return jnp.concatenate(blocks, axis=0)
    me = lax.axis_index("seq")
    size = blocks[0].shape[0]
    out = jnp.zeros((len(blocks) * size,) + blocks[0].shape[1:], blocks[0].dtype)
    for bits, block in enumerate(blocks):
        out = lax.dynamic_update_slice(out, block, ((me ^ bits) * size, 0))
    return out


def row_block(array, index):
    size = array.shape[0] // lax.axis_size("seq")
    return lax.dynamic_slice_in_dim(array, index * size, size, 0)


def to_send(array):
    if not on_square():
        return [array.astype(LOW)]
    me = lax.axis_index("seq")
    return [row_block(array, me ^ bits).astype(LOW) for bits in (3, 1, 2)]


def send(blocks):
    if not on_square():
        return [lax.psum_scatter(blocks[0], "seq", scatter_dimension=0, tiled=True)]
    return [swap(block, "seq", bits) for bits, block in zip((3, 1, 2), blocks)]


def total(array, got):
    if not on_square():
        return got[0].astype(F32)
    return row_block(array, lax.axis_index("seq")).astype(F32) + sum(block.astype(F32) for block in got)


def exchange_unordered(blocks):
    me = lax.axis_index("seq")
    sends = tuple(lax.dynamic_index_in_dim(blocks, me ^ bits, 0, True) for bits in (0, 1, 2, 3))
    sends = lax.optimization_barrier(sends)
    got = tuple(swap(sends[bits], "seq", bits) for bits in (3, 1, 2))
    far, beside, below = lax.optimization_barrier(got)
    return [sends[0], beside, below, far]


def exchange(blocks):
    if not on_square():
        return lax.all_to_all(blocks, "seq", 0, 0, tiled=True)
    me = lax.axis_index("seq")
    others = (3, 1, 2)
    sends = lax.optimization_barrier(tuple(lax.dynamic_index_in_dim(blocks, me ^ bits, 0, True) for bits in others))
    got = lax.optimization_barrier(tuple(swap(block, "seq", bits) for bits, block in zip(others, sends)))
    out = blocks
    for bits, block in zip(others, got):
        out = lax.dynamic_update_slice(out, block, (me ^ bits, 0, 0))
    return out


def sum_over(array, axis):
    if not power_of_two(axis):
        return lax.psum(array, axis)
    bits = 1
    while bits < lax.axis_size(axis):
        array = array + swap(array, axis, bits)
        bits *= 2
    return array


def gather_rows(mine):
    return lax.all_gather(mine, "rows", axis=0)


def in_rows(whole):
    rows, count, size, width = whole.shape
    return whole.transpose(1, 0, 2, 3).reshape(count * rows * size, width)


def by_rows(grad):
    count, rows = lax.axis_size("seq"), lax.axis_size("rows")
    size = grad.shape[0] // (count * rows)
    grad = grad.astype(LOW).reshape(count, rows, size, grad.shape[1])
    return grad.transpose(1, 0, 2, 3).reshape(-1, grad.shape[3])


def sum_rows(grad):
    count = lax.axis_size("seq")
    summed = lax.psum_scatter(grad, "rows", scatter_dimension=0, tiled=True)
    return summed.reshape(count, -1, grad.shape[1])


def project(left, right):
    return jnp.dot(left, right, preferred_element_type=F32)


def outer_sum(left, right):
    return lax.dot_general(left, right, FORMS["tn"], preferred_element_type=F32)


def back_project(left, right):
    return lax.dot_general(left, right, FORMS["nt"], preferred_element_type=F32)


def norm_scale(features):
    return lax.rsqrt(jnp.mean(features * features, axis=-1, keepdims=True) + EPS_NORM)


def norm_back(features, scale, grad):
    return scale * grad - features * scale**3 * jnp.mean(grad * features, axis=-1, keepdims=True)


def on_device(
    block_input, valid_length, query_weight, key_weight, value_weight, beta_weight, decay_weight, gate_weight,
    out_weight, ffn_gate_weight, ffn_up_weight, ffn_down_weight, norm_gain, ffn_norm_gain, head_norm_gain,
    decay_log, decay_bias, conv_weight, output_grad,
):
    count = lax.axis_size("seq")
    me = lax.axis_index("seq")
    rows_here, tokens_here, model_width = block_input.shape
    share = query_weight.shape[0]
    head_count = decay_log.shape[0]
    heads = max(1, head_count // count)
    blocks = head_count // heads
    copies = count // blocks
    block = me // copies
    wide = heads * 128
    hidden = ffn_gate_weight.shape[1] // count
    square = on_square() and copies == 1

    def cut(weight, pieces, at):
        width = weight.shape[1] // (pieces * blocks)
        at = at // copies
        return [
            weight[:, (p * blocks + at) * width : (p * blocks + at + 1) * width] for p in range(pieces)
        ]

    def cut_hidden(weight, at):
        return [weight[:, at * hidden : (at + 1) * hidden]]

    gains = jnp.stack([norm_gain, ffn_norm_gain], axis=1)

    def tail_of(at):
        parts = cut(beta_weight, 2, at) + cut(decay_weight, 1, at) + [gains]
        return parts + [jnp.zeros((share, 128 - 3 * heads - 2), LOW)]

    def first_of(at):
        parts = cut(query_weight, 1, at) + cut(key_weight, 2, at) + cut(value_weight, 2, at)
        return jnp.concatenate(parts + cut(gate_weight, 1, at) + tail_of(at) + cut(out_weight, 1, at), axis=1)

    def rest_of(at):
        parts = cut_hidden(ffn_gate_weight, at) + cut_hidden(ffn_up_weight, at) + cut_hidden(ffn_down_weight, at)
        return jnp.concatenate(parts, axis=1)

    def pack(part):
        return jnp.stack([part(at) for at in range(count)])

    info = jnp.stack([valid_length[0], me if on_square() else jnp.int32(0)])
    mixer_weights = (query_weight, key_weight, value_weight, beta_weight, decay_weight, gate_weight)
    if on_square():
        packed = pack_weights(heads, head_count, info, mixer_weights, out_weight, (norm_gain, ffn_norm_gain))
        got = tuple(swap(packed[bits], "seq", bits) for bits in (3, 1, 2))
        far, beside, below = lax.optimization_barrier(got)
        first_share = jnp.zeros((count,) + packed[0].shape[1:], LOW)
        for bits, block_got in enumerate((packed[0], beside, below, far)):
            first_share = lax.dynamic_update_slice(first_share, block_got, (me ^ bits, 0, 0))
    else:
        first_share = exchange(pack(first_of))
    own, own_grad, rest_pack, first_share = lax.optimization_barrier(
        (block_input.reshape(tokens_here, model_width), output_grad.reshape(tokens_here, model_width), pack(rest_of),
         first_share)
    )
    mixed_parts = gather_rows(first_share)
    everyone_got, grads_got = spread_out_near(own, own_grad)
    rest_share = exchange(rest_pack)
    everyone, grad_branch = in_place_order(everyone_got), in_place_order(grads_got)
    rest_parts = gather_rows(rest_share)
    if not square:
        mixed_parts = in_rows(mixed_parts)[None, None]
    mixed_parts, everyone, grad_branch = lax.optimization_barrier((mixed_parts, everyone, grad_branch))
    out_got = spread_out(mixed_parts[:, :, :, 6 * wide + 128 :])
    mixed_weight = mixed_parts[0, 0, :, : 6 * wide + 128]
    if not square:
        out_own = mixed_parts[0, 0, :, 6 * wide + 128 :]
        out_all = jnp.concatenate([block_got[0, 0] for block_got in out_got[:: 1 if on_square() else copies]], axis=1)
        rest_weight = in_rows(rest_parts)
        ffn_in, ffn_down = rest_weight[:, : 2 * hidden], rest_weight[:, 2 * hidden :]

    def block_lanes(vector, first):
        mine = lax.dynamic_slice_in_dim(vector, block * heads, heads)
        return jnp.pad(mine, (first, 128 - first - heads))

    small = jnp.stack([block_lanes(-jnp.exp(decay_log), 2 * heads), block_lanes(decay_bias, 2 * heads), head_norm_gain])
    small = jnp.pad(small, ((0, 5), (0, 0)))
    taps = [
        lax.dynamic_slice_in_dim(conv_weight, (slot * blocks + block) * wide, wide, 1) for slot in range(5)
    ]
    taps = jnp.pad(jnp.concatenate(taps, axis=1), ((0, 8 - conv_weight.shape[0]), (0, 0)))
    level = level_table()

    length = count * tokens_here
    part = length // 2
    tie = lax.optimization_barrier

    zero_state = jnp.zeros((heads, 128, 128), F32)
    no_rim = jnp.zeros((8, 5 * wide), F32)

    def forward(first, start, rim):
        outs = mixer_forward(heads, first, part, info, everyone, mixed_parts, taps, small, level, start, rim)
        return outs[0], outs[1:5], outs[5], outs[6], outs[7], outs[8], outs[9]

    gated_a, kept_a, end, mixed_a, normed_a, gains, middle_rim = forward(0, zero_state, no_rim)
    end, out_got = tie((end, out_got))
    gated_got_a = spread_out(gated_a)
    gated_b, kept_b, end, mixed_b, normed_b, _, _ = forward(part, end, middle_rim)
    gated_b, gated_got_a = tie((gated_b, gated_got_a))
    gated_got_b = spread_out(gated_b)
    gain_first, gain_second = gains[0], gains[1]

    def feed_forward(index, gated_got, got=None):
        if square:
            outs = feed_forward_part(
                hidden, index * part, everyone, grad_branch, gated_got, out_got, rest_parts, gains
            )
            return (*tie(tuple(outs[:5]) + (got,)), outs[5:])
        rows = slice(index * part, (index + 1) * part)
        gated_all = jnp.concatenate(gated_got[:: 1 if on_square() else copies], axis=1)
        second = everyone[rows].astype(F32) + back_project(gated_all, out_all)
        normed_two = (second * norm_scale(second) * gain_second).astype(LOW)
        if got is not None:
            normed_two, got = tie((normed_two, got))
        acts = project(normed_two, ffn_in)
        gate_act, up_act = acts[:, :hidden], acts[:, hidden:]
        sig = jax.nn.sigmoid(gate_act)
        hidden_low = (gate_act * sig * up_act).astype(LOW)
        grad_hidden = project(grad_branch[rows], ffn_down)
        grad_acts = [grad_hidden * up_act * sig * (1.0 + gate_act * (1.0 - sig)), grad_hidden * gate_act * sig]
        grad_acts = jnp.concatenate(grad_acts, axis=1).astype(LOW)
        return second, normed_two, hidden_low, grad_acts, back_project(grad_acts, ffn_in), got, None

    def second_back(index, second, partial, got):
        grad = total(partial, got) * gain_second
        second = row_block(second, me)
        out_grad = row_block(grad_branch[index * part : (index + 1) * part], me)
        return (out_grad.astype(F32) + norm_back(second, norm_scale(second), grad)).astype(LOW)

    second_a, normed_two_a, hidden_a, grad_acts_a, partial_a, _, kept = feed_forward(0, gated_got_a)
    if square:
        out_own, ffn_down = kept
    sends_a, gated_got_b = tie((to_send(partial_a), gated_got_b))
    got_a = send(sends_a)
    second_b, normed_two_b, hidden_b, grad_acts_b, partial_b, got_a, _ = feed_forward(1, gated_got_b, got_a)
    sends_b, hidden_b, grad_acts_b = tie((to_send(partial_b), hidden_b, grad_acts_b))
    got_b = send(sends_b)

    join_parts = lambda a, b: jnp.concatenate([a, b], axis=0)
    hidden_low = join_parts(hidden_a, hidden_b)
    down = back_project(hidden_low, ffn_down)
    down_sends = to_send(down)
    grad_second_a = second_back(0, second_a, partial_a, got_a)
    got_b, down_sends, grad_second_a = tie((got_b, down_sends, grad_second_a))
    grad_second_b, grad_acts_b = tie((second_back(1, second_b, partial_b, got_b), grad_acts_b))
    grads_two_b = spread_out(grad_second_b)
    if square:
        pairs = [((normed_two_a, normed_two_b), (grad_acts_a, grad_acts_b)), ((grad_branch,), (hidden_a, hidden_b))]
        (early,) = weight_grads(lax.axis_size("rows"), count, pairs)
    else:
        early_in = outer_sum(join_parts(normed_two_a, normed_two_b), join_parts(grad_acts_a, grad_acts_b))
        early = by_rows(jnp.concatenate([early_in, outer_sum(grad_branch, hidden_low)], axis=1))
    grads_two_b, early, down_sends, grad_second_a = tie((grads_two_b, early, down_sends, grad_second_a))
    early = sum_rows(early)
    grads_two_a = spread_out(grad_second_a)

    grad_gated = project(jnp.concatenate(grads_two_b, axis=0), out_own)
    grad_pre_b, taps_b, small_b, end, rim = mixer_backward(
        heads, part, part, part // count, info, mixed_b, kept_b[0], grad_gated, taps, small, level, *kept_b[1:],
        zero_state, no_rim, middle_rim,
    )
    end, grads_two_a, down_sends = tie((end, grads_two_a, down_sends))
    down_got = send(down_sends)
    grad_gated = project(jnp.concatenate(grads_two_a, axis=0), out_own)
    grad_second = join_parts(in_place_order(grads_two_a), in_place_order(grads_two_b))

    def once(array):
        return array if copies == 1 else array * (me % copies == 0).astype(array.dtype)

    grad_pre_a, taps_a, small_a, end, rim = mixer_backward(
        heads, 0, part, part // count, info, mixed_a, kept_a[0], grad_gated, taps, small, level, *kept_a[1:], end, rim,
        no_rim,
    )
    grad_pre_a, taps_a, small_a, down_got = tie((grad_pre_a, taps_a, small_a, down_got))
    grad_pre_a, grad_pre_b = once(grad_pre_a), once(grad_pre_b)
    if square:
        pairs = [((normed_a, normed_b), (grad_pre_a, grad_pre_b)), ((grad_second,), (gated_a, gated_b))]
        late, grad_normed = weight_grads(lax.axis_size("rows"), count, pairs, mixed_parts)
    else:
        out_grad = once(outer_sum(grad_second, join_parts(gated_a, gated_b)).astype(LOW))
        late = outer_sum(join_parts(normed_a, normed_b), join_parts(grad_pre_a, grad_pre_b)).astype(LOW)
        late = by_rows(jnp.concatenate([late, out_grad], axis=1))
        grad_normed = back_project(join_parts(grad_pre_a, grad_pre_b), mixed_weight)
    grad_taps, grad_small = taps_a + taps_b, small_a + small_b
    late, early, grad_taps, grad_small, down_got, grad_normed = tie(
        (late, early, grad_taps, grad_small, down_got, grad_normed)
    )
    grad_normed_got = send(to_send(grad_normed))
    late = sum_rows(late)
    early = exchange(early)

    def at_block(vector, first, width):
        mine = once(vector[first : first + width])
        return lax.dynamic_update_slice(jnp.zeros((blocks * width,), F32), mine, (block * width,))

    flat = [once(grad_small[2]), at_block(grad_small[0], 2 * heads, heads), at_block(grad_small[1], 2 * heads, heads)]
    flat = jnp.concatenate(flat)
    taps_wide = 5 * wide
    flat = jnp.pad(flat, (0, -flat.shape[0] % taps_wide)).reshape(-1, taps_wide)
    pooled = sum_over(jnp.concatenate([once(grad_taps[:4]), flat], axis=0), "rows")
    pooled, grad_normed_got = tie((pooled, grad_normed_got))
    by_place = lax.dynamic_update_slice(jnp.zeros((blocks, 4, taps_wide), F32), pooled[None, :4], (block, 0, 0))
    pooled = sum_over(jnp.concatenate([by_place.reshape(-1, taps_wide), pooled[4:]], axis=0), "seq")
    ends = [128, 128 + head_count, 128 + 2 * head_count]

    second = row_block(join_parts(second_a, second_b), me)
    result = (second + total(down, down_got)).astype(LOW).reshape(block_input.shape)
    def join(grads, first, pieces, width, every=copies):
        return jnp.concatenate(
            [
                grads[b, :, first + p * width : first + (p + 1) * width]
                for p in range(pieces)
                for b in range(0, count, every)
            ],
            axis=1,
        ).astype(F32)

    def gain_grad(gain, *pairs):
        summed = sum(jnp.sum(weight.astype(F32) * grad, axis=1) for weight, grad in pairs)
        return summed / gain.astype(F32)

    grad_ffn_gate = join(early, 0, 1, hidden, 1)
    grad_ffn_up = join(early, hidden, 1, hidden, 1)
    grad_ffn_down = join(early, 2 * hidden, 1, hidden, 1)
    grad_gain_second = gain_grad(ffn_norm_gain, (ffn_gate_weight, grad_ffn_gate), (ffn_up_weight, grad_ffn_up))
    flat = pooled[4 * blocks :].reshape(-1)
    grad_conv = pooled[: 4 * blocks].reshape(blocks, 4, taps_wide)
    grad_conv = jnp.concatenate(
        [grad_conv[b, :, slot * wide : (slot + 1) * wide] for slot in range(5) for b in range(blocks)], axis=1
    )
    late, result, grad_ffn_gate, grad_ffn_up, grad_ffn_down, grad_gain_second, grad_normed_got = tie(
        (late, result, grad_ffn_gate, grad_ffn_up, grad_ffn_down, grad_gain_second, grad_normed_got)
    )
    tokens = own.astype(F32)
    grad_tokens = norm_back(tokens, norm_scale(tokens), total(grad_normed, grad_normed_got) * gain_first)
    grad_input = row_block(grad_second, me).astype(F32) + grad_tokens
    grad_input = grad_input.reshape(block_input.shape)

    if on_square():
        late = exchange_unordered(late)
        *mixer_grads, grad_out, grad_gain_first = unpack_grads(heads, head_count, info, late, mixer_weights, norm_gain)
        grad_query, grad_key, grad_value, grad_beta, grad_decay, grad_gate = mixer_grads
    else:
        late = exchange(late)
        grad_query = join(late, 0, 1, wide)
        grad_key = join(late, wide, 2, wide)
        grad_value = join(late, 3 * wide, 2, wide)
        grad_beta = join(late, 6 * wide, 2, heads)
        grad_decay = join(late, 6 * wide + 2 * heads, 1, heads)
        grad_gate = join(late, 5 * wide, 1, wide)
        grad_out = join(late, 6 * wide + 128, 1, wide)
        mixer_grads = (grad_query, grad_key, grad_value, grad_beta, grad_decay, grad_gate)
        grad_gain_first = gain_grad(norm_gain, *zip(mixer_weights, mixer_grads))
    return (
        result,
        grad_input,
        grad_query,
        grad_key,
        grad_value,
        grad_beta,
        grad_decay,
        grad_gate,
        grad_out,
        grad_ffn_gate,
        grad_ffn_up,
        grad_ffn_down,
        grad_gain_first,
        grad_gain_second,
        flat[: ends[0]],
        flat[ends[0] : ends[1]],
        flat[ends[1] : ends[2]],
        grad_conv,
    )


def solution(mesh):
    tokens, weight, vector, whole = P("rows", "seq", None), P(BOTH, None), P(BOTH), P()
    return jax.shard_map(
        on_device,
        mesh=mesh,
        in_specs=(tokens, P("rows")) + (weight,) * 10 + (vector,) * 2 + (whole,) * 4 + (tokens,),
        out_specs=(tokens, tokens) + (weight,) * 10 + (vector,) * 2 + (whole,) * 4,
        check_vma=False,
    )
```

```python
import functools

import jax
import jax.numpy as jnp
from jax import lax
from jax.experimental import pallas as pl
from jax.experimental.pallas import tpu as pltpu
from jax.sharding import PartitionSpec as P

GROUP = 64
EPS_NORM = 1e-06
EPS_KEY = 1e-06
EPS_HEAD = 1e-05
LOW = jnp.bfloat16
F32 = jnp.float32
HIGHEST = lax.Precision.HIGHEST
BOTH = ("seq", "rows")

FORMS = {
    "nn": (((1,), (0,)), ((), ())),
    "nt": (((1,), (1,)), ((), ())),
    "tn": (((0,), (0,)), ((), ())),
}


def split_low(a):
    high = a.astype(LOW)
    return high, (a - high.astype(F32)).astype(LOW)


def mm(a, b, form):
    a_axis = 0 if form == "tn" else 1
    b_axis = 1 if form == "nt" else 0
    a_two = jnp.concatenate(split_low(a), axis=a_axis)
    b_high, b_low = split_low(b)
    b_two = jnp.concatenate([b_high, b_low], axis=1 - b_axis)
    b_two = jnp.concatenate([b_two, b_two], axis=b_axis)
    out = lax.dot_general(a_two, b_two, FORMS[form], preferred_element_type=F32)
    half = out.shape[1] // 2
    return out[:, :half] + out[:, half:]


def mm_low(a, b, form):
    return lax.dot_general(a.astype(LOW), b.astype(LOW), FORMS[form], preferred_element_type=F32)


def mm_high(a, b, form):
    return lax.dot_general(a, b, FORMS[form], precision=HIGHEST, preferred_element_type=F32)


def row_dot(a, b):
    return jnp.sum(a * b, axis=1, keepdims=True)


def place(shape, axis):
    return lax.broadcasted_iota(jnp.int32, shape, axis)


def level_table():
    time = 2 * (jnp.arange(2 * GROUP) % GROUP) + jnp.arange(2 * GROUP) // GROUP
    row, col = time[:, None], time[None, :]
    differ = row ^ col
    level = sum((differ >= 2**m).astype(jnp.int32) for m in range(1, 7))
    return jnp.where(row > col, level, -1)


def inverses(systems, level):
    size = level.shape[0]
    eye = (place((size, size), 0) == place((size, size), 1)).astype(F32)
    found = [eye - jnp.where(level == 0, a, 0.0) for a in systems]
    for m in range(1, 7):
        inner = [mm(jnp.where(level == m, a, 0.0), t, "nn") for a, t in zip(systems, found)]
        found = [t - mm(t, s, "nn") for t, s in zip(found, inner)]
    return found


def conv_active(pad_ref, taps_ref, first, count):
    cols = slice(first, first + 128)
    summed = 0.0
    for back in range(4):
        summed = summed + pad_ref[pl.ds(8 - back, count), cols] * taps_ref[3 - back : 4 - back, cols]
    return summed


def silu(x):
    return x * jax.nn.sigmoid(x)


def softplus(x):
    return jnp.maximum(x, 0.0) + jnp.log1p(jnp.exp(-jnp.abs(x)))


def cum_decays(log_decay):
    tril = (place((GROUP, GROUP), 0) >= place((GROUP, GROUP), 1)).astype(F32)
    across = (place((GROUP, 2 * GROUP), 0) <= place((GROUP, 2 * GROUP), 1) % GROUP).astype(F32)
    return mm_high(tril, log_decay, "nn"), mm_high(log_decay, across, "tn")


def twice(a):
    return jnp.concatenate([a, a], axis=0)


def group_setup(level, beta, cum, across, head, heads):
    lane = 2 * heads + head
    c = cum[:, lane : lane + 1]
    row = across[lane : lane + 1, :]
    c_two = twice(c)
    end = c[GROUP - 1 : GROUP, :]
    b = jnp.concatenate([beta[:, head : head + 1], beta[:, heads + head : heads + head + 1]], axis=0)
    strict = level >= 0
    pair = jnp.where(strict, jnp.exp(jnp.where(strict, c_two - row, 0.0)), 0.0)
    seen = place((GROUP, 2 * GROUP), 1) % GROUP <= place((GROUP, 2 * GROUP), 0)
    view = jnp.where(seen, jnp.exp(jnp.where(seen, c - row, 0.0)), 0.0)
    return c, c_two, end, b, pair, view


def forward_kernel(
    heads, first, info_ref, tokens_ref, weight_ref, taps_ref, small_ref, level_ref, start_ref, rim_ref,
    out_ref, raw_ref, solve_ref, fresh_ref, state_ref, end_ref, mixed_ref, normed_ref, gains_ref, last_rim_ref,
    carried, padded, held,
):
    step = pl.program_id(0)
    count = mixed_ref.shape[0]
    hold(weight_ref, held)
    tokens = tokens_ref[...].astype(F32)
    scale = lax.rsqrt(jnp.mean(tokens * tokens, axis=1, keepdims=True) + EPS_NORM)
    chosen = (place((8, 128), 1) == place((8, 128), 0) + 3 * heads).astype(F32)
    gains = mm_low(chosen, held[:, 6 * heads * 128 :], "nt")
    gains_ref[...] = gains
    normed = (tokens * scale * gains[0:1]).astype(LOW)
    normed_ref[...] = normed
    mixed_ref[...] = jnp.dot(normed, held[...], preferred_element_type=F32)
    block = step + first // count
    groups = count // GROUP
    wide = heads * 128

    @pl.when(step == 0)
    def _():
        carried[...] = start_ref[...]

    padded[0:8, :] = jnp.where(step > 0, padded[count : count + 8, :], rim_ref[...])
    padded[8 : 8 + count, :] = mixed_ref[:, : 5 * wide]
    last_rim_ref[...] = padded[count : count + 8, :]
    valid = (block * count + place((count, 1), 0) < info_ref[0]).astype(F32)
    level = level_ref[...]
    tail = mixed_ref[:, 6 * wide :]
    beta = jax.nn.sigmoid(tail) * valid
    log_decay = small_ref[0:1, :] * softplus(tail + small_ref[1:2, :]) * valid

    def active(slot, head):
        return silu(conv_active(padded, taps_ref, slot * wide + head * 128, count))

    def unit(x):
        return x * lax.rsqrt(row_dot(x, x) + EPS_KEY)

    queries = [unit(active(0, h)) * 128**-0.5 for h in range(heads)]
    keys = [[unit(active(1 + j, h)) for j in range(2)] for h in range(heads)]
    values = [[active(3 + j, h) for j in range(2)] for h in range(heads)]
    work = []
    for g in range(groups):
        rows = slice(g * GROUP, (g + 1) * GROUP)
        cum, across = cum_decays(log_decay[rows])
        for h in range(heads):
            key = jnp.concatenate([keys[h][0][rows], keys[h][1][rows]], axis=0)
            value = jnp.concatenate([values[h][0][rows], values[h][1][rows]], axis=0)
            c, c_two, end, b, pair, view = group_setup(level, beta[rows], cum, across, h, heads)
            gram = mm(key, key, "nt")
            work.append((g, h, rows, key, value, c, c_two, end, b, view, b * pair * gram))
    solves = inverses([w[-1] for w in work], level)
    raws = [[None] * groups for _ in range(heads)]
    ready = []
    for (g, h, rows, key, value, c, c_two, end, b, view, _), solve in zip(work, solves):
        solve_ref[g, h] = solve
        query = queries[h][rows]
        weights = view * mm(query, key, "nt")
        key_solve = mm(solve, b * jnp.exp(c_two) * key, "nn")
        pseudo = mm(solve, b * value, "nn")
        ready.append((query, weights, key_solve, pseudo))
    for (g, h, rows, key, value, c, c_two, end, b, view, _), made in zip(work, ready):
        query, weights, key_solve, pseudo = made
        state = carried[h]
        state_ref[g, h] = state
        fresh = pseudo - mm(key_solve, state, "nn")
        fresh_ref[g, h] = fresh
        carried[h] = jnp.exp(end) * state + mm(jnp.exp(end - c_two) * key, fresh, "tn")
        raws[h][g] = jnp.exp(c) * mm(query, state, "nn") + mm(weights, fresh, "nn")
    for h in range(heads):
        cols = slice(h * 128, (h + 1) * 128)
        raw = jnp.concatenate(raws[h], axis=0)
        raw_ref[:, cols] = raw
        scale = lax.rsqrt(jnp.mean(raw * raw, axis=1, keepdims=True) + EPS_HEAD)
        gated = raw * scale * small_ref[2:3, :] * silu(mixed_ref[:, 5 * wide + h * 128 : 5 * wide + (h + 1) * 128]) * valid
        out_ref[:, cols] = gated.astype(LOW)
    end_ref[...] = carried[...]


def backward_kernel(
    heads, first, pieces, info_ref, mixed_ref, halo_ref, raw_ref, taps_ref, small_ref, level_ref,
    solve_ref, fresh_ref, state_ref, start_ref, rim_ref, before_ref, *refs,
):
    grad_refs = refs[:pieces]
    grad_mixed_ref, grad_taps_ref, grad_small_ref, end_ref, last_rim_ref, carried, padded, spread = refs[pieces:]
    step = pl.program_id(0)
    count = mixed_ref.shape[0]
    local = pl.num_programs(0) - 1 - step
    block = local + first // count
    groups = count // GROUP
    wide = heads * 128

    @pl.when(step == 0)
    def _():
        carried[...] = start_ref[...]
        spread[0:8, :] = rim_ref[...]
        grad_taps_ref[...] = jnp.zeros_like(grad_taps_ref)
        grad_small_ref[...] = jnp.zeros_like(grad_small_ref)

    spread[count : count + 8, :] = spread[0:8, :]
    padded[0:8, :] = jnp.where(local > 0, halo_ref[:, : 5 * wide], before_ref[...])
    padded[8 : 8 + count, :] = mixed_ref[:, : 5 * wide]
    valid = (block * count + place((count, 1), 0) < info_ref[0]).astype(F32)
    level = level_ref[...]
    strict = level >= 0
    tail = mixed_ref[:, 6 * wide :]
    sigmoid_tail = jax.nn.sigmoid(tail)
    beta = sigmoid_tail * valid
    log_decay = small_ref[0:1, :] * softplus(tail + small_ref[1:2, :]) * valid
    lanes = place((1, 128), 1)

    grad_raws = []
    for h in range(heads):
        cols = slice(h * 128, (h + 1) * 128)
        gate_cols = slice(5 * wide + h * 128, 5 * wide + (h + 1) * 128)
        raw, gate = raw_ref[:, cols], mixed_ref[:, gate_cols]
        grad = jnp.concatenate([ref[:, cols] for ref in grad_refs], axis=0) * valid
        sig = jax.nn.sigmoid(gate)
        scale = lax.rsqrt(jnp.mean(raw * raw, axis=1, keepdims=True) + EPS_HEAD)
        shaped = raw * scale
        gain = small_ref[2:3, :]
        grad_mixed_ref[:, gate_cols] = (grad * shaped * gain * sig * (1.0 + gate * (1.0 - sig))).astype(LOW)
        grad_normed = grad * gate * sig
        grad_small_ref[2:3, :] += jnp.sum(grad_normed * shaped, axis=0, keepdims=True)
        grad_shaped = grad_normed * gain
        grad_raws.append(scale * (grad_shaped - shaped * jnp.mean(grad_shaped * shaped, axis=1, keepdims=True)))

    def summed(slot, head):
        return conv_active(padded, taps_ref, slot * wide + head * 128, count)

    def unit(x):
        return x * lax.rsqrt(row_dot(x, x) + EPS_KEY)

    queries = [unit(silu(summed(0, h))) * 128**-0.5 for h in range(heads)]
    keys = [[unit(silu(summed(1 + j, h))) for j in range(2)] for h in range(heads)]
    values = [[silu(summed(3 + j, h)) for j in range(2)] for h in range(heads)]
    work = []
    for g in reversed(range(groups)):
        rows = slice(g * GROUP, (g + 1) * GROUP)
        cum, across = cum_decays(log_decay[rows])
        for h in range(heads):
            key = jnp.concatenate([keys[h][0][rows], keys[h][1][rows]], axis=0)
            value = jnp.concatenate([values[h][0][rows], values[h][1][rows]], axis=0)
            c, c_two, end, b, pair, view = group_setup(level, beta[rows], cum, across, h, heads)
            query, grad_raw = queries[h][rows], grad_raws[h][rows]
            scores = view * mm(query, key, "nt")
            late = mm(scores, grad_raw, "tn")
            grad_scores = view * mm(grad_raw, fresh_ref[g, h], "nt")
            work.append((g, h, rows, key, value, c, c_two, end, b, pair, query, grad_raw, late, grad_scores))
    grad_parts = [[[None] * groups for _ in range(5)] for _ in range(heads)]
    grad_betas, grad_cums = [0.0] * groups, [0.0] * groups
    for (g, h, rows, key, value, c, c_two, end, b, pair, query, grad_raw, late, grad_scores) in work:
        state, fresh, solve = state_ref[g, h], fresh_ref[g, h], solve_ref[g, h]
        grad_state = carried[h]
        grow, fade, all_fade = jnp.exp(c_two), jnp.exp(end - c_two), jnp.exp(end)
        grad_seen = jnp.exp(c) * grad_raw
        grad_fresh = late + mm(fade * key, grad_state, "nn")
        adjoint = mm(solve, grad_fresh, "tn")
        carried[h] = (
            all_fade * grad_state
            + mm(query, grad_seen, "tn")
            - mm(b * grow * key, adjoint, "tn")
        )
        grad_query = mm(grad_seen, state, "nt") + mm(grad_scores, key, "nn")
        part_one = mm(grad_scores, query, "tn")
        part_two = fade * mm(fresh, grad_state, "nt")
        part_three = -mm(adjoint, state, "nt")
        coupled = jnp.where(strict, -mm(adjoint, fresh, "nt"), 0.0) * pair
        part_four = mm(coupled, key, "nn")
        part_five = mm(b * coupled, key, "tn")
        grad_key = part_one + part_two + b * grow * part_three + b * part_four + part_five
        grad_value = b * adjoint
        through = grow * row_dot(part_three, key)
        pulled = row_dot(part_four, key)
        grad_b = row_dot(adjoint, value) + through + pulled
        ends = row_dot(part_two, key)
        grad_c = b * (through + pulled) - ends - row_dot(part_one + part_five, key)
        grad_c = row_dot(query, grad_query) + grad_c[:GROUP] + grad_c[GROUP:]
        grad_end = jnp.sum(ends) + jnp.sum(all_fade * grad_state * state)
        grad_c = grad_c + jnp.where(place((GROUP, 1), 0) == GROUP - 1, grad_end, 0.0)
        grad_cums[g] = grad_cums[g] + jnp.where(lanes == 2 * heads + h, grad_c, 0.0)
        for j in range(2):
            half = slice(j * GROUP, (j + 1) * GROUP)
            grad_betas[g] = grad_betas[g] + jnp.where(lanes == j * heads + h, grad_b[half], 0.0)
            grad_parts[h][1 + j][g] = grad_key[half]
            grad_parts[h][3 + j][g] = grad_value[half]
        grad_parts[h][0][g] = grad_query
    triu = (place((GROUP, GROUP), 0) <= place((GROUP, GROUP), 1)).astype(F32)
    grad_log = jnp.concatenate([mm_high(triu, x, "nn") for x in grad_cums], axis=0)
    grad_beta = jnp.concatenate(grad_betas, axis=0)
    grad_decay = grad_log * small_ref[0:1, :] * valid * jax.nn.sigmoid(tail + small_ref[1:2, :])
    grad_mixed_ref[:, 6 * wide :] = (
        grad_beta * beta * (1.0 - sigmoid_tail) + grad_decay
    ).astype(LOW)
    grad_small_ref[0:1, :] += jnp.sum(grad_log * log_decay, axis=0, keepdims=True)
    grad_small_ref[1:2, :] += jnp.sum(grad_decay, axis=0, keepdims=True)

    for h in range(heads):
        for slot in range(5):
            cols = slice(slot * wide + h * 128, slot * wide + (h + 1) * 128)
            grad = jnp.concatenate(grad_parts[h][slot], axis=0)
            pre = summed(slot, h)
            sig = jax.nn.sigmoid(pre)
            if slot < 3:
                act = pre * sig
                scale = lax.rsqrt(row_dot(act, act) + EPS_KEY)
                shaped = act * scale
                if slot == 0:
                    grad = grad * 128**-0.5
                grad = scale * (grad - shaped * row_dot(grad, shaped))
            grad = grad * sig * (1.0 + pre * (1.0 - sig))
            spread[0:count, cols] = grad
            back = 0.0
            for ahead in range(4):
                back = back + spread[pl.ds(ahead, count), cols] * taps_ref[3 - ahead : 4 - ahead, cols]
            grad_mixed_ref[:, cols] = back.astype(LOW)
            for tap in range(4):
                grad_taps_ref[tap : tap + 1, cols] += jnp.sum(
                    grad * padded[pl.ds(5 + tap, count), cols], axis=0, keepdims=True
                )
    end_ref[...] = carried[...]
    last_rim_ref[...] = spread[0:8, :]


def step_tokens(tokens):
    return min(256, tokens)


def block_specs(heads, count, per, order):
    wide = heads * 128
    all_wide = 6 * wide + 128
    piece = min(per, count)
    per, pieces = per // piece, count // piece

    def moved(j):
        def at(i, info):
            i = order(i) * pieces + j
            return (((i // per) ^ info[1]) * per + i % per, 0)

        return at

    whole = lambda *shape: pl.BlockSpec(shape, lambda i, info: (0,) * len(shape))
    return dict(
        mixed=pl.BlockSpec((count, all_wide), lambda i, info: (order(i), 0)),
        halo=pl.BlockSpec((8, all_wide), lambda i, info: (jnp.maximum(order(i) * (count // 8) - 1, 0), 0)),
        head=pl.BlockSpec((count, wide), lambda i, info: (order(i), 0)),
        moved_head=[pl.BlockSpec((piece, wide), moved(j)) for j in range(pieces)],
        taps=whole(8, 5 * wide),
        small=whole(8, 128),
        level=whole(2 * GROUP, 2 * GROUP),
        state=whole(heads, 128, 128),
        kept=pl.BlockSpec((count // GROUP, heads, 128, 128), lambda i, info: (order(i), 0, 0, 0)),
    )


VMEM_BYTES = 40 * 2**20


def mixer_forward(heads, first, length, info, tokens, weight, taps, small, level, start, rim):
    count = step_tokens(length)
    skip = first // count
    wide = heads * 128
    width = tokens.shape[1]
    all_wide = 6 * wide + 128
    s = block_specs(heads, count, count, lambda i: i)
    kept = jax.ShapeDtypeStruct((length // GROUP, heads, 128, 128), F32)
    out = lambda cols, kind: jax.ShapeDtypeStruct((length, cols), kind)
    rows = pl.BlockSpec((count, width), lambda i, info: (i, 0))
    gains = pl.BlockSpec((8, width), lambda i, info: (0, 0))
    held = weight.shape[:3] + (all_wide,)
    return pl.pallas_call(
        functools.partial(forward_kernel, heads, first),
        grid_spec=pltpu.PrefetchScalarGridSpec(
            num_scalar_prefetch=1,
            grid=(length // count,),
            in_specs=[
                pl.BlockSpec((count, width), lambda i, info: (i + skip, 0)),
                pl.BlockSpec(held, lambda i, info: (0, 0, 0, 0)),
                s["taps"], s["small"], s["level"], s["state"], s["taps"],
            ],
            out_specs=[
                s["head"], s["head"], s["kept"], s["kept"], s["kept"], s["state"], s["mixed"], rows, gains, s["taps"]
            ],
            scratch_shapes=[
                pltpu.VMEM((heads, 128, 128), F32),
                pltpu.VMEM((count + 8, 5 * wide), F32),
                pltpu.VMEM((width, all_wide), LOW),
            ],
        ),
        out_shape=[
            out(wide, LOW), out(wide, F32), kept, kept, kept, jax.ShapeDtypeStruct(start.shape, F32),
            out(all_wide, F32), out(width, LOW), jax.ShapeDtypeStruct((8, width), F32),
            jax.ShapeDtypeStruct(rim.shape, F32),
        ],
        compiler_params=pltpu.CompilerParams(vmem_limit_bytes=56 * 2**20),
        cost_estimate=pl.CostEstimate(
            flops=length * heads * (4_000_000 if first == 0 else 18_000_000),
            bytes_accessed=length * heads * 10_000,
            transcendentals=0,
        ),
        name="mixer_forward",
    )(info, tokens, weight, taps, small, level, start, rim)


def mixer_backward(
    heads, first, tokens, per, info, mixed, raw, grad, taps, small, level, solve, fresh, state, start, rim, before
):
    count = step_tokens(tokens)
    steps = tokens // count
    wide = heads * 128
    s = block_specs(heads, count, per, lambda i: steps - 1 - i)
    return pl.pallas_call(
        functools.partial(backward_kernel, heads, first, len(s["moved_head"])),
        grid_spec=pltpu.PrefetchScalarGridSpec(
            num_scalar_prefetch=1,
            grid=(steps,),
            in_specs=[
                s["mixed"], s["halo"], s["head"], s["taps"], s["small"], s["level"],
                s["kept"], s["kept"], s["kept"], s["state"], s["taps"], s["taps"], *s["moved_head"],
            ],
            out_specs=[s["mixed"], s["taps"], s["small"], s["state"], s["taps"]],
            scratch_shapes=[
                pltpu.VMEM((heads, 128, 128), F32),
                pltpu.VMEM((count + 8, 5 * wide), F32),
                pltpu.VMEM((count + 8, 5 * wide), F32),
            ],
        ),
        out_shape=[
            jax.ShapeDtypeStruct((tokens, mixed.shape[1]), LOW),
            jax.ShapeDtypeStruct((8, 5 * wide), F32),
            jax.ShapeDtypeStruct((8, 128), F32),
            jax.ShapeDtypeStruct(start.shape, F32),
            jax.ShapeDtypeStruct(rim.shape, F32),
        ],
        compiler_params=pltpu.CompilerParams(vmem_limit_bytes=VMEM_BYTES),
        cost_estimate=pl.CostEstimate(
            flops=tokens * heads * 26_000_000, bytes_accessed=tokens * heads * 10_000, transcendentals=0
        ),
        name="mixer_backward",
    )(info, mixed, mixed, raw, taps, small, level, solve, fresh, state, start, rim, before, *(grad,) * len(s["moved_head"]))


def unpack_kernel(heads, head_count, info_ref, *refs):
    blocks, refs = refs[:4], refs[4:]
    query_weight, key_weight, value_weight, gate_weight, beta_across, decay_across, gain = refs[:7]
    grad_query, grad_key, grad_value, grad_gate, grad_out, grad_beta, grad_decay, grad_gain = refs[7:]
    wide, full = heads * 128, head_count * 128
    small = 0.0
    for bits, block in enumerate(blocks):
        source = info_ref[1] ^ bits
        slot = 0
        for ref, pieces in ((grad_query, 1), (grad_key, 2), (grad_value, 2), (grad_gate, 1)):
            for piece in range(pieces):
                cols = pl.ds(pl.multiple_of(piece * full + source * wide, 128), wide)
                ref[:, cols] = block[0, :, slot * wide : (slot + 1) * wide].astype(F32)
                slot += 1
        cols = pl.ds(pl.multiple_of(source * wide, 128), wide)
        grad_out[:, cols] = block[0, :, 6 * wide + 128 :].astype(F32)
        row, col = place((128, 128), 1), place((128, 128), 0)
        chosen = (row < 3 * heads) & (col == row // heads * head_count + source * heads + row % heads)
        small = small + mm_low(chosen.astype(F32), block[0, :, 6 * wide : 6 * wide + 128], "nt")
    grad_beta[...] = small[: 2 * head_count]
    grad_decay[...] = small[2 * head_count : 3 * head_count]
    total = 0.0
    for weight, grad in (
        (query_weight, grad_query), (key_weight, grad_key), (value_weight, grad_value), (gate_weight, grad_gate),
    ):
        product = weight[...].astype(F32) * grad[...]
        total = total + mm_high(jnp.ones((8, product.shape[1]), F32), product, "nt")[0:1]
    for weight, grad in ((beta_across, grad_beta), (decay_across, grad_decay)):
        total = total + jnp.sum(weight[...].astype(F32) * grad[...], axis=0, keepdims=True)
    grad_gain[...] = total / gain[...]


def unpack_grads(heads, head_count, info, blocks, weights, gain):
    query, key, value, beta, decay, gate = weights
    share = query.shape[0]
    like = lambda rows, cols: jax.ShapeDtypeStruct((rows, cols), F32)
    vmem = pl.BlockSpec(memory_space=pltpu.VMEM)
    outs = [like(share, weight.shape[1]) for weight in (query, key, value, gate)]
    outs += [like(share, head_count * 128), like(2 * head_count, share), like(head_count, share), like(1, share)]
    ins = [*blocks, query, key, value, gate, beta.T, decay.T, gain.astype(F32)[None, :]]
    query, key, value, gate, out, beta, decay, gain = pl.pallas_call(
        functools.partial(unpack_kernel, heads, head_count),
        in_specs=[pl.BlockSpec(memory_space=pltpu.SMEM)] + [vmem] * len(ins),
        out_specs=[vmem] * len(outs),
        out_shape=outs,
        name="unpack_grads",
    )(info, *ins)
    return query, key, value, beta.T, decay.T, gate, out, gain[0]


def pack_kernel(heads, head_count, info_ref, query, key, value, gate, last, beta_across, decay_across, gains, *outs):
    wide, full = heads * 128, head_count * 128
    small = [ref[...].astype(F32) for ref in (beta_across, decay_across, gains)]
    small = jnp.concatenate(small, axis=0)
    for bits, out in enumerate(outs):
        target = info_ref[1] ^ bits
        slot = 0
        for ref, pieces in ((query, 1), (key, 2), (value, 2), (gate, 1)):
            for piece in range(pieces):
                cols = pl.ds(pl.multiple_of(piece * full + target * wide, 128), wide)
                out[0, :, slot * wide : (slot + 1) * wide] = ref[:, cols]
                slot += 1
        row, col = place((small.shape[0], 128), 0), place((small.shape[0], 128), 1)
        head = col // heads * head_count + target * heads + col % heads
        gain = 3 * head_count + col - 3 * heads
        chosen = row == jnp.where(col < 3 * heads, head, jnp.where(col < 3 * heads + 2, gain, -1))
        out[0, :, 6 * wide + 128 :] = last[:, pl.ds(pl.multiple_of(target * wide, 128), wide)]
        out[0, :, 6 * wide : 6 * wide + 128] = mm_low(small, chosen.astype(F32), "tn").astype(LOW)


def pack_weights(heads, head_count, info, weights, last, gains):
    query, key, value, beta, decay, gate = weights
    share = query.shape[0]
    vmem = pl.BlockSpec(memory_space=pltpu.VMEM)
    gains = jnp.concatenate([gain.astype(F32)[None, :] for gain in gains] + [jnp.zeros((6, share), F32)], axis=0)
    out = jax.ShapeDtypeStruct((1, share, 7 * heads * 128 + 128), LOW)
    return pl.pallas_call(
        functools.partial(pack_kernel, heads, head_count),
        in_specs=[pl.BlockSpec(memory_space=pltpu.SMEM)] + [vmem] * 8,
        out_specs=[vmem] * 4,
        out_shape=[out] * 4,
        name="pack_weights",
    )(info, query, key, value, gate, last, beta.T, decay.T, gains)


def features(weight_ref, index, first=0, last=None):
    piece = weight_ref[:, index, :, first:last]
    return piece.reshape(piece.shape[0] * piece.shape[1], piece.shape[2])


def hold(weight_ref, held_ref, first=0):
    size = weight_ref.shape[0] * weight_ref.shape[2]

    @pl.when(pl.program_id(0) == 0)
    def _():
        for index in range(weight_ref.shape[1]):
            held_ref[index * size : (index + 1) * size, first : first + weight_ref.shape[3]] = features(weight_ref, index)


def feed_forward_kernel(hidden, blocks, *refs):
    gated_refs, out_refs, refs = refs[:blocks], refs[blocks : 2 * blocks], refs[2 * blocks :]
    tokens_ref, grad_ref, weight_ref, gains_ref, second_ref, normed_ref, hidden_ref, acts_ref, partial_ref = refs[:9]
    *kept, held = refs[9:]
    gated = jnp.concatenate([ref[...] for ref in gated_refs], axis=1)
    first = gated.shape[1]
    for index, ref in enumerate(out_refs):
        hold(ref, held, index * ref.shape[3])
    hold(weight_ref, held, first)
    last = first + 2 * hidden
    if kept:

        @pl.when(pl.program_id(0) == 0)
        def _():
            kept[0][...] = held[:, : kept[0].shape[1]]
            kept[1][...] = held[:, last:]

    second = tokens_ref[...].astype(F32) + mm_low(gated, held[:, :first], "nt")
    second_ref[...] = second
    scale = lax.rsqrt(jnp.mean(second * second, axis=1, keepdims=True) + EPS_NORM)
    normed = (second * scale * gains_ref[1:2, :]).astype(LOW)
    normed_ref[...] = normed
    grad_hidden = mm_low(grad_ref[...], held[:, last:], "nn")
    acts = mm_low(normed, held[:, first:last], "nn")
    gate, up = acts[:, :hidden], acts[:, hidden:]
    sig = jax.nn.sigmoid(gate)
    silu_gate = gate * sig
    hidden_ref[...] = (silu_gate * up).astype(LOW)
    grads = [grad_hidden * up * sig * (1.0 + gate * (1.0 - sig)), grad_hidden * silu_gate]
    grads = jnp.concatenate(grads, axis=1).astype(LOW)
    acts_ref[...] = grads
    partial_ref[...] = mm_low(grads, held[:, first:last], "nt").astype(LOW)


def feed_forward_part(hidden, first, tokens, grads, gated, outs, weight, gains):
    length, width = gated[0].shape[0], tokens.shape[1]
    count = min(256, length)
    skip = first // count
    whole_rows = pl.BlockSpec((count, width), lambda i: (i + skip, 0))
    rows = lambda cols: pl.BlockSpec((count, cols), lambda i: (i, 0))
    out = lambda cols, kind: jax.ShapeDtypeStruct((length, cols), kind)
    kept = [gated[0].shape[1], hidden] if first == 0 else []
    return pl.pallas_call(
        functools.partial(feed_forward_kernel, hidden, len(gated)),
        grid=(length // count,),
        in_specs=[rows(block.shape[1]) for block in gated]
        + [pl.BlockSpec(block.shape, lambda i: (0, 0, 0, 0)) for block in outs]
        + [whole_rows, whole_rows, pl.BlockSpec(weight.shape, lambda i: (0, 0, 0, 0))]
        + [pl.BlockSpec((8, width), lambda i: (0, 0))],
        out_specs=[rows(width), rows(width), rows(hidden), rows(2 * hidden), rows(width)]
        + [pl.BlockSpec((width, cols), lambda i: (0, 0)) for cols in kept],
        out_shape=[out(width, F32), out(width, LOW), out(hidden, LOW), out(2 * hidden, LOW), out(width, LOW)]
        + [jax.ShapeDtypeStruct((width, cols), LOW) for cols in kept],
        scratch_shapes=[pltpu.VMEM((width, weight.shape[3] + sum(block.shape[3] for block in outs)), LOW)],
        compiler_params=pltpu.CompilerParams(vmem_limit_bytes=56 * 2**20),
        cost_estimate=pl.CostEstimate(flops=8 * 10**9, bytes_accessed=10**7, transcendentals=0),
        name="feed_forward",
    )(*gated, *outs, tokens, grads, weight, gains)


def weight_grads_kernel(counts, back, *refs):
    if back:
        refs, weight_ref, out_ref, back_ref = refs[:-3], *refs[-3:]
        weight, at = features(weight_ref, 0), 0
        for ref in refs[counts[0][0] : counts[0][0] + counts[0][1]]:
            tokens = ref.shape[0]
            back_ref[at : at + tokens, :] = mm_low(ref[...], weight, "nt").astype(LOW)
            at += tokens
    else:
        *refs, out_ref = refs
    first = 0
    places, share = out_ref.shape[0], out_ref.shape[2]
    for lefts, rights in counts:
        left_refs, right_refs, refs = refs[:lefts], refs[lefts : lefts + rights], refs[lefts + rights :]
        total, at = 0.0, 0
        for right in right_refs:
            tokens = right.shape[0]
            if lefts == rights:
                left = left_refs[at // tokens][...]
            else:
                left = left_refs[0][at : at + tokens, :]
            total = total + mm_low(left, right[...], "tn")
            at += tokens
        width = total.shape[1]
        out_ref[:, 0, :, first : first + width] = total.astype(LOW).reshape(places, share, width)
        first += width


def weight_grads(places, count, pairs, weight=None):
    features_all = pairs[0][0][0].shape[1]
    size = features_all // count
    share = size // places
    width = sum(rights[0].shape[1] for _, rights in pairs)
    specs, arrays, flops = [], [], 0
    for lefts, rights in pairs:
        specs += [pl.BlockSpec((left.shape[0], size), lambda i: (0, i)) for left in lefts]
        specs += [pl.BlockSpec(right.shape, lambda i: (0, 0)) for right in rights]
        arrays += [*lefts, *rights]
        flops += sum(2 * right.shape[0] * right.shape[1] * features_all for right in rights)
    out_specs = [pl.BlockSpec((places, 1, share, width), lambda i: (0, i, 0, 0))]
    out_shape = [jax.ShapeDtypeStruct((places, count, share, width), LOW)]
    if weight is not None:
        tokens = sum(right.shape[0] for right in pairs[0][1])
        specs.append(pl.BlockSpec((places, 1, share, pairs[0][1][0].shape[1]), lambda i: (0, i, 0, 0)))
        arrays.append(weight)
        out_specs.append(pl.BlockSpec((tokens, size), lambda i: (0, i)))
        out_shape.append(jax.ShapeDtypeStruct((tokens, features_all), LOW))
    counts = tuple((len(lefts), len(rights)) for lefts, rights in pairs)
    out, *back = pl.pallas_call(
        functools.partial(weight_grads_kernel, counts, weight is not None),
        grid=(count,),
        in_specs=specs,
        out_specs=out_specs,
        out_shape=out_shape,
        compiler_params=pltpu.CompilerParams(vmem_limit_bytes=56 * 2**20),
        cost_estimate=pl.CostEstimate(flops=flops, bytes_accessed=10**7, transcendentals=0),
        name="weight_grads",
    )(*arrays)
    return out.reshape(-1, width), *back


def swap(array, axis, bits):
    return lax.ppermute(array, axis, [(i, i ^ bits) for i in range(lax.axis_size(axis))])


def on_square():
    return lax.axis_size("seq") == 4


def power_of_two(axis):
    return lax.axis_size(axis) & (lax.axis_size(axis) - 1) == 0


def after(array, *others):
    return lax.optimization_barrier((array,) + others)[0]


def spread_out(array):
    if not on_square():
        whole = lax.all_gather(array, "seq")
        return [whole[i] for i in range(whole.shape[0])]
    far, beside, below = (swap(array, "seq", bits) for bits in (3, 1, 2))
    return [array, beside, below, far]


def spread_out_near(*arrays):
    if not on_square():
        return [spread_out(array) for array in arrays]
    half = arrays[0].shape[0] // 2
    near = [(swap(array, "seq", 1), swap(array, "seq", 2)) for array in arrays]
    far = [(swap(below[:half], "seq", 1), swap(beside[half:], "seq", 2)) for beside, below in near]
    return [
        [array, beside, below, jnp.concatenate(parts, axis=0)]
        for array, (beside, below), parts in zip(arrays, near, far)
    ]


def in_place_order(blocks):
    if not on_square():
        return jnp.concatenate(blocks, axis=0)
    me = lax.axis_index("seq")
    size = blocks[0].shape[0]
    out = jnp.zeros((len(blocks) * size,) + blocks[0].shape[1:], blocks[0].dtype)
    for bits, block in enumerate(blocks):
        out = lax.dynamic_update_slice(out, block, ((me ^ bits) * size, 0))
    return out


def row_block(array, index):
    size = array.shape[0] // lax.axis_size("seq")
    return lax.dynamic_slice_in_dim(array, index * size, size, 0)


def to_send(array):
    if not on_square():
        return [array.astype(LOW)]
    me = lax.axis_index("seq")
    return [row_block(array, me ^ bits).astype(LOW) for bits in (3, 1, 2)]


def send(blocks):
    if not on_square():
        return [lax.psum_scatter(blocks[0], "seq", scatter_dimension=0, tiled=True)]
    return [swap(block, "seq", bits) for bits, block in zip((3, 1, 2), blocks)]


def total(array, got):
    if not on_square():
        return got[0].astype(F32)
    return row_block(array, lax.axis_index("seq")).astype(F32) + sum(block.astype(F32) for block in got)


def exchange_unordered(blocks):
    me = lax.axis_index("seq")
    sends = tuple(lax.dynamic_index_in_dim(blocks, me ^ bits, 0, True) for bits in (0, 1, 2, 3))
    sends = lax.optimization_barrier(sends)
    got = tuple(swap(sends[bits], "seq", bits) for bits in (3, 1, 2))
    far, beside, below = lax.optimization_barrier(got)
    return [sends[0], beside, below, far]


def exchange(blocks):
    if not on_square():
        return lax.all_to_all(blocks, "seq", 0, 0, tiled=True)
    me = lax.axis_index("seq")
    others = (3, 1, 2)
    sends = lax.optimization_barrier(tuple(lax.dynamic_index_in_dim(blocks, me ^ bits, 0, True) for bits in others))
    got = lax.optimization_barrier(tuple(swap(block, "seq", bits) for bits, block in zip(others, sends)))
    out = blocks
    for bits, block in zip(others, got):
        out = lax.dynamic_update_slice(out, block, (me ^ bits, 0, 0))
    return out


def sum_over(array, axis):
    if not power_of_two(axis):
        return lax.psum(array, axis)
    bits = 1
    while bits < lax.axis_size(axis):
        array = array + swap(array, axis, bits)
        bits *= 2
    return array


def gather_rows(mine):
    return lax.all_gather(mine, "rows", axis=0)


def in_rows(whole):
    rows, count, size, width = whole.shape
    return whole.transpose(1, 0, 2, 3).reshape(count * rows * size, width)


def by_rows(grad):
    count, rows = lax.axis_size("seq"), lax.axis_size("rows")
    size = grad.shape[0] // (count * rows)
    grad = grad.astype(LOW).reshape(count, rows, size, grad.shape[1])
    return grad.transpose(1, 0, 2, 3).reshape(-1, grad.shape[3])


def sum_rows(grad):
    count = lax.axis_size("seq")
    summed = lax.psum_scatter(grad, "rows", scatter_dimension=0, tiled=True)
    return summed.reshape(count, -1, grad.shape[1])


def project(left, right):
    return jnp.dot(left, right, preferred_element_type=F32)


def outer_sum(left, right):
    return lax.dot_general(left, right, FORMS["tn"], preferred_element_type=F32)


def back_project(left, right):
    return lax.dot_general(left, right, FORMS["nt"], preferred_element_type=F32)


def norm_scale(features):
    return lax.rsqrt(jnp.mean(features * features, axis=-1, keepdims=True) + EPS_NORM)


def norm_back(features, scale, grad):
    return scale * grad - features * scale**3 * jnp.mean(grad * features, axis=-1, keepdims=True)


def on_device(
    block_input, valid_length, query_weight, key_weight, value_weight, beta_weight, decay_weight, gate_weight,
    out_weight, ffn_gate_weight, ffn_up_weight, ffn_down_weight, norm_gain, ffn_norm_gain, head_norm_gain,
    decay_log, decay_bias, conv_weight, output_grad,
):
    count = lax.axis_size("seq")
    me = lax.axis_index("seq")
    rows_here, tokens_here, model_width = block_input.shape
    share = query_weight.shape[0]
    head_count = decay_log.shape[0]
    heads = max(1, head_count // count)
    blocks = head_count // heads
    copies = count // blocks
    block = me // copies
    wide = heads * 128
    hidden = ffn_gate_weight.shape[1] // count
    square = on_square() and copies == 1

    def cut(weight, pieces, at):
        width = weight.shape[1] // (pieces * blocks)
        at = at // copies
        return [
            weight[:, (p * blocks + at) * width : (p * blocks + at + 1) * width] for p in range(pieces)
        ]

    def cut_hidden(weight, at):
        return [weight[:, at * hidden : (at + 1) * hidden]]

    gains = jnp.stack([norm_gain, ffn_norm_gain], axis=1)

    def tail_of(at):
        parts = cut(beta_weight, 2, at) + cut(decay_weight, 1, at) + [gains]
        return parts + [jnp.zeros((share, 128 - 3 * heads - 2), LOW)]

    def first_of(at):
        parts = cut(query_weight, 1, at) + cut(key_weight, 2, at) + cut(value_weight, 2, at)
        return jnp.concatenate(parts + cut(gate_weight, 1, at) + tail_of(at) + cut(out_weight, 1, at), axis=1)

    def rest_of(at):
        parts = cut_hidden(ffn_gate_weight, at) + cut_hidden(ffn_up_weight, at) + cut_hidden(ffn_down_weight, at)
        return jnp.concatenate(parts, axis=1)

    def pack(part):
        return jnp.stack([part(at) for at in range(count)])

    info = jnp.stack([valid_length[0], me if on_square() else jnp.int32(0)])
    mixer_weights = (query_weight, key_weight, value_weight, beta_weight, decay_weight, gate_weight)
    if on_square():
        packed = pack_weights(heads, head_count, info, mixer_weights, out_weight, (norm_gain, ffn_norm_gain))
        got = tuple(swap(packed[bits], "seq", bits) for bits in (3, 1, 2))
        far, beside, below = lax.optimization_barrier(got)
        first_share = jnp.zeros((count,) + packed[0].shape[1:], LOW)
        for bits, block_got in enumerate((packed[0], beside, below, far)):
            first_share = lax.dynamic_update_slice(first_share, block_got, (me ^ bits, 0, 0))
    else:
        first_share = exchange(pack(first_of))
    own, own_grad, rest_pack, first_share = lax.optimization_barrier(
        (block_input.reshape(tokens_here, model_width), output_grad.reshape(tokens_here, model_width), pack(rest_of),
         first_share)
    )
    mixed_parts = gather_rows(first_share)
    everyone_got, grads_got = spread_out_near(own, own_grad)
    rest_share = exchange(rest_pack)
    everyone, grad_branch = in_place_order(everyone_got), in_place_order(grads_got)
    rest_parts = gather_rows(rest_share)
    if not square:
        mixed_parts = in_rows(mixed_parts)[None, None]
    mixed_parts, everyone, grad_branch = lax.optimization_barrier((mixed_parts, everyone, grad_branch))
    out_got = spread_out(mixed_parts[:, :, :, 6 * wide + 128 :])
    mixed_weight = mixed_parts[0, 0, :, : 6 * wide + 128]
    if not square:
        out_own = mixed_parts[0, 0, :, 6 * wide + 128 :]
        out_all = jnp.concatenate([block_got[0, 0] for block_got in out_got[:: 1 if on_square() else copies]], axis=1)
        rest_weight = in_rows(rest_parts)
        ffn_in, ffn_down = rest_weight[:, : 2 * hidden], rest_weight[:, 2 * hidden :]

    def block_lanes(vector, first):
        mine = lax.dynamic_slice_in_dim(vector, block * heads, heads)
        return jnp.pad(mine, (first, 128 - first - heads))

    small = jnp.stack([block_lanes(-jnp.exp(decay_log), 2 * heads), block_lanes(decay_bias, 2 * heads), head_norm_gain])
    small = jnp.pad(small, ((0, 5), (0, 0)))
    taps = [
        lax.dynamic_slice_in_dim(conv_weight, (slot * blocks + block) * wide, wide, 1) for slot in range(5)
    ]
    taps = jnp.pad(jnp.concatenate(taps, axis=1), ((0, 8 - conv_weight.shape[0]), (0, 0)))
    level = level_table()

    length = count * tokens_here
    part = length // 2
    tie = lax.optimization_barrier

    zero_state = jnp.zeros((heads, 128, 128), F32)
    no_rim = jnp.zeros((8, 5 * wide), F32)

    def forward(first, start, rim):
        outs = mixer_forward(heads, first, part, info, everyone, mixed_parts, taps, small, level, start, rim)
        return outs[0], outs[1:5], outs[5], outs[6], outs[7], outs[8], outs[9]

    gated_a, kept_a, end, mixed_a, normed_a, gains, middle_rim = forward(0, zero_state, no_rim)
    end, out_got = tie((end, out_got))
    gated_got_a = spread_out(gated_a)
    gated_b, kept_b, end, mixed_b, normed_b, _, _ = forward(part, end, middle_rim)
    gated_b, gated_got_a = tie((gated_b, gated_got_a))
    gated_got_b = spread_out(gated_b)
    if not square:
        gain_second = gains[1]

    def feed_forward(index, gated_got, got=None):
        if square:
            outs = feed_forward_part(
                hidden, index * part, everyone, grad_branch, gated_got, out_got, rest_parts, gains
            )
            return (*tie(tuple(outs[:5]) + (got,)), outs[5:])
        rows = slice(index * part, (index + 1) * part)
        gated_all = jnp.concatenate(gated_got[:: 1 if on_square() else copies], axis=1)
        second = everyone[rows].astype(F32) + back_project(gated_all, out_all)
        normed_two = (second * norm_scale(second) * gain_second).astype(LOW)
        if got is not None:
            normed_two, got = tie((normed_two, got))
        acts = project(normed_two, ffn_in)
        gate_act, up_act = acts[:, :hidden], acts[:, hidden:]
        sig = jax.nn.sigmoid(gate_act)
        hidden_low = (gate_act * sig * up_act).astype(LOW)
        grad_hidden = project(grad_branch[rows], ffn_down)
        grad_acts = [grad_hidden * up_act * sig * (1.0 + gate_act * (1.0 - sig)), grad_hidden * gate_act * sig]
        grad_acts = jnp.concatenate(grad_acts, axis=1).astype(LOW)
        return second, normed_two, hidden_low, grad_acts, back_project(grad_acts, ffn_in), got, None

    def second_back(index, second, partial, got):
        grad = total(partial, got) * gain_second
        second = row_block(second, me)
        out_grad = row_block(grad_branch_late[index * part : (index + 1) * part], me)
        return (out_grad.astype(F32) + norm_back(second, norm_scale(second), grad)).astype(LOW)

    second_a, normed_two_a, hidden_a, grad_acts_a, partial_a, _, kept = feed_forward(0, gated_got_a)
    if square:
        out_own, ffn_down = kept
    sends_a, gated_got_b = tie((to_send(partial_a), gated_got_b))
    got_a = send(sends_a)
    second_b, normed_two_b, hidden_b, grad_acts_b, partial_b, got_a, _ = feed_forward(1, gated_got_b, got_a)
    sends_b, hidden_b, grad_acts_b, gains_late, grad_branch_late = tie(
        (to_send(partial_b), hidden_b, grad_acts_b, gains, grad_branch)
    )
    gain_first, gain_second = gains_late[0], gains_late[1]
    got_b = send(sends_b)

    join_parts = lambda a, b: jnp.concatenate([a, b], axis=0)
    hidden_low = join_parts(hidden_a, hidden_b)
    down = back_project(hidden_low, ffn_down)
    down_sends = to_send(down)
    grad_second_a = second_back(0, second_a, partial_a, got_a)
    got_b, down_sends, grad_second_a = tie((got_b, down_sends, grad_second_a))
    grad_second_b, grad_acts_b = tie((second_back(1, second_b, partial_b, got_b), grad_acts_b))
    grads_two_b = spread_out(grad_second_b)
    if square:
        pairs = [((normed_two_a, normed_two_b), (grad_acts_a, grad_acts_b)), ((grad_branch,), (hidden_a, hidden_b))]
        (early,) = weight_grads(lax.axis_size("rows"), count, pairs)
    else:
        early_in = outer_sum(join_parts(normed_two_a, normed_two_b), join_parts(grad_acts_a, grad_acts_b))
        early = by_rows(jnp.concatenate([early_in, outer_sum(grad_branch, hidden_low)], axis=1))
    grads_two_b, early, down_sends, grad_second_a = tie((grads_two_b, early, down_sends, grad_second_a))
    early = sum_rows(early)
    grads_two_a = spread_out(grad_second_a)

    grad_gated = project(jnp.concatenate(grads_two_b, axis=0), out_own)
    grad_pre_b, taps_b, small_b, end, rim = mixer_backward(
        heads, part, part, part // count, info, mixed_b, kept_b[0], grad_gated, taps, small, level, *kept_b[1:],
        zero_state, no_rim, middle_rim,
    )
    end, grads_two_a, down_sends = tie((end, grads_two_a, down_sends))
    down_got = send(down_sends)
    grad_gated = project(jnp.concatenate(grads_two_a, axis=0), out_own)
    grad_second = join_parts(in_place_order(grads_two_a), in_place_order(grads_two_b))

    def once(array):
        return array if copies == 1 else array * (me % copies == 0).astype(array.dtype)

    grad_pre_a, taps_a, small_a, end, rim = mixer_backward(
        heads, 0, part, part // count, info, mixed_a, kept_a[0], grad_gated, taps, small, level, *kept_a[1:], end, rim,
        no_rim,
    )
    grad_pre_a, taps_a, small_a, down_got = tie((grad_pre_a, taps_a, small_a, down_got))
    grad_pre_a, grad_pre_b = once(grad_pre_a), once(grad_pre_b)
    if square:
        pairs = [((normed_a, normed_b), (grad_pre_a, grad_pre_b)), ((grad_second,), (gated_a, gated_b))]
        late, grad_normed = weight_grads(lax.axis_size("rows"), count, pairs, mixed_parts)
    else:
        out_grad = once(outer_sum(grad_second, join_parts(gated_a, gated_b)).astype(LOW))
        late = outer_sum(join_parts(normed_a, normed_b), join_parts(grad_pre_a, grad_pre_b)).astype(LOW)
        late = by_rows(jnp.concatenate([late, out_grad], axis=1))
        grad_normed = back_project(join_parts(grad_pre_a, grad_pre_b), mixed_weight)
    grad_taps, grad_small = taps_a + taps_b, small_a + small_b
    late, early, grad_taps, grad_small, down_got, grad_normed = tie(
        (late, early, grad_taps, grad_small, down_got, grad_normed)
    )
    grad_normed_got = send(to_send(grad_normed))
    late = sum_rows(late)
    early = exchange(early)

    def at_block(vector, first, width):
        mine = once(vector[first : first + width])
        return lax.dynamic_update_slice(jnp.zeros((blocks * width,), F32), mine, (block * width,))

    flat = [once(grad_small[2]), at_block(grad_small[0], 2 * heads, heads), at_block(grad_small[1], 2 * heads, heads)]
    flat = jnp.concatenate(flat)
    taps_wide = 5 * wide
    flat = jnp.pad(flat, (0, -flat.shape[0] % taps_wide)).reshape(-1, taps_wide)
    pooled = sum_over(jnp.concatenate([once(grad_taps[:4]), flat], axis=0), "rows")
    pooled, grad_normed_got = tie((pooled, grad_normed_got))
    by_place = lax.dynamic_update_slice(jnp.zeros((blocks, 4, taps_wide), F32), pooled[None, :4], (block, 0, 0))
    pooled = sum_over(jnp.concatenate([by_place.reshape(-1, taps_wide), pooled[4:]], axis=0), "seq")
    ends = [128, 128 + head_count, 128 + 2 * head_count]

    second = row_block(join_parts(second_a, second_b), me)
    result = (second + total(down, down_got)).astype(LOW).reshape(block_input.shape)
    def join(grads, first, pieces, width, every=copies):
        return jnp.concatenate(
            [
                grads[b, :, first + p * width : first + (p + 1) * width]
                for p in range(pieces)
                for b in range(0, count, every)
            ],
            axis=1,
        ).astype(F32)

    def gain_grad(gain, *pairs):
        summed = sum(jnp.sum(weight.astype(F32) * grad, axis=1) for weight, grad in pairs)
        return summed / gain.astype(F32)

    grad_ffn_gate = join(early, 0, 1, hidden, 1)
    grad_ffn_up = join(early, hidden, 1, hidden, 1)
    grad_ffn_down = join(early, 2 * hidden, 1, hidden, 1)
    grad_gain_second = gain_grad(ffn_norm_gain, (ffn_gate_weight, grad_ffn_gate), (ffn_up_weight, grad_ffn_up))
    flat = pooled[4 * blocks :].reshape(-1)
    grad_conv = pooled[: 4 * blocks].reshape(blocks, 4, taps_wide)
    grad_conv = jnp.concatenate(
        [grad_conv[b, :, slot * wide : (slot + 1) * wide] for slot in range(5) for b in range(blocks)], axis=1
    )
    late, result, grad_normed_got = tie((late, result, grad_normed_got))
    tokens = own.astype(F32)
    grad_tokens = norm_back(tokens, norm_scale(tokens), total(grad_normed, grad_normed_got) * gain_first)
    grad_input = row_block(grad_second, me).astype(F32) + grad_tokens
    grad_input = grad_input.reshape(block_input.shape)

    if on_square():
        late = exchange_unordered(late)
        *mixer_grads, grad_out, grad_gain_first = unpack_grads(heads, head_count, info, late, mixer_weights, norm_gain)
        grad_query, grad_key, grad_value, grad_beta, grad_decay, grad_gate = mixer_grads
    else:
        late = exchange(late)
        grad_query = join(late, 0, 1, wide)
        grad_key = join(late, wide, 2, wide)
        grad_value = join(late, 3 * wide, 2, wide)
        grad_beta = join(late, 6 * wide, 2, heads)
        grad_decay = join(late, 6 * wide + 2 * heads, 1, heads)
        grad_gate = join(late, 5 * wide, 1, wide)
        grad_out = join(late, 6 * wide + 128, 1, wide)
        mixer_grads = (grad_query, grad_key, grad_value, grad_beta, grad_decay, grad_gate)
        grad_gain_first = gain_grad(norm_gain, *zip(mixer_weights, mixer_grads))
    return (
        result,
        grad_input,
        grad_query,
        grad_key,
        grad_value,
        grad_beta,
        grad_decay,
        grad_gate,
        grad_out,
        grad_ffn_gate,
        grad_ffn_up,
        grad_ffn_down,
        grad_gain_first,
        grad_gain_second,
        flat[: ends[0]],
        flat[ends[0] : ends[1]],
        flat[ends[1] : ends[2]],
        grad_conv,
    )


def solution(mesh):
    tokens, weight, vector, whole = P("rows", "seq", None), P(BOTH, None), P(BOTH), P()
    return jax.shard_map(
        on_device,
        mesh=mesh,
        in_specs=(tokens, P("rows")) + (weight,) * 10 + (vector,) * 2 + (whole,) * 4 + (tokens,),
        out_specs=(tokens, tokens) + (weight,) * 10 + (vector,) * 2 + (whole,) * 4,
        check_vma=False,
    )
```
